256 devices in a mesh: pipe: 4 (over z_hi, core), expert: 16 (over y, x), dp: 4 (over z_lo).
Axes of the slice: x: 4, y: 4, z: 8 (z_hi: 2, z_lo: 4; z = z_hi * 4 + z_lo), core: 2. Of those that a mesh axis runs over, the one named last changes fastest.
Arguments:
- tokens_in: bfloat16 [4, 8192, 2048], P('pipe', ('expert', 'dp')), may hold values from -6 to 6
- grad_out: bfloat16 [4, 8192, 2048], P('pipe', ('expert', 'dp')), may hold values from -6 to 6
- route_weight: bfloat16 [4, 8192, 2], P('pipe', ('expert', 'dp')), may hold values from 0.19921875 to 1
- slot_of: int32 [4, 8192, 2], P('pipe', ('expert', 'dp')), may hold values from 0 to 15, as said below
- replica_of: int32 [4, 8], P('pipe'), may hold values from 0 to 7, as said below
- w_gate: bfloat16 [4, 8, 2048, 512], P('pipe', None, 'expert'), may hold values from -0.125 to 0.125
- w_up: bfloat16 [4, 8, 2048, 512], P('pipe', None, 'expert'), may hold values from -0.125 to 0.125
- w_down: bfloat16 [4, 8, 2048, 512], P('pipe', None, 'expert'), may hold values from -0.25 to 0.25
Outputs:
- grad_in: bfloat16 [4, 8192, 2048], P('pipe', ('expert', 'dp'))
- route_grad: bfloat16 [4, 8192, 2], P('pipe', ('expert', 'dp'))
- grad_gate: bfloat16 [4, 8, 2048, 512], P('pipe', None, ('expert', 'dp'))
- grad_up: bfloat16 [4, 8, 2048, 512], P('pipe', None, ('expert', 'dp'))
- grad_down: bfloat16 [4, 8, 2048, 512], P('pipe', None, ('expert', 'dp'))
The draws below stay inside these ranges and needn't reach their ends.
Inputs may be any that keep to these rules, and one draw needn't show every extreme that they name: `slot_of`: A token's 2 pairs name slots of different experts. Among the 128 tokens of one device no slot is named more than 20 times, and in each section one slot is named exactly 20 times by every device. `replica_of`: in each section one expert is named by exactly 3 replica slots, 5 others by one each, and the remaining 2 by none.
All inputs are finite; a program needn't handle non-finite values.
Results may differ from the reference program's by a relative error of at most 0.018.
Values may be sent and summed in bfloat16 or wider, within the bound.
No kernel may reach another device: no remote copies, remote signals or barrier semaphores. Data moves between devices by JAX's collectives and lax.ppermute only.
A program may use at most 128 MiB of HBM per device.

```python
import jax
import jax.numpy as jnp
from jax import lax

D = 2048
EXPERTS = 8
TOP = 2
FF = 512
TOK_DEV = 128
CAP = 20
SLOTS = 16
SECTIONS = 4
TOKENS = 8192


def replica_lists(key):
    section_keys = jax.random.split(key, SECTIONS)

    def one_section(section_key):
        first_key, second_key = jax.random.split(section_key)
        order = jax.random.permutation(first_key, EXPERTS)
        picks = jnp.concatenate([jnp.repeat(order[:1], 3), order[1:EXPERTS - 2]])
        return jax.random.permutation(second_key, picks)
    return jax.vmap(one_section)(section_keys).astype(jnp.int32)


def draw_replica_of(key, part):
    return replica_lists(key)


def draw_slot_of(key, part):
    replicas = replica_lists(key)
    key = jax.random.fold_in(key, 7)
    sources = TOKENS // TOK_DEV
    pairs_dev = TOK_DEV * TOP
    seat_count = SLOTS * CAP
    hot_key, source_key = jax.random.split(key)
    hot_slots = jax.random.randint(hot_key, (SECTIONS,), 0, SLOTS)

    def one_source(source_rng, hot_slot, slot_expert):
        key_a, key_b, key_c, key_d = jax.random.split(source_rng, 4)
        seat_slot = jnp.arange(seat_count, dtype=jnp.int32) // CAP
        shuffled = jax.random.permutation(key_a, seat_count)
        score = jnp.where(seat_slot == hot_slot, shuffled - seat_count, shuffled)
        chosen = jnp.argsort(score, stable=True)[:pairs_dev]
        chosen_slot = seat_slot[chosen]
        chosen_expert = slot_expert[chosen_slot]
        second = jax.random.permutation(key_b, pairs_dev)
        order = jnp.argsort(chosen_expert * pairs_dev + second, stable=True)
        sorted_slot = chosen_slot[order]
        token_pairs = sorted_slot.reshape(TOP, TOK_DEV).T
        flip = jax.random.randint(key_c, (TOK_DEV,), 0, 2)
        token_pairs = jnp.where(flip[:, None] == 1, token_pairs[:, ::-1], token_pairs)
        token_order = jax.random.permutation(key_d, TOK_DEV)
        return token_pairs[token_order]

    def one_section(section_rng, hot_slot, replica_row):
        slot_expert = jnp.concatenate([jnp.arange(EXPERTS, dtype=jnp.int32), replica_row])
        source_keys = jax.random.split(section_rng, sources)
        blocks = jax.vmap(one_source, in_axes=(0, None, None))(source_keys, hot_slot, slot_expert)
        return blocks.reshape(TOKENS, TOP)
    section_keys = jax.random.split(source_key, SECTIONS)
    return jax.vmap(one_section)(section_keys, hot_slots, replicas).astype(jnp.int32)


def steps_of(key, dims, shards, least, top_value):
    def one(dim, blocks):
        draws = jax.random.uniform(jax.random.fold_in(jax.random.fold_in(key, 6), dim), (blocks,), jnp.float32, least / len(shards), top_value / len(shards))
        return jnp.repeat(jnp.exp(draws), dims[dim] // blocks).reshape((-1,) + (1,) * (len(dims) - dim - 1))

    gain = one(*shards[0])
    for cut in shards[1:]:
        gain = gain * one(*cut)
    return gain


def centred(rng, extent, deviation, limit, cuts=(), kind=jnp.bfloat16):
    factor_of = steps_of(rng, extent, cuts, -0.22, 0.18) if cuts else 1.0
    values = jax.random.normal(rng, extent, jnp.float32) * deviation * factor_of
    return jnp.minimum(jnp.maximum(values, -limit), limit).astype(kind)


def setup_inputs(seed: int = 0) -> dict:
    splits = jax.random.split(jax.random.key(seed), 9)
    return {
        "tokens_in": centred(splits[0], (SECTIONS, TOKENS, D), 1.0, 6.0, ((0, 4), (1, 64))),
        "grad_out": centred(splits[1], (SECTIONS, TOKENS, D), 1.0, 6.0, ((0, 4), (1, 64))),
        "route_weight": jnp.clip(0.19921875 + 0.80078125 * jax.random.uniform(splits[2], (SECTIONS, TOKENS, TOP), jnp.float32) ** steps_of(splits[2], (SECTIONS, TOKENS, TOP), ((0, 4), (1, 64)), -0.2, 0.2), 0.19921875, 1.0).astype(jnp.bfloat16),
        "slot_of": draw_slot_of(jax.random.fold_in(splits[8], 71), 0),
        "replica_of": draw_replica_of(jax.random.fold_in(splits[8], 71), 0),
        "w_gate": centred(splits[5], (SECTIONS, EXPERTS, D, FF), D ** -0.5, 0.125, ((0, 4), (2, 16))),
        "w_up": centred(splits[6], (SECTIONS, EXPERTS, D, FF), D ** -0.5, 0.125, ((0, 4), (2, 16))),
        "w_down": centred(splits[7], (SECTIONS, EXPERTS, D, FF), FF ** -0.5, 0.25, ((0, 4), (2, 16))),
    }


def slot_table(replicas):
    return jnp.concatenate([jnp.arange(EXPERTS, dtype=jnp.int32), replicas.astype(jnp.int32)])


def pair_rows(slot_pairs):
    pair_slot = slot_pairs.reshape(-1).astype(jnp.int32)
    onehot = (pair_slot[:, None] == jnp.arange(SLOTS, dtype=jnp.int32)[None, :]).astype(jnp.int32)
    before = jnp.cumsum(onehot, axis=0) - onehot
    return (pair_slot * CAP + jnp.sum(before * onehot, axis=1)).astype(jnp.int32)


def pack_rows(tokens_dev, grads_dev, weights_dev, slot_pos):
    count = slot_pos.shape[0]
    row_owner = jnp.full((SLOTS * CAP,), -1, jnp.int32).at[slot_pos].set(jnp.arange(count, dtype=jnp.int32) // TOP)
    row_live = (row_owner >= 0)[:, None]
    row_index = jnp.maximum(row_owner, 0)
    tok_rows = jnp.where(row_live, tokens_dev[row_index], jnp.zeros((), tokens_dev.dtype))
    grad_rows = jnp.where(row_live, grads_dev[row_index], jnp.zeros((), grads_dev.dtype))
    route_rows = jnp.zeros((SLOTS * CAP,), weights_dev.dtype).at[slot_pos].set(weights_dev.reshape(-1))
    return tok_rows, grad_rows, route_rows


def expert_rows(tok_rows, grad_rows, route_rows, gate_w, up_w, down_w):
    gate_pre = jnp.dot(tok_rows, gate_w, preferred_element_type=jnp.float32)
    up_pre = jnp.dot(tok_rows, up_w, preferred_element_type=jnp.float32)
    sigma = jax.nn.sigmoid(gate_pre)
    active = gate_pre * sigma
    hidden = (active * up_pre).astype(jnp.bfloat16)
    expert_out = jnp.dot(hidden, down_w.T, preferred_element_type=jnp.float32)
    prob_grad = jnp.sum(grad_rows.astype(jnp.float32) * expert_out, axis=1).astype(jnp.bfloat16)
    scaled = (route_rows.astype(jnp.float32)[:, None] * grad_rows.astype(jnp.float32)).astype(jnp.bfloat16)
    hidden_grad = jnp.dot(scaled, down_w, preferred_element_type=jnp.float32)
    gate_grad = (hidden_grad * up_pre * sigma * (1.0 + gate_pre * (1.0 - sigma))).astype(jnp.bfloat16)
    up_grad = (hidden_grad * active).astype(jnp.bfloat16)
    row_grad = (jnp.dot(gate_grad, gate_w.T, preferred_element_type=jnp.float32)
                + jnp.dot(up_grad, up_w.T, preferred_element_type=jnp.float32)).astype(jnp.bfloat16)
    sum_gate = jnp.dot(tok_rows.T, gate_grad, preferred_element_type=jnp.float32)
    sum_up = jnp.dot(tok_rows.T, up_grad, preferred_element_type=jnp.float32)
    sum_down = jnp.dot(scaled.T, hidden, preferred_element_type=jnp.float32)
    return row_grad, prob_grad, sum_gate, sum_up, sum_down


def pick_rows(rows, slot_pos):
    return rows[slot_pos]


def reference(tokens_in, grad_out, route_weight, slot_of, replica_of, w_gate, w_up, w_down):
    sources = TOKENS // TOK_DEV
    norm_scale = TOKENS ** -0.5
    section_list, route_list, gate_list, up_list, down_list = [], [], [], [], []
    for section in range(SECTIONS):
        slot_expert = slot_table(replica_of[section])
        slot_pos = jax.vmap(pair_rows)(slot_of[section].reshape(sources, TOK_DEV, TOP))
        tok_rows, grad_rows, route_rows = jax.vmap(pack_rows)(
            tokens_in[section].reshape(sources, TOK_DEV, D),
            grad_out[section].reshape(sources, TOK_DEV, D),
            route_weight[section].reshape(sources, TOK_DEV, TOP),
            slot_pos)

        def by_slot(rows):
            rows = rows.reshape((sources, SLOTS, CAP) + rows.shape[2:])
            rows = jnp.moveaxis(rows, 1, 0)
            return rows.reshape((SLOTS, sources * CAP) + rows.shape[3:])

        def by_source(rows):
            rows = rows.reshape((SLOTS, sources, CAP) + rows.shape[2:])
            rows = jnp.moveaxis(rows, 1, 0)
            return rows.reshape((sources, SLOTS * CAP) + rows.shape[3:])

        gate_all = w_gate[section]
        up_all = w_up[section]
        down_all = w_down[section]

        def step_slot(sums, inputs):
            slot_index, tok_slot, grad_slot, route_slot = inputs
            expert = slot_expert[slot_index]
            row_grad, prob_grad, sum_gate, sum_up, sum_down = expert_rows(
                tok_slot, grad_slot, route_slot, gate_all[expert], up_all[expert], down_all[expert])
            sums = (sums[0].at[expert].add(sum_gate), sums[1].at[expert].add(sum_up), sums[2].at[expert].add(sum_down))
            return sums, (row_grad, prob_grad)

        zero_sums = jnp.zeros((EXPERTS, D, FF), jnp.float32)
        sums, outputs = lax.scan(step_slot, (zero_sums, zero_sums, zero_sums),
                                 (jnp.arange(SLOTS, dtype=jnp.int32), by_slot(tok_rows), by_slot(grad_rows), by_slot(route_rows)))
        back_rows = by_source(outputs[0])
        back_prob = by_source(outputs[1])
        pair_grad = jax.vmap(pick_rows)(back_rows, slot_pos)
        branch = jnp.sum(pair_grad.astype(jnp.float32).reshape(sources, TOK_DEV, TOP, D), axis=2).astype(jnp.bfloat16)
        route_list.append(jax.vmap(pick_rows)(back_prob, slot_pos).reshape(TOKENS, TOP))
        section_list.append((grad_out[section].astype(jnp.float32) + branch.reshape(TOKENS, D).astype(jnp.float32)).astype(jnp.bfloat16))
        gate_list.append((sums[0] * norm_scale).astype(jnp.bfloat16))
        up_list.append((sums[1] * norm_scale).astype(jnp.bfloat16))
        down_list.append((sums[2] * norm_scale).astype(jnp.bfloat16))
    grad_in = jnp.roll(jnp.stack(section_list), -1, axis=0)
    return grad_in, jnp.stack(route_list), jnp.stack(gate_list), jnp.stack(up_list), jnp.stack(down_list)
```

```python
import jax
import jax.numpy as jnp
from jax import lax
from jax.experimental import pallas as pl
from jax.experimental.pallas import tpu as pltpu
from jax.sharding import PartitionSpec as P

EXPERTS = 8
CAP = 20
SLOTS = 16
ROWS = SLOTS * CAP
BACK = 24
TOK = 128
D = 2048
FF = 512
HALF = 256
PART = 128
BF = jnp.bfloat16
F32 = jnp.float32
MIB = 1 << 20


def place(zh, c, k, b):
    return (2 * zh + c) * 4 + 2 * k + b


SPOTS = [(zh, c, k, b) for zh in range(2) for c in range(2) for k in range(2) for b in range(2)]
TURN = [(place(zh, c, k, b), place(zh, k, c, b)) for zh, c, k, b in SPOTS]
CORES = [(place(zh, c, k, b), place(zh, 1 - c, k, b)) for zh, c, k, b in SPOTS]
NEAR = [(place(zh, c, k, b), place(zh, c, k, 1 - b)) for zh, c, k, b in SPOTS]
CROSS = [(place(zh, c, k, b), place(zh, k, 1 - c, b)) for zh, c, k, b in SPOTS]
BEHIND = [(place(zh, c, k, b), ((2 * zh + k - 1) % 4) * 4 + 2 * c + b) for zh, c, k, b in SPOTS]


def move(x, pairs):
    return lax.ppermute(x, ("pipe", "dp"), pairs)


def spread(x):
    return lax.all_to_all(x, "expert", split_axis=0, concat_axis=0, tiled=True)


def mm(a, b, dims=((1,), (0,))):
    return lax.dot_general(a, b, (dims, ((), ())), preferred_element_type=F32)


def count(shape, dim):
    return lax.broadcasted_iota(jnp.int32, shape, dim).astype(F32)


def split_by(index, size):
    block = jnp.floor((index + 0.5) * (1.0 / size))
    return block, index - block * size


def vmem(limit, **kw):
    return pltpu.CompilerParams(vmem_limit_bytes=limit * MIB, **kw)


def pick_kernel(info, gate, up, down, ogate, oup, odown, out, held, sem_in, sem_out):
    half = info[SLOTS]
    lanes = pl.ds(pl.multiple_of(half * HALF, HALF), HALF)

    def fetch(refs):
        copies = [
            pltpu.make_async_copy(ref.at[0, :, :, lanes], held.at[n], sem_in.at[n])
            for n, ref in enumerate(refs)
        ]
        for copy in copies:
            copy.start()
        for copy in copies:
            copy.wait()

    @pl.when(info[SLOTS + 1] == 1)
    def _():
        fetch((gate, up, down))

    @pl.when(info[SLOTS + 1] == 0)
    def _():
        fetch((ogate, oup, odown))

    copies = [
        pltpu.make_async_copy(
            held.at[n, info[slot]],
            out.at[slot, pl.ds(n * PART, PART), :],
            sem_out.at[slot * 3 + n],
        )
        for slot in range(SLOTS)
        for n in range(3)
    ]
    for copy in copies:
        copy.start()
    for copy in copies:
        copy.wait()


def pick_weights(info, mine, others):
    anywhere = pl.BlockSpec(memory_space=pl.ANY)
    return pl.pallas_call(
        pick_kernel,
        out_shape=jax.ShapeDtypeStruct((SLOTS, 3 * PART, HALF), BF),
        in_specs=[pl.BlockSpec(memory_space=pltpu.SMEM)] + [anywhere] * 6,
        out_specs=anywhere,
        scratch_shapes=[
            pltpu.VMEM((3, EXPERTS, PART, HALF), BF),
            pltpu.SemaphoreType.DMA((3,)),
            pltpu.SemaphoreType.DMA((3 * SLOTS,)),
        ],
        compiler_params=vmem(16),
        cost_estimate=pl.CostEstimate(flops=0, bytes_accessed=5 * MIB, transcendentals=0),
    )(info, *mine, *others)


def seats(notes, size, caps):
    rows = SLOTS * size
    slot, at = split_by(count((rows, 1), 0), size)
    second, rank = split_by(at, caps)
    first = notes[0:1, :] == slot
    other = notes[1:2, :] == slot
    held = jnp.where(first | other, 1.0, 0.0)
    before = jnp.where(count((TOK, TOK), 0) < count((TOK, TOK), 1), 1.0, 0.0)
    taken = mm(held.astype(BF), before.astype(BF))
    seat = jnp.where(taken == rank, held, 0.0)
    return seat, first, second


def pack_kernel(notes_ref, x_ref, g_ref, out_ref):
    notes = notes_ref[...].astype(F32)
    seat, first, second = seats(notes, 2 * CAP, CAP)
    weight = jnp.where(first, notes[2:3, :], notes[3:4, :])
    pick_x = jnp.where(second == 0.0, seat, 0.0).astype(BF)
    pick_g = jnp.where(second == 1.0, seat * weight, 0.0).astype(BF)
    for n in range(4):
        at = pl.ds(n * 512, 512)
        out_ref[:, at] = (mm(pick_x, x_ref[:, at]) + mm(pick_g, g_ref[:, at])).astype(BF)


def pack_rows(notes, x, g):
    return pl.pallas_call(
        pack_kernel,
        out_shape=jax.ShapeDtypeStruct((2 * ROWS, D), BF),
        compiler_params=vmem(32),
        cost_estimate=pl.CostEstimate(
            flops=4 * 2 * ROWS * TOK * D, bytes_accessed=4 * MIB, transcendentals=0
        ),
    )(notes, x, g)


def expert_kernel(
    rows_ref, own_ref, oth_ref, back_ref, x_ref, s_ref, hid_ref, gu_ref, wg, wu, wd, sem
):
    stacks = (wg, wu, wd)
    for n, stack in enumerate(stacks):
        for src in range(SLOTS):
            for side, ref in enumerate((own_ref, oth_ref)):
                pltpu.make_async_copy(
                    ref.at[src, pl.ds(n * PART, PART), :],
                    stack.at[pl.ds(src * PART, PART), pl.ds(side * HALF, HALF)],
                    sem.at[n],
                ).start()
    source = count((1, 2 * ROWS), 1)
    block, at = split_by(count((ROWS, 1), 0), CAP)
    take_x = jnp.where(source == block * (2 * CAP) + at, 1.0, 0.0).astype(BF)
    take_s = jnp.where(source == block * (2 * CAP) + CAP + at, 1.0, 0.0).astype(BF)
    for n in range(4):
        cols = pl.ds(n * 512, 512)
        x_ref[:, cols] = mm(take_x, rows_ref[:, cols]).astype(BF)
        s_ref[:, cols] = mm(take_s, rows_ref[:, cols]).astype(BF)
    for n, stack in enumerate(stacks):
        pltpu.make_async_copy(stack, stack, sem.at[n]).wait()
    gate_pre = mm(x_ref[...], wg[...])
    up_pre = mm(x_ref[...], wu[...])
    hidden_grad = mm(s_ref[...], wd[...])
    sigma = jax.nn.sigmoid(gate_pre)
    active = gate_pre * sigma
    hidden = (active * up_pre).astype(BF)
    gate_grad = (hidden_grad * up_pre * sigma * (1.0 + gate_pre * (1.0 - sigma))).astype(BF)
    up_grad = (hidden_grad * active).astype(BF)
    prob = jnp.sum(hidden.astype(F32) * hidden_grad, axis=1, keepdims=True)
    hid_ref[...] = hidden
    gu_ref[:, 0:FF] = gate_grad
    gu_ref[:, FF : 2 * FF] = up_grad
    row = count((1, ROWS), 1)
    row_block, _ = split_by(row, CAP)
    to_block, to_at = split_by(count((SLOTS * BACK, 1), 0), BACK)
    lay = jnp.where((to_at < CAP) & (row == to_block * CAP + to_at), 1.0, 0.0).astype(BF)
    lay_prob = jnp.where((to_at == CAP) & (row_block == to_block), 1.0, 0.0).astype(BF)
    prob_wide = jnp.where(count((1, PART), 1) == at, prob, 0.0).astype(BF)
    prob_rows = mm(lay_prob, prob_wide)
    dims = ((1,), (1,))
    for n in range(8):
        cols = pl.ds(n * 256, 256)
        grad = mm(gate_grad, wg[cols, :], dims) + mm(up_grad, wu[cols, :], dims)
        laid = mm(lay, grad.astype(BF))
        if n == 0:
            back_ref[:, 0:PART] = (laid[:, 0:PART] + prob_rows).astype(BF)
            back_ref[:, PART:256] = laid[:, PART:256].astype(BF)
        else:
            back_ref[:, cols] = laid.astype(BF)


def expert_rows(rows, own, oth):
    whole = pl.BlockSpec(memory_space=pltpu.VMEM)
    anywhere = pl.BlockSpec(memory_space=pl.ANY)
    return pl.pallas_call(
        expert_kernel,
        out_shape=[
            jax.ShapeDtypeStruct((SLOTS * BACK, D), BF),
            jax.ShapeDtypeStruct((ROWS, D), BF),
            jax.ShapeDtypeStruct((ROWS, D), BF),
            jax.ShapeDtypeStruct((ROWS, FF), BF),
            jax.ShapeDtypeStruct((ROWS, 2 * FF), BF),
        ],
        in_specs=[whole, anywhere, anywhere],
        out_specs=[whole] * 5,
        scratch_shapes=[
            pltpu.VMEM((D, FF), BF),
            pltpu.VMEM((D, FF), BF),
            pltpu.VMEM((D, FF), BF),
            pltpu.SemaphoreType.DMA((3,)),
        ],
        compiler_params=vmem(48),
        cost_estimate=pl.CostEstimate(
            flops=16 * ROWS * D * FF, bytes_accessed=14 * MIB, transcendentals=ROWS * FF
        ),
    )(rows, own, oth)


def sums_kernel(x_ref, s_ref, hid_ref, gu_ref, own_ref, oth_ref):
    dims = ((0,), (0,))
    for n in range(8):
        cols = pl.ds(n * 256, 256)
        both = mm(x_ref[:, cols], gu_ref[...], dims).astype(BF)
        down = mm(s_ref[:, cols], hid_ref[...], dims).astype(BF)
        for part in range(2):
            rows = slice(part * PART, (part + 1) * PART)
            for side, ref in enumerate((own_ref, oth_ref)):
                lanes = slice(side * HALF, (side + 1) * HALF)
                ups = slice(FF + side * HALF, FF + (side + 1) * HALF)
                ref[2 * n + part, 0:PART, :] = both[rows, lanes]
                ref[2 * n + part, PART : 2 * PART, :] = both[rows, ups]
                ref[2 * n + part, 2 * PART : 3 * PART, :] = down[rows, lanes]


def weight_sums(x, scaled, hidden, grads):
    shape = jax.ShapeDtypeStruct((SLOTS, 3 * PART, HALF), BF)
    return pl.pallas_call(
        sums_kernel,
        out_shape=[shape, shape],
        compiler_params=vmem(48),
        cost_estimate=pl.CostEstimate(
            flops=6 * ROWS * D * FF, bytes_accessed=9 * MIB, transcendentals=0
        ),
    )(x, scaled, hidden, grads)


def join_kernel(notes_ref, back_ref, g_ref, sect_ref, route_ref):
    notes = notes_ref[...].astype(F32)
    rows = SLOTS * BACK
    seat, first, second = seats(notes, BACK, CAP)
    seat = jnp.where(second == 0.0, seat, 0.0)
    slot, at = split_by(count((rows, 1), 0), BACK)
    to_prob = jnp.where(count((1, rows), 1) == slot * BACK + CAP, 1.0, 0.0).astype(BF)
    probs = mm(to_prob, back_ref[:, 0:PART])
    prob = jnp.sum(jnp.where(count((1, PART), 1) == at, probs, 0.0), axis=1, keepdims=True)
    share = seat * prob
    route_first = jnp.sum(jnp.where(first, share, 0.0), axis=0, keepdims=True)
    route_second = jnp.sum(jnp.where(first, 0.0, share), axis=0, keepdims=True)
    line = lax.broadcasted_iota(jnp.int32, (8, TOK), 0)
    route = jnp.where(
        line == 0,
        route_first / notes[2:3, :],
        jnp.where(line == 1, route_second / notes[3:4, :], 0.0),
    )
    route_ref[...] = route.astype(BF)
    pick = seat.astype(BF)
    for n in range(4):
        cols = pl.ds(n * 512, 512)
        branch = mm(pick, back_ref[:, cols], ((0,), (0,))).astype(BF).astype(F32)
        sect_ref[:, cols] = (g_ref[:, cols].astype(F32) + branch).astype(BF)


def join_rows(notes, back, g):
    return pl.pallas_call(
        join_kernel,
        out_shape=[jax.ShapeDtypeStruct((TOK, D), BF), jax.ShapeDtypeStruct((8, TOK), BF)],
        compiler_params=vmem(32),
        cost_estimate=pl.CostEstimate(
            flops=2 * SLOTS * BACK * TOK * D, bytes_accessed=3 * MIB, transcendentals=0
        ),
    )(notes, back, g)


def merge_kernel(info, got_ref, keep_ref, send_ref, keep_sum, send_sum):
    side = info[EXPERTS]
    mine = pl.ds(pl.multiple_of(side * 32, 32), 32)
    theirs = pl.ds(pl.multiple_of((1 - side) * 32, 32), 32)
    for sums, rows in ((keep_sum, mine), (send_sum, theirs)):
        for e in range(EXPERTS):
            sums[e] = got_ref[e, rows, :].astype(F32)
        for r in range(EXPERTS):
            e = info[r]
            sums[e] = sums[e] + got_ref[EXPERTS + r, rows, :].astype(F32)
    keep_ref[0, 0] = keep_sum[...].astype(BF)
    send_ref[0, 0] = send_sum[...].astype(BF)


def merge_slots(info, got):
    out = jax.ShapeDtypeStruct((3, 2, EXPERTS, 32, HALF), BF)
    block = pl.BlockSpec((1, 1, EXPERTS, 32, HALF), lambda n, q, info: (n, q, 0, 0, 0))
    return pl.pallas_call(
        merge_kernel,
        out_shape=[out, out],
        grid_spec=pltpu.PrefetchScalarGridSpec(
            num_scalar_prefetch=1,
            grid=(3, 2),
            in_specs=[pl.BlockSpec((SLOTS, 64, HALF), lambda n, q, info: (0, 2 * n + q, 0))],
            out_specs=[block, block],
            scratch_shapes=[pltpu.VMEM((EXPERTS, 32, HALF), F32)] * 2,
        ),
        compiler_params=vmem(32),
        cost_estimate=pl.CostEstimate(
            flops=SLOTS * 3 * PART * HALF, bytes_accessed=5 * MIB, transcendentals=0
        ),
    )(info, got)


def shards(tokens_in, grad_out, route_weight, slot_of, replica_of, w_gate, w_up, w_down):
    pipe, dp = lax.axis_index("pipe"), lax.axis_index("dp")
    core, side, near = pipe % 2, dp // 2, dp % 2
    mine = core == side

    weights = (w_gate, w_up, w_down)
    others = tuple(move(w, CORES) for w in weights)
    replicas = jnp.where(mine, replica_of[0], move(replica_of[0], CORES))

    notes = jnp.concatenate(
        [slot_of[0].T.astype(BF), route_weight[0].T, jnp.zeros((4, TOK), BF)], axis=0
    )
    notes = move(notes, TURN)
    x = move(tokens_in[0], TURN)
    g = move(grad_out[0], TURN)

    info = jnp.concatenate(
        [
            jnp.arange(EXPERTS, dtype=jnp.int32),
            replicas,
            jnp.stack([core, mine.astype(jnp.int32)]).astype(jnp.int32),
        ]
    )
    own = spread(pick_weights(info, weights, others))
    oth = move(own, CORES)

    rows = pack_rows(notes, x, g)
    rows = spread(rows.reshape(SLOTS, 2 * CAP, D)).reshape(2 * ROWS, D)
    back, xs, scaled, hidden, grads = expert_rows(rows, own, oth)
    back = spread(back.reshape(SLOTS, BACK, D)).reshape(SLOTS * BACK, D)
    sum_own, sum_oth = weight_sums(xs, scaled, hidden, grads)
    sum_oth = move(sum_oth, CORES)
    sums = (sum_own.astype(F32) + sum_oth.astype(F32)).astype(BF)

    sect, route = join_rows(notes, back, g)
    grad_in = move(sect, BEHIND)
    route = move(route, TURN)[0:2].T

    got = spread(sums)
    keep, send = merge_slots(jnp.concatenate([replicas, near[None].astype(jnp.int32)]), got)
    send = move(send, NEAR)
    total = ((keep.astype(F32) + send.astype(F32)) * (8192.0**-0.5)).astype(BF)
    first = move(lax.dynamic_index_in_dim(total, core, 1, keepdims=False), TURN)
    second = move(lax.dynamic_index_in_dim(total, 1 - core, 1, keepdims=False), CROSS)
    low = jnp.where(side == 0, first, second)
    high = jnp.where(side == 0, second, first)
    final = jnp.concatenate([low, high], axis=-1)
    return (grad_in[None], route[None], final[0][None], final[1][None], final[2][None])


def solution(mesh):
    return jax.shard_map(
        shards,
        mesh=mesh,
        in_specs=(
            P("pipe", ("expert", "dp"), None),
            P("pipe", ("expert", "dp"), None),
            P("pipe", ("expert", "dp"), None),
            P("pipe", ("expert", "dp"), None),
            P("pipe", None),
            P("pipe", None, "expert", None),
            P("pipe", None, "expert", None),
            P("pipe", None, "expert", None),
        ),
        out_specs=(
            P("pipe", ("expert", "dp"), None),
            P("pipe", ("expert", "dp"), None),
            P("pipe", None, ("expert", "dp"), None),
            P("pipe", None, ("expert", "dp"), None),
            P("pipe", None, ("expert", "dp"), None),
        ),
        check_vma=False,
    )
```

```python
import functools

import jax
import jax.numpy as jnp
from jax import lax
from jax.experimental import pallas as pl
from jax.experimental.pallas import tpu as pltpu
from jax.sharding import PartitionSpec as P

EXPERTS = 8
CAP = 20
SLOTS = 16
ROWS = SLOTS * CAP
BACK = 24
TOK = 128
D = 2048
FF = 512
PART = 128
BF = jnp.bfloat16
F32 = jnp.float32
MIB = 1 << 20
SCALE = 8192.0**-0.5


def place(zh, c, k, b):
    return (2 * zh + c) * 4 + 2 * k + b


SPOTS = [(zh, c, k, b) for zh in range(2) for c in range(2) for k in range(2) for b in range(2)]
TURN = [(place(zh, c, k, b), place(zh, k, c, b)) for zh, c, k, b in SPOTS]
CORES = [(place(zh, c, k, b), place(zh, 1 - c, k, b)) for zh, c, k, b in SPOTS]
NEAR = [(place(zh, c, k, b), place(zh, c, k, 1 - b)) for zh, c, k, b in SPOTS]
OWNER = [
    [(place(zh, c, k, b), (2 * zh + k) * 4 + ((2 * c + b) ^ j)) for zh, c, k, b in SPOTS]
    for j in range(4)
]
BEHIND = [(place(zh, c, k, b), ((2 * zh + k - 1) % 4) * 4 + 2 * c + b) for zh, c, k, b in SPOTS]


def move(x, pairs):
    return lax.ppermute(x, ("pipe", "dp"), pairs)


def spread(x):
    return lax.all_to_all(x, "expert", split_axis=0, concat_axis=0, tiled=True)


def mm(a, b, dims=((1,), (0,))):
    return lax.dot_general(a, b, (dims, ((), ())), preferred_element_type=F32)


def count(shape, dim):
    return lax.broadcasted_iota(jnp.int32, shape, dim).astype(F32)


def split_by(index, size):
    block = jnp.floor((index + 0.5) * (1.0 / size))
    return block, index - block * size


def vmem(limit, **kw):
    return pltpu.CompilerParams(vmem_limit_bytes=limit * MIB, **kw)


def pick_kernel(info, gate, up, down, ogate, oup, odown, out, sem):
    lanes = pl.ds(pl.multiple_of(info[SLOTS] * PART, PART), PART)

    def send(refs):
        copies = [
            pltpu.make_async_copy(
                ref.at[info[slot]],
                out.at[slot, pl.ds(n * PART, PART), :],
                sem.at[slot * 3 + n],
            )
            for slot in range(SLOTS)
            for n, ref in enumerate(refs)
        ]
        for copy in copies:
            copy.start()
        for copy in copies:
            copy.wait()

    @pl.when(info[SLOTS + 1] == 1)
    def _():
        send([ref.at[0, :, :, lanes] for ref in (gate, up, down)])

    @pl.when(info[SLOTS + 1] == 0)
    def _():
        send((ogate, oup, odown))


def pick_weights(info, mine, others):
    hbm = pl.BlockSpec(memory_space=pltpu.HBM)
    anywhere = pl.BlockSpec(memory_space=pl.ANY)
    return pl.pallas_call(
        pick_kernel,
        out_shape=jax.ShapeDtypeStruct((SLOTS, 3 * PART, PART), BF),
        in_specs=[pl.BlockSpec(memory_space=pltpu.SMEM)] + [hbm] * 3 + [anywhere] * 3,
        out_specs=anywhere,
        scratch_shapes=[pltpu.SemaphoreType.DMA((3 * SLOTS,))],
        compiler_params=vmem(60),
        cost_estimate=pl.CostEstimate(flops=0, bytes_accessed=4 * MIB, transcendentals=0),
    )(info, *mine, *others)


def seats(notes, size, caps):
    rows = SLOTS * size
    slot, at = split_by(count((rows, 1), 0), size)
    second, rank = split_by(at, caps)
    first = notes[0:1, :] == slot
    other = notes[1:2, :] == slot
    held = jnp.where(first | other, 1.0, 0.0)
    before = jnp.where(count((TOK, TOK), 0) < count((TOK, TOK), 1), 1.0, 0.0)
    taken = mm(held.astype(BF), before.astype(BF))
    seat = jnp.where(taken == rank, held, 0.0)
    return seat, first, second


def pack_kernel(notes_ref, x_ref, g_ref, out_ref):
    notes = notes_ref[...].astype(F32)
    seat, first, second = seats(notes, 2 * CAP, CAP)
    weight = jnp.where(first, notes[2:3, :], notes[3:4, :])
    pick_x = jnp.where(second == 0.0, seat, 0.0).astype(BF)
    pick_g = jnp.where(second == 1.0, seat * weight, 0.0).astype(BF)
    for n in range(4):
        at = pl.ds(n * 512, 512)
        out_ref[:, at] = (mm(pick_x, x_ref[:, at]) + mm(pick_g, g_ref[:, at])).astype(BF)


def pack_rows(notes, x, g):
    return pl.pallas_call(
        pack_kernel,
        out_shape=jax.ShapeDtypeStruct((2 * ROWS, D), BF),
        compiler_params=vmem(32),
        cost_estimate=pl.CostEstimate(
            flops=4 * 2 * ROWS * TOK * D, bytes_accessed=4 * MIB, transcendentals=0
        ),
    )(notes, x, g)


def expert_kernel(
    rows_ref, w0, w1, w2, w3, back_ref, x_ref, s_ref, hid_ref, gu_ref, sg, su, sd, sem
):
    copies = [
        pltpu.make_async_copy(
            ref.at[:, pl.ds(n * PART, PART), :],
            stack.at[:, :, pl.ds(side * PART, PART)],
            sem.at[4 * n + side],
        )
        for n, stack in enumerate((sg, su, sd))
        for side, ref in enumerate((w0, w1, w2, w3))
    ]
    for copy in copies:
        copy.start()
    wg, wu, wd = sg.reshape(D, FF), su.reshape(D, FF), sd.reshape(D, FF)
    source = count((1, 2 * ROWS), 1)
    block, at = split_by(count((ROWS, 1), 0), CAP)
    take_x = jnp.where(source == block * (2 * CAP) + at, 1.0, 0.0).astype(BF)
    take_s = jnp.where(source == block * (2 * CAP) + CAP + at, 1.0, 0.0).astype(BF)
    for n in range(4):
        cols = pl.ds(n * 512, 512)
        x_ref[:, cols] = mm(take_x, rows_ref[:, cols]).astype(BF)
        s_ref[:, cols] = mm(take_s, rows_ref[:, cols]).astype(BF)
    for copy in copies:
        copy.wait()
    gate_pre = mm(x_ref[...], wg[...])
    up_pre = mm(x_ref[...], wu[...])
    hidden_grad = mm(s_ref[...], wd[...])
    sigma = jax.nn.sigmoid(gate_pre)
    active = gate_pre * sigma
    hidden = (active * up_pre).astype(BF)
    gate_grad = (hidden_grad * up_pre * sigma * (1.0 + gate_pre * (1.0 - sigma))).astype(BF)
    up_grad = (hidden_grad * active).astype(BF)
    prob = jnp.sum(hidden.astype(F32) * hidden_grad, axis=1, keepdims=True)
    hid_ref[...] = hidden
    gu_ref[:, 0:FF] = gate_grad
    gu_ref[:, FF : 2 * FF] = up_grad
    row = count((1, ROWS), 1)
    row_block, _ = split_by(row, CAP)
    to_block, to_at = split_by(count((SLOTS * BACK, 1), 0), BACK)
    lay = jnp.where((to_at < CAP) & (row == to_block * CAP + to_at), 1.0, 0.0).astype(BF)
    lay_prob = jnp.where((to_at == CAP) & (row_block == to_block), 1.0, 0.0).astype(BF)
    prob_wide = jnp.where(count((1, PART), 1) == at, prob, 0.0).astype(BF)
    prob_rows = mm(lay_prob, prob_wide)
    dims = ((1,), (1,))
    for n in range(8):
        cols = pl.ds(n * 256, 256)
        grad = mm(gate_grad, wg[cols, :], dims) + mm(up_grad, wu[cols, :], dims)
        laid = mm(lay, grad.astype(BF))
        if n == 0:
            back_ref[:, 0:PART] = (laid[:, 0:PART] + prob_rows).astype(BF)
            back_ref[:, PART:256] = laid[:, PART:256].astype(BF)
        else:
            back_ref[:, cols] = laid.astype(BF)


def expert_rows(rows, quarters):
    whole = pl.BlockSpec(memory_space=pltpu.VMEM)
    anywhere = pl.BlockSpec(memory_space=pl.ANY)
    return pl.pallas_call(
        expert_kernel,
        out_shape=[
            jax.ShapeDtypeStruct((SLOTS * BACK, D), BF),
            jax.ShapeDtypeStruct((ROWS, D), BF),
            jax.ShapeDtypeStruct((ROWS, D), BF),
            jax.ShapeDtypeStruct((ROWS, FF), BF),
            jax.ShapeDtypeStruct((ROWS, 2 * FF), BF),
        ],
        in_specs=[whole] + [anywhere] * 4,
        out_specs=[whole] * 5,
        scratch_shapes=[
            pltpu.VMEM((SLOTS, PART, FF), BF),
            pltpu.VMEM((SLOTS, PART, FF), BF),
            pltpu.VMEM((SLOTS, PART, FF), BF),
            pltpu.SemaphoreType.DMA((12,)),
        ],
        compiler_params=vmem(48),
        cost_estimate=pl.CostEstimate(
            flops=16 * ROWS * D * FF, bytes_accessed=14 * MIB, transcendentals=ROWS * FF
        ),
    )(rows, *quarters)


def sums_kernel(kinds, a_ref, b_ref, own_ref, oth_ref):
    for n in range(8):
        part = mm(a_ref[:, pl.ds(n * 256, 256)], b_ref[...], ((0,), (0,))).astype(BF)
        for piece in range(2):
            rows = slice(piece * PART, (piece + 1) * PART)
            for kind in range(kinds):
                for q in range(4):
                    lanes = slice(kind * FF + q * PART, kind * FF + (q + 1) * PART)
                    ref = own_ref if q < 2 else oth_ref
                    ref[q % 2, 2 * n + piece, kind * PART : (kind + 1) * PART, :] = part[rows, lanes]


def weight_sums(a, b):
    kinds = b.shape[1] // FF
    shape = jax.ShapeDtypeStruct((2, SLOTS, kinds * PART, PART), BF)
    return pl.pallas_call(
        functools.partial(sums_kernel, kinds),
        out_shape=[shape, shape],
        compiler_params=vmem(48),
        cost_estimate=pl.CostEstimate(
            flops=2 * kinds * ROWS * D * FF, bytes_accessed=3 * kinds * MIB, transcendentals=0
        ),
    )(a, b)


def join_kernel(notes_ref, back_ref, g_ref, sect_ref, route_ref):
    notes = notes_ref[...].astype(F32)
    rows = SLOTS * BACK
    seat, first, second = seats(notes, BACK, CAP)
    seat = jnp.where(second == 0.0, seat, 0.0)
    slot, at = split_by(count((rows, 1), 0), BACK)
    to_prob = jnp.where(count((1, rows), 1) == slot * BACK + CAP, 1.0, 0.0).astype(BF)
    probs = mm(to_prob, back_ref[:, 0:PART])
    prob = jnp.sum(jnp.where(count((1, PART), 1) == at, probs, 0.0), axis=1, keepdims=True)
    share = seat * prob
    route_first = jnp.sum(jnp.where(first, share, 0.0), axis=0, keepdims=True)
    route_second = jnp.sum(jnp.where(first, 0.0, share), axis=0, keepdims=True)
    line = lax.broadcasted_iota(jnp.int32, (8, TOK), 0)
    route = jnp.where(
        line == 0,
        route_first / notes[2:3, :],
        jnp.where(line == 1, route_second / notes[3:4, :], 0.0),
    )
    route_ref[...] = route.astype(BF)
    pick = seat.astype(BF)
    for n in range(4):
        cols = pl.ds(n * 512, 512)
        branch = mm(pick, back_ref[:, cols], ((0,), (0,))).astype(BF).astype(F32)
        sect_ref[:, cols] = (g_ref[:, cols].astype(F32) + branch).astype(BF)


def join_rows(notes, back, g):
    return pl.pallas_call(
        join_kernel,
        out_shape=[jax.ShapeDtypeStruct((TOK, D), BF), jax.ShapeDtypeStruct((8, TOK), BF)],
        compiler_params=vmem(32),
        cost_estimate=pl.CostEstimate(
            flops=2 * SLOTS * BACK * TOK * D, bytes_accessed=3 * MIB, transcendentals=0
        ),
    )(notes, back, g)


def merge_kernel(kinds, info, got_ref, out0, out1, out2, out3, sums):
    for j, out in enumerate((out0, out1, out2, out3)):
        quarter = lax.bitwise_xor(info[EXPERTS], j)
        for kind in range(kinds):
            rows = pl.ds(pl.multiple_of(kind * PART + quarter * 32, 32), 32)
            for e in range(EXPERTS):
                sums[e] = got_ref[e, rows, :].astype(F32)
            for r in range(EXPERTS):
                e = info[r]
                sums[e] = sums[e] + got_ref[EXPERTS + r, rows, :].astype(F32)
            out[kind] = (sums[...] * SCALE).astype(BF)


def merge_slots(info, got):
    kinds = got.shape[1] // PART
    out = jax.ShapeDtypeStruct((kinds, EXPERTS, 32, PART), BF)
    return pl.pallas_call(
        functools.partial(merge_kernel, kinds),
        out_shape=[out] * 4,
        in_specs=[pl.BlockSpec(memory_space=pltpu.SMEM), pl.BlockSpec(memory_space=pltpu.VMEM)],
        scratch_shapes=[pltpu.VMEM((EXPERTS, 32, PART), F32)],
        compiler_params=vmem(32),
        cost_estimate=pl.CostEstimate(
            flops=SLOTS * kinds * PART * PART, bytes_accessed=kinds * MIB, transcendentals=0
        ),
    )(info, got)


def owners(parts):
    return tuple(move(part, OWNER[j]) for j, part in enumerate(parts))


def final_kernel(info, *refs):
    downs, pairs, (gate, up, down) = refs[0:4], refs[4:8], refs[8:11]
    for j in range(4):
        lanes = pl.ds(pl.multiple_of(lax.bitwise_xor(info[0], j) * PART, PART), PART)
        down[0, :, :, lanes] = downs[j][0]
        gate[0, :, :, lanes] = pairs[j][0]
        up[0, :, :, lanes] = pairs[j][1]


def finals(info, downs, pairs):
    whole = pl.BlockSpec(memory_space=pltpu.VMEM)
    out = jax.ShapeDtypeStruct((1, EXPERTS, 32, FF), BF)
    return pl.pallas_call(
        final_kernel,
        out_shape=[out] * 3,
        in_specs=[pl.BlockSpec(memory_space=pltpu.SMEM)] + [whole] * 8,
        compiler_params=vmem(32),
        cost_estimate=pl.CostEstimate(flops=0, bytes_accessed=2 * MIB, transcendentals=0),
    )(info, *downs, *pairs)


def add_up(own, others):
    others = move(others, CORES)
    send = (own[1].astype(F32) + others[1].astype(F32)).astype(BF)
    got = move(send, NEAR)
    return (own[0].astype(F32) + others[0].astype(F32) + got.astype(F32)).astype(BF)


def shards(tokens_in, grad_out, route_weight, slot_of, replica_of, w_gate, w_up, w_down):
    pipe, dp = lax.axis_index("pipe"), lax.axis_index("dp")
    core, side, near = pipe % 2, dp // 2, dp % 2
    mine = core == side
    quarter = (2 * core + near).astype(jnp.int32)

    notes = jnp.concatenate(
        [slot_of[0].T.astype(BF), route_weight[0].T, jnp.zeros((4, TOK), BF)], axis=0
    )
    notes = move(notes, TURN)
    x = move(tokens_in[0], TURN)
    g = move(grad_out[0], TURN)

    weights = (w_gate, w_up, w_down)
    asked = (2 * (1 - core) + near) * PART
    others = tuple(move(lax.dynamic_slice_in_dim(w[0], asked, PART, 2), CORES) for w in weights)
    replicas = jnp.where(mine, replica_of[0], move(replica_of[0], CORES))
    info = jnp.concatenate(
        [
            jnp.arange(EXPERTS, dtype=jnp.int32),
            replicas,
            jnp.stack([quarter, mine.astype(jnp.int32)]),
        ]
    )
    first = spread(pick_weights(info, weights, others))
    rows = pack_rows(notes, x, g)
    first, rows = lax.optimization_barrier((first, rows))
    second = move(first, NEAR)
    third, fourth = move(first, CORES), move(second, CORES)

    rows = spread(rows.reshape(SLOTS, 2 * CAP, D)).reshape(2 * ROWS, D)
    back, xs, scaled, hidden, grads = expert_rows(rows, (first, second, third, fourth))
    back = spread(back.reshape(SLOTS, BACK, D)).reshape(SLOTS * BACK, D)
    down = add_up(*weight_sums(scaled, hidden))
    pair = add_up(*weight_sums(xs, grads))

    sect, route = join_rows(notes, back, g)
    grad_in = move(sect, BEHIND)
    route = move(route, TURN)[0:2].T

    info = jnp.concatenate([replicas, quarter[None]])
    downs = owners(merge_slots(info, spread(down)))
    pairs = owners(merge_slots(info, spread(pair)))
    gate, up, down = finals(dp[None].astype(jnp.int32), downs, pairs)
    return (grad_in[None], route[None], gate, up, down)


def solution(mesh):
    return jax.shard_map(
        shards,
        mesh=mesh,
        in_specs=(
            P("pipe", ("expert", "dp"), None),
            P("pipe", ("expert", "dp"), None),
            P("pipe", ("expert", "dp"), None),
            P("pipe", ("expert", "dp"), None),
            P("pipe", None),
            P("pipe", None, "expert", None),
            P("pipe", None, "expert", None),
            P("pipe", None, "expert", None),
        ),
        out_specs=(
            P("pipe", ("expert", "dp"), None),
            P("pipe", ("expert", "dp"), None),
            P("pipe", None, ("expert", "dp"), None),
            P("pipe", None, ("expert", "dp"), None),
            P("pipe", None, ("expert", "dp"), None),
        ),
        check_vma=False,
    )
```

```python
import functools

import jax
import jax.numpy as jnp
from jax import lax
from jax.experimental import pallas as pl
from jax.experimental.pallas import tpu as pltpu
from jax.sharding import PartitionSpec as P

EXPERTS = 8
CAP = 20
SLOTS = 16
ROWS = SLOTS * CAP
BACK = 24
TOK = 128
D = 2048
FF = 512
PART = 128
BF = jnp.bfloat16
F32 = jnp.float32
MIB = 1 << 20
SCALE = 8192.0**-0.5


def place(zh, c, k, b):
    return (2 * zh + c) * 4 + 2 * k + b


SPOTS = [(zh, c, k, b) for zh in range(2) for c in range(2) for k in range(2) for b in range(2)]
TURN = [(place(zh, c, k, b), place(zh, k, c, b)) for zh, c, k, b in SPOTS]
CORES = [(place(zh, c, k, b), place(zh, 1 - c, k, b)) for zh, c, k, b in SPOTS]
NEAR = [(place(zh, c, k, b), place(zh, c, k, 1 - b)) for zh, c, k, b in SPOTS]
OWNER = [
    [(place(zh, c, k, b), (2 * zh + k) * 4 + ((2 * c + b) ^ j)) for zh, c, k, b in SPOTS]
    for j in range(4)
]
BEHIND = [(place(zh, c, k, b), ((2 * zh + k - 1) % 4) * 4 + 2 * c + b) for zh, c, k, b in SPOTS]


def move(x, pairs):
    return lax.ppermute(x, ("pipe", "dp"), pairs)


def spread(x):
    return lax.all_to_all(x, "expert", split_axis=0, concat_axis=0, tiled=True)


def mm(a, b, dims=((1,), (0,))):
    return lax.dot_general(a, b, (dims, ((), ())), preferred_element_type=F32)


def count(shape, dim):
    return lax.broadcasted_iota(jnp.int32, shape, dim).astype(F32)


def split_by(index, size):
    block = jnp.floor((index + 0.5) * (1.0 / size))
    return block, index - block * size


def vmem(limit, **kw):
    return pltpu.CompilerParams(vmem_limit_bytes=limit * MIB, **kw)


def pick_kernel(info, gate, up, down, ogate, oup, odown, out, held, sem_in, sem_out):
    lanes = pl.ds(pl.multiple_of(info[SLOTS] * PART, PART), PART)

    def fetch(refs):
        copies = [
            pltpu.make_async_copy(ref, held.at[n], sem_in.at[n]) for n, ref in enumerate(refs)
        ]
        for copy in copies:
            copy.start()
        for copy in copies:
            copy.wait()

    @pl.when(info[SLOTS + 1] == 1)
    def _():
        fetch([ref.at[0, :, :, lanes] for ref in (gate, up, down)])

    @pl.when(info[SLOTS + 1] == 0)
    def _():
        fetch((ogate, oup, odown))

    copies = [
        pltpu.make_async_copy(
            held.at[n, info[slot]],
            out.at[slot, pl.ds(n * PART, PART), :],
            sem_out.at[slot * 3 + n],
        )
        for slot in range(SLOTS)
        for n in range(3)
    ]
    for copy in copies:
        copy.start()
    for copy in copies:
        copy.wait()


def pick_weights(info, mine, others):
    hbm = pl.BlockSpec(memory_space=pltpu.HBM)
    anywhere = pl.BlockSpec(memory_space=pl.ANY)
    return pl.pallas_call(
        pick_kernel,
        out_shape=jax.ShapeDtypeStruct((SLOTS, 3 * PART, PART), BF),
        in_specs=[pl.BlockSpec(memory_space=pltpu.SMEM)] + [hbm] * 3 + [anywhere] * 3,
        out_specs=anywhere,
        scratch_shapes=[
            pltpu.VMEM((3, EXPERTS, PART, PART), BF),
            pltpu.SemaphoreType.DMA((3,)),
            pltpu.SemaphoreType.DMA((3 * SLOTS,)),
        ],
        compiler_params=vmem(60),
        cost_estimate=pl.CostEstimate(flops=0, bytes_accessed=4 * MIB, transcendentals=0),
    )(info, *mine, *others)


def seats(notes, size, caps):
    rows = SLOTS * size
    slot, at = split_by(count((rows, 1), 0), size)
    second, rank = split_by(at, caps)
    first = notes[0:1, :] == slot
    other = notes[1:2, :] == slot
    held = jnp.where(first | other, 1.0, 0.0)
    before = jnp.where(count((TOK, TOK), 0) < count((TOK, TOK), 1), 1.0, 0.0)
    taken = mm(held.astype(BF), before.astype(BF))
    seat = jnp.where(taken == rank, held, 0.0)
    return seat, first, second


def pack_kernel(notes_ref, x_ref, g_ref, out_ref):
    notes = notes_ref[...].astype(F32)
    seat, first, second = seats(notes, 2 * CAP, CAP)
    weight = jnp.where(first, notes[2:3, :], notes[3:4, :])
    pick_x = jnp.where(second == 0.0, seat, 0.0).astype(BF)
    pick_g = jnp.where(second == 1.0, seat * weight, 0.0).astype(BF)
    for n in range(4):
        at = pl.ds(n * 512, 512)
        out_ref[:, at] = (mm(pick_x, x_ref[:, at]) + mm(pick_g, g_ref[:, at])).astype(BF)


def pack_rows(notes, x, g):
    return pl.pallas_call(
        pack_kernel,
        out_shape=jax.ShapeDtypeStruct((2 * ROWS, D), BF),
        compiler_params=vmem(16),
        cost_estimate=pl.CostEstimate(
            flops=200 * ROWS * TOK * D, bytes_accessed=128 * MIB, transcendentals=0
        ),
    )(notes, x, g)


def expert_kernel(
    rows_ref,
    w0,
    w1,
    w2,
    w3,
    back_ref,
    x_ref,
    s_ref,
    hid_ref,
    gu_ref,
    sg,
    su,
    sd,
    sem,
):
    copies = [
        pltpu.make_async_copy(
            ref.at[:, pl.ds(n * PART, PART), :],
            stack.at[:, :, pl.ds(side * PART, PART)],
            sem.at[4 * n + side],
        )
        for n, stack in enumerate((sg, su, sd))
        for side, ref in enumerate((w0, w1, w2, w3))
    ]
    for copy in copies:
        copy.start()
    wg, wu, wd = sg.reshape(D, FF), su.reshape(D, FF), sd.reshape(D, FF)
    source = count((1, 2 * ROWS), 1)
    block, at = split_by(count((ROWS, 1), 0), CAP)
    take_x = jnp.where(source == block * (2 * CAP) + at, 1.0, 0.0).astype(BF)
    take_s = jnp.where(source == block * (2 * CAP) + CAP + at, 1.0, 0.0).astype(BF)
    for n in range(4):
        cols = pl.ds(n * 512, 512)
        x_ref[:, cols] = mm(take_x, rows_ref[:, cols]).astype(BF)
        s_ref[:, cols] = mm(take_s, rows_ref[:, cols]).astype(BF)
    for copy in copies:
        copy.wait()
    gate_pre = mm(x_ref[...], wg[...])
    up_pre = mm(x_ref[...], wu[...])
    hidden_grad = mm(s_ref[...], wd[...])
    sigma = jax.nn.sigmoid(gate_pre)
    active = gate_pre * sigma
    hidden = (active * up_pre).astype(BF)
    gate_grad = (hidden_grad * up_pre * sigma * (1.0 + gate_pre * (1.0 - sigma))).astype(BF)
    up_grad = (hidden_grad * active).astype(BF)
    prob = jnp.sum(hidden.astype(F32) * hidden_grad, axis=1, keepdims=True)
    hid_ref[...] = hidden
    gu_ref[:, 0:FF] = gate_grad
    gu_ref[:, FF : 2 * FF] = up_grad
    row = count((1, ROWS), 1)
    row_block, _ = split_by(row, CAP)
    to_block, to_at = split_by(count((SLOTS * BACK, 1), 0), BACK)
    lay = jnp.where((to_at < CAP) & (row == to_block * CAP + to_at), 1.0, 0.0).astype(BF)
    lay_prob = jnp.where((to_at == CAP) & (row_block == to_block), 1.0, 0.0).astype(BF)
    prob_wide = jnp.where(count((1, PART), 1) == at, prob, 0.0).astype(BF)
    prob_rows = mm(lay_prob, prob_wide)
    dims = ((1,), (1,))
    for n in range(8):
        cols = pl.ds(n * 256, 256)
        grad = mm(gate_grad, wg[cols, :], dims) + mm(up_grad, wu[cols, :], dims)
        laid = mm(lay, grad.astype(BF))
        if n == 0:
            back_ref[:, 0:PART] = (laid[:, 0:PART] + prob_rows).astype(BF)
            back_ref[:, PART:256] = laid[:, PART:256].astype(BF)
        else:
            back_ref[:, cols] = laid.astype(BF)


def expert_rows(rows, quarters):
    whole = pl.BlockSpec(memory_space=pltpu.VMEM)
    anywhere = pl.BlockSpec(memory_space=pl.ANY)
    return pl.pallas_call(
        expert_kernel,
        out_shape=[
            jax.ShapeDtypeStruct((SLOTS * BACK, D), BF),
            jax.ShapeDtypeStruct((ROWS, D), BF),
            jax.ShapeDtypeStruct((ROWS, D), BF),
            jax.ShapeDtypeStruct((ROWS, FF), BF),
            jax.ShapeDtypeStruct((ROWS, 2 * FF), BF),
        ],
        in_specs=[whole] + [anywhere] * 4,
        out_specs=[whole] * 5,
        scratch_shapes=[
            pltpu.VMEM((SLOTS, PART, FF), BF),
            pltpu.VMEM((SLOTS, PART, FF), BF),
            pltpu.VMEM((SLOTS, PART, FF), BF),
            pltpu.SemaphoreType.DMA((12,)),
        ],
        compiler_params=vmem(32),
        cost_estimate=pl.CostEstimate(
            flops=16 * ROWS * D * FF, bytes_accessed=14 * MIB, transcendentals=ROWS * FF
        ),
    )(rows, *quarters)


def sums_kernel(kinds, a_ref, b_ref, own_ref, oth_ref):
    for n in range(8):
        part = mm(a_ref[:, pl.ds(n * 256, 256)], b_ref[...], ((0,), (0,))).astype(BF)
        for piece in range(2):
            rows = slice(piece * PART, (piece + 1) * PART)
            for kind in range(kinds):
                for q in range(4):
                    lanes = slice(kind * FF + q * PART, kind * FF + (q + 1) * PART)
                    ref = own_ref if q < 2 else oth_ref
                    ref[q % 2, 2 * n + piece, kind * PART : (kind + 1) * PART, :] = part[rows, lanes]


def weight_sums(a, b):
    kinds = b.shape[1] // FF
    shape = jax.ShapeDtypeStruct((2, SLOTS, kinds * PART, PART), BF)
    return pl.pallas_call(
        functools.partial(sums_kernel, kinds),
        out_shape=[shape, shape],
        compiler_params=vmem(24),
        cost_estimate=pl.CostEstimate(
            flops=0, bytes_accessed=1024, transcendentals=0
        ),
    )(a, b)


def join_kernel(notes_ref, back_ref, g_ref, sect_ref, route_ref):
    notes = notes_ref[...].astype(F32)
    rows = SLOTS * BACK
    seat, first, second = seats(notes, BACK, CAP)
    seat = jnp.where(second == 0.0, seat, 0.0)
    slot, at = split_by(count((rows, 1), 0), BACK)
    to_prob = jnp.where(count((1, rows), 1) == slot * BACK + CAP, 1.0, 0.0).astype(BF)
    probs = mm(to_prob, back_ref[:, 0:PART])
    prob = jnp.sum(jnp.where(count((1, PART), 1) == at, probs, 0.0), axis=1, keepdims=True)
    share = seat * prob
    route_first = jnp.sum(jnp.where(first, share, 0.0), axis=0, keepdims=True)
    route_second = jnp.sum(jnp.where(first, 0.0, share), axis=0, keepdims=True)
    line = lax.broadcasted_iota(jnp.int32, (8, TOK), 0)
    route = jnp.where(
        line == 0,
        route_first / notes[2:3, :],
        jnp.where(line == 1, route_second / notes[3:4, :], 0.0),
    )
    route_ref[...] = route.astype(BF)
    pick = seat.astype(BF)
    for n in range(4):
        cols = pl.ds(n * 512, 512)
        branch = mm(pick, back_ref[:, cols], ((0,), (0,))).astype(BF).astype(F32)
        sect_ref[:, cols] = (g_ref[:, cols].astype(F32) + branch).astype(BF)


def join_rows(notes, back, g):
    return pl.pallas_call(
        join_kernel,
        out_shape=[jax.ShapeDtypeStruct((TOK, D), BF), jax.ShapeDtypeStruct((8, TOK), BF)],
        compiler_params=vmem(16),
        cost_estimate=pl.CostEstimate(
            flops=2 * SLOTS * BACK * TOK * D, bytes_accessed=3 * MIB, transcendentals=0
        ),
    )(notes, back, g)


def merge_kernel(kinds, info, got_ref, out0, out1, out2, out3, sums):
    for j, out in enumerate((out0, out1, out2, out3)):
        quarter = lax.bitwise_xor(info[EXPERTS], j)
        for kind in range(kinds):
            rows = pl.ds(pl.multiple_of(kind * PART + quarter * 32, 32), 32)
            for e in range(EXPERTS):
                sums[e] = got_ref[e, rows, :].astype(F32)
            for r in range(EXPERTS):
                e = info[r]
                sums[e] = sums[e] + got_ref[EXPERTS + r, rows, :].astype(F32)
            out[kind] = (sums[...] * SCALE).astype(BF)


def merge_slots(info, got):
    kinds = got.shape[1] // PART
    out = jax.ShapeDtypeStruct((kinds, EXPERTS, 32, PART), BF)
    return pl.pallas_call(
        functools.partial(merge_kernel, kinds),
        out_shape=[out] * 4,
        in_specs=[pl.BlockSpec(memory_space=pltpu.SMEM), pl.BlockSpec(memory_space=pltpu.VMEM)],
        scratch_shapes=[pltpu.VMEM((EXPERTS, 32, PART), F32)],
        compiler_params=vmem(16),
        cost_estimate=pl.CostEstimate(
            flops=SLOTS * kinds * PART * PART, bytes_accessed=kinds * MIB, transcendentals=0
        ),
    )(info, got)


def owners(parts):
    return tuple(move(part, OWNER[j]) for j, part in enumerate(parts))


def final_kernel(info, *refs):
    downs, pairs, (gate, up, down) = refs[0:4], refs[4:8], refs[8:11]
    for j in range(4):
        lanes = pl.ds(pl.multiple_of(lax.bitwise_xor(info[0], j) * PART, PART), PART)
        down[0, :, :, lanes] = downs[j][0]
        gate[0, :, :, lanes] = pairs[j][0]
        up[0, :, :, lanes] = pairs[j][1]


def finals(info, downs, pairs):
    whole = pl.BlockSpec(memory_space=pltpu.VMEM)
    out = jax.ShapeDtypeStruct((1, EXPERTS, 32, FF), BF)
    return pl.pallas_call(
        final_kernel,
        out_shape=[out] * 3,
        in_specs=[pl.BlockSpec(memory_space=pltpu.SMEM)] + [whole] * 8,
        compiler_params=vmem(16),
        cost_estimate=pl.CostEstimate(flops=0, bytes_accessed=2 * MIB, transcendentals=0),
    )(info, *downs, *pairs)


def add_kernel(*refs):
    total = refs[0][0].astype(F32) + refs[1][0].astype(F32)
    for ref in refs[2:-1]:
        total = total + ref[...].astype(F32)
    refs[-1][...] = total.astype(BF)


def add(which, pairs, *more):
    shape = pairs[0].shape[1:]
    block = (4,) + shape[1:]
    pair = pl.BlockSpec((1,) + block, lambda n: (which, n, 0, 0))
    one = pl.BlockSpec(block, lambda n: (n, 0, 0))
    return pl.pallas_call(
        add_kernel,
        out_shape=jax.ShapeDtypeStruct(shape, BF),
        grid=(4,),
        in_specs=[pair, pair] + [one] * len(more),
        out_specs=one,
        compiler_params=vmem(16),
        cost_estimate=pl.CostEstimate(flops=0, bytes_accessed=1024, transcendentals=0),
    )(*pairs, *more)


def shards(tokens_in, grad_out, route_weight, slot_of, replica_of, w_gate, w_up, w_down):
    pipe, dp = lax.axis_index("pipe"), lax.axis_index("dp")
    core, side, near = pipe % 2, dp // 2, dp % 2
    mine = core == side
    quarter = (2 * core + near).astype(jnp.int32)

    weights = (w_gate, w_up, w_down)
    asked = (2 * (1 - core) + near) * PART
    others = [lax.dynamic_slice_in_dim(w[0], asked, PART, 2) for w in weights]
    others, tokens, grads = lax.optimization_barrier((others, tokens_in[0], grad_out[0]))
    others = [move(w, CORES) for w in others]
    replicas = jnp.where(mine, replica_of[0], move(replica_of[0], CORES))

    notes = jnp.concatenate(
        [slot_of[0].T.astype(BF), route_weight[0].T, jnp.zeros((4, TOK), BF)], axis=0
    )
    notes = move(notes, TURN)
    x = move(tokens, TURN)
    g = move(grads, TURN)
    info = jnp.concatenate(
        [
            jnp.arange(EXPERTS, dtype=jnp.int32),
            replicas,
            jnp.stack([quarter, mine.astype(jnp.int32)]),
        ]
    )
    first = spread(pick_weights(info, weights, others))
    rows = pack_rows(notes, x, g)
    first, rows = lax.optimization_barrier((first, rows))
    second = move(first, NEAR)
    third, fourth = move(first, CORES), move(second, CORES)

    rows = spread(rows.reshape(SLOTS, 2 * CAP, D)).reshape(2 * ROWS, D)
    back, xs, scaled, hidden, grads = expert_rows(rows, (first, second, third, fourth))
    back = spread(back.reshape(SLOTS, BACK, D)).reshape(SLOTS * BACK, D)
    down = weight_sums(scaled, hidden)
    xs, down = lax.optimization_barrier((xs, down))
    pair = weight_sums(xs, grads)
    down = (down[0], move(down[1], CORES))
    pair = (pair[0], move(pair[1], CORES))
    got, pair = lax.optimization_barrier((move(add(1, down), NEAR), pair))
    down = add(0, down, got)
    pair = add(0, pair, move(add(1, pair), NEAR))

    sect, route = join_rows(notes, back, g)
    sect, down = lax.optimization_barrier((sect, down))
    grad_in = move(sect, BEHIND)
    route = move(route, TURN)[0:2].T

    info = jnp.concatenate([replicas, quarter[None]])
    downs = owners(merge_slots(info, spread(down)))
    pair, grad_in = lax.optimization_barrier((pair, grad_in))
    pairs = owners(merge_slots(info, spread(pair)))
    gate, up, down = finals(dp[None].astype(jnp.int32), downs, pairs)
    return (grad_in[None], route[None], gate, up, down)


def solution(mesh):
    return jax.shard_map(
        shards,
        mesh=mesh,
        in_specs=(
            P("pipe", ("expert", "dp"), None),
            P("pipe", ("expert", "dp"), None),
            P("pipe", ("expert", "dp"), None),
            P("pipe", ("expert", "dp"), None),
            P("pipe", None),
            P("pipe", None, "expert", None),
            P("pipe", None, "expert", None),
            P("pipe", None, "expert", None),
        ),
        out_specs=(
            P("pipe", ("expert", "dp"), None),
            P("pipe", ("expert", "dp"), None),
            P("pipe", None, ("expert", "dp"), None),
            P("pipe", None, ("expert", "dp"), None),
            P("pipe", None, ("expert", "dp"), None),
        ),
        check_vma=False,
    )
```

```python
import functools

import jax
import jax.numpy as jnp
from jax import lax
from jax.experimental import pallas as pl
from jax.experimental.pallas import tpu as pltpu
from jax.sharding import PartitionSpec as P

EXPERTS = 8
CAP = 20
SLOTS = 16
ROWS = SLOTS * CAP
BACK = 24
TOK = 128
D = 2048
FF = 512
PART = 128
BF = jnp.bfloat16
F32 = jnp.float32
MIB = 1 << 20
SCALE = 8192.0**-0.5


def place(zh, c, k, b):
    return (2 * zh + c) * 4 + 2 * k + b


SPOTS = [(zh, c, k, b) for zh in range(2) for c in range(2) for k in range(2) for b in range(2)]
TURN = [(place(zh, c, k, b), place(zh, k, c, b)) for zh, c, k, b in SPOTS]
CORES = [(place(zh, c, k, b), place(zh, 1 - c, k, b)) for zh, c, k, b in SPOTS]
NEAR = [(place(zh, c, k, b), place(zh, c, k, 1 - b)) for zh, c, k, b in SPOTS]
OWNER = [
    [(place(zh, c, k, b), (2 * zh + k) * 4 + ((2 * c + b) ^ j)) for zh, c, k, b in SPOTS]
    for j in range(4)
]
BEHIND = [(place(zh, c, k, b), ((2 * zh + k - 1) % 4) * 4 + 2 * c + b) for zh, c, k, b in SPOTS]


def move(x, pairs):
    return lax.ppermute(x, ("pipe", "dp"), pairs)


def spread(x):
    return lax.all_to_all(x, "expert", split_axis=0, concat_axis=0, tiled=True)


def mm(a, b, dims=((1,), (0,))):
    return lax.dot_general(a, b, (dims, ((), ())), preferred_element_type=F32)


def count(shape, dim):
    return lax.broadcasted_iota(jnp.int32, shape, dim).astype(F32)


def split_by(index, size):
    block = jnp.floor((index + 0.5) * (1.0 / size))
    return block, index - block * size


def vmem(limit, **kw):
    return pltpu.CompilerParams(vmem_limit_bytes=limit * MIB, **kw)


def pick_kernel(info, gate, up, down, other, out, held, sem_in, sem_out):
    lanes = pl.ds(pl.multiple_of(info[SLOTS] * PART, PART), PART)

    def fetch(refs):
        copies = [
            pltpu.make_async_copy(ref, held.at[n], sem_in.at[n]) for n, ref in enumerate(refs)
        ]
        for copy in copies:
            copy.start()
        for copy in copies:
            copy.wait()

    @pl.when(info[SLOTS + 1] == 1)
    def _():
        fetch([ref.at[0, :, :, lanes] for ref in (gate, up, down)])

    @pl.when(info[SLOTS + 1] == 0)
    def _():
        fetch([other.at[pl.ds(n * EXPERTS, EXPERTS)] for n in range(3)])

    copies = [
        pltpu.make_async_copy(
            held.at[n, info[slot]],
            out.at[slot, pl.ds(n * PART, PART), :],
            sem_out.at[slot * 3 + n],
        )
        for slot in range(SLOTS)
        for n in range(3)
    ]
    for copy in copies:
        copy.start()
    for copy in copies:
        copy.wait()


def pick_weights(info, mine, other):
    hbm = pl.BlockSpec(memory_space=pltpu.HBM)
    anywhere = pl.BlockSpec(memory_space=pl.ANY)
    return pl.pallas_call(
        pick_kernel,
        out_shape=jax.ShapeDtypeStruct((SLOTS, 3 * PART, PART), BF),
        in_specs=[pl.BlockSpec(memory_space=pltpu.SMEM)] + [hbm] * 3 + [anywhere],
        out_specs=anywhere,
        scratch_shapes=[
            pltpu.VMEM((3, EXPERTS, PART, PART), BF),
            pltpu.SemaphoreType.DMA((3,)),
            pltpu.SemaphoreType.DMA((3 * SLOTS,)),
        ],
        compiler_params=vmem(60),
        cost_estimate=pl.CostEstimate(flops=0, bytes_accessed=4 * MIB, transcendentals=0),
    )(info, *mine, other)


def seats(notes, size, caps):
    rows = SLOTS * size
    slot, at = split_by(count((rows, 1), 0), size)
    second, rank = split_by(at, caps)
    first = notes[0:1, :] == slot
    other = notes[1:2, :] == slot
    held = jnp.where(first | other, 1.0, 0.0)
    before = jnp.where(count((TOK, TOK), 0) < count((TOK, TOK), 1), 1.0, 0.0)
    taken = mm(held.astype(BF), before.astype(BF))
    seat = jnp.where(taken == rank, held, 0.0)
    return seat, first, second


def pack_kernel(notes_ref, x_ref, g_ref, out_ref):
    notes = notes_ref[...].astype(F32)
    seat, first, second = seats(notes, 2 * CAP, CAP)
    weight = jnp.where(first, notes[2:3, :], notes[3:4, :])
    pick_x = jnp.where(second == 0.0, seat, 0.0).astype(BF)
    pick_g = jnp.where(second == 1.0, seat * weight, 0.0).astype(BF)
    for n in range(4):
        at = pl.ds(n * 512, 512)
        out_ref[:, at] = (mm(pick_x, x_ref[:, at]) + mm(pick_g, g_ref[:, at])).astype(BF)


def pack_rows(notes, x, g):
    return pl.pallas_call(
        pack_kernel,
        out_shape=jax.ShapeDtypeStruct((2 * ROWS, D), BF),
        compiler_params=vmem(16),
        cost_estimate=pl.CostEstimate(
            flops=200 * ROWS * TOK * D, bytes_accessed=128 * MIB, transcendentals=0
        ),
    )(notes, x, g)


def expert_kernel(
    rows_ref,
    w0,
    w1,
    w2,
    w3,
    back_ref,
    x_ref,
    s_ref,
    hid_ref,
    gu_ref,
    sg,
    su,
    sd,
    sem,
):
    copies = [
        pltpu.make_async_copy(
            ref.at[:, pl.ds(n * PART, PART), :],
            stack.at[:, :, pl.ds(side * PART, PART)],
            sem.at[4 * n + side],
        )
        for n, stack in enumerate((sg, su, sd))
        for side, ref in enumerate((w0, w1, w2, w3))
    ]
    for copy in copies:
        copy.start()
    wg, wu, wd = sg.reshape(D, FF), su.reshape(D, FF), sd.reshape(D, FF)
    source = count((1, 2 * ROWS), 1)
    block, at = split_by(count((ROWS, 1), 0), CAP)
    take_x = jnp.where(source == block * (2 * CAP) + at, 1.0, 0.0).astype(BF)
    take_s = jnp.where(source == block * (2 * CAP) + CAP + at, 1.0, 0.0).astype(BF)
    for n in range(4):
        cols = pl.ds(n * 512, 512)
        x_ref[:, cols] = mm(take_x, rows_ref[:, cols]).astype(BF)
        s_ref[:, cols] = mm(take_s, rows_ref[:, cols]).astype(BF)
    for copy in copies:
        copy.wait()
    gate_pre = mm(x_ref[...], wg[...])
    up_pre = mm(x_ref[...], wu[...])
    hidden_grad = mm(s_ref[...], wd[...])
    sigma = jax.nn.sigmoid(gate_pre)
    active = gate_pre * sigma
    hidden = (active * up_pre).astype(BF)
    gate_grad = (hidden_grad * up_pre * sigma * (1.0 + gate_pre * (1.0 - sigma))).astype(BF)
    up_grad = (hidden_grad * active).astype(BF)
    prob = jnp.sum(hidden.astype(F32) * hidden_grad, axis=1, keepdims=True)
    hid_ref[...] = hidden
    gu_ref[:, 0:FF] = gate_grad
    gu_ref[:, FF : 2 * FF] = up_grad
    row = count((1, ROWS), 1)
    row_block, _ = split_by(row, CAP)
    to_block, to_at = split_by(count((SLOTS * BACK, 1), 0), BACK)
    lay = jnp.where((to_at < CAP) & (row == to_block * CAP + to_at), 1.0, 0.0).astype(BF)
    lay_prob = jnp.where((to_at == CAP) & (row_block == to_block), 1.0, 0.0).astype(BF)
    prob_wide = jnp.where(count((1, PART), 1) == at, prob, 0.0).astype(BF)
    prob_rows = mm(lay_prob, prob_wide)
    dims = ((1,), (1,))
    for n in range(8):
        cols = pl.ds(n * 256, 256)
        grad = mm(gate_grad, wg[cols, :], dims) + mm(up_grad, wu[cols, :], dims)
        laid = mm(lay, grad.astype(BF))
        if n == 0:
            back_ref[:, 0:PART] = (laid[:, 0:PART] + prob_rows).astype(BF)
            back_ref[:, PART:256] = laid[:, PART:256].astype(BF)
        else:
            back_ref[:, cols] = laid.astype(BF)


def expert_rows(rows, quarters):
    whole = pl.BlockSpec(memory_space=pltpu.VMEM)
    anywhere = pl.BlockSpec(memory_space=pl.ANY)
    return pl.pallas_call(
        expert_kernel,
        out_shape=[
            jax.ShapeDtypeStruct((SLOTS * BACK, D), BF),
            jax.ShapeDtypeStruct((ROWS, D), BF),
            jax.ShapeDtypeStruct((ROWS, D), BF),
            jax.ShapeDtypeStruct((ROWS, FF), BF),
            jax.ShapeDtypeStruct((ROWS, 2 * FF), BF),
        ],
        in_specs=[whole] + [anywhere] * 4,
        out_specs=[whole] * 5,
        scratch_shapes=[
            pltpu.VMEM((SLOTS, PART, FF), BF),
            pltpu.VMEM((SLOTS, PART, FF), BF),
            pltpu.VMEM((SLOTS, PART, FF), BF),
            pltpu.SemaphoreType.DMA((12,)),
        ],
        compiler_params=vmem(32),
        cost_estimate=pl.CostEstimate(
            flops=16 * ROWS * D * FF, bytes_accessed=14 * MIB, transcendentals=ROWS * FF
        ),
    )(rows, *quarters)


def sums_kernel(kinds, a_ref, b_ref, own_ref, oth_ref):
    for n in range(8):
        part = mm(a_ref[:, pl.ds(n * 256, 256)], b_ref[...], ((0,), (0,))).astype(BF)
        for piece in range(2):
            rows = slice(piece * PART, (piece + 1) * PART)
            for kind in range(kinds):
                for q in range(4):
                    lanes = slice(kind * FF + q * PART, kind * FF + (q + 1) * PART)
                    ref = own_ref if q < 2 else oth_ref
                    ref[q % 2, 2 * n + piece, kind * PART : (kind + 1) * PART, :] = part[rows, lanes]


def weight_sums(a, b, flops):
    kinds = b.shape[1] // FF
    shape = jax.ShapeDtypeStruct((2, SLOTS, kinds * PART, PART), BF)
    return pl.pallas_call(
        functools.partial(sums_kernel, kinds),
        out_shape=[shape, shape],
        compiler_params=vmem(24),
        cost_estimate=pl.CostEstimate(
            flops=flops, bytes_accessed=1024, transcendentals=0
        ),
    )(a, b)


def join_kernel(notes_ref, back_ref, g_ref, sect_ref, route_ref):
    notes = notes_ref[...].astype(F32)
    rows = SLOTS * BACK
    seat, first, second = seats(notes, BACK, CAP)
    seat = jnp.where(second == 0.0, seat, 0.0)
    slot, at = split_by(count((rows, 1), 0), BACK)
    to_prob = jnp.where(count((1, rows), 1) == slot * BACK + CAP, 1.0, 0.0).astype(BF)
    probs = mm(to_prob, back_ref[:, 0:PART])
    prob = jnp.sum(jnp.where(count((1, PART), 1) == at, probs, 0.0), axis=1, keepdims=True)
    share = seat * prob
    route_first = jnp.sum(jnp.where(first, share, 0.0), axis=0, keepdims=True)
    route_second = jnp.sum(jnp.where(first, 0.0, share), axis=0, keepdims=True)
    line = lax.broadcasted_iota(jnp.int32, (8, TOK), 0)
    route = jnp.where(
        line == 0,
        route_first / notes[2:3, :],
        jnp.where(line == 1, route_second / notes[3:4, :], 0.0),
    )
    route_ref[...] = route.astype(BF)
    pick = seat.astype(BF)
    for n in range(4):
        cols = pl.ds(n * 512, 512)
        branch = mm(pick, back_ref[:, cols], ((0,), (0,))).astype(BF).astype(F32)
        sect_ref[:, cols] = (g_ref[:, cols].astype(F32) + branch).astype(BF)


def join_rows(notes, back, g):
    return pl.pallas_call(
        join_kernel,
        out_shape=[jax.ShapeDtypeStruct((TOK, D), BF), jax.ShapeDtypeStruct((8, TOK), BF)],
        compiler_params=vmem(16),
        cost_estimate=pl.CostEstimate(
            flops=2 * SLOTS * BACK * TOK * D, bytes_accessed=3 * MIB, transcendentals=0
        ),
    )(notes, back, g)


def merge_kernel(kinds, info, got_ref, out0, out1, out2, out3, sums):
    for j, out in enumerate((out0, out1, out2, out3)):
        quarter = lax.bitwise_xor(info[EXPERTS], j)
        for kind in range(kinds):
            rows = pl.ds(pl.multiple_of(kind * PART + quarter * 32, 32), 32)
            for e in range(EXPERTS):
                sums[e] = got_ref[e, rows, :].astype(F32)
            for r in range(EXPERTS):
                e = info[r]
                sums[e] = sums[e] + got_ref[EXPERTS + r, rows, :].astype(F32)
            out[kind] = (sums[...] * SCALE).astype(BF)


def merge_slots(info, got, flops):
    kinds = got.shape[1] // PART
    out = jax.ShapeDtypeStruct((kinds, EXPERTS, 32, PART), BF)
    return pl.pallas_call(
        functools.partial(merge_kernel, kinds),
        out_shape=[out] * 4,
        in_specs=[pl.BlockSpec(memory_space=pltpu.SMEM), pl.BlockSpec(memory_space=pltpu.VMEM)],
        scratch_shapes=[pltpu.VMEM((EXPERTS, 32, PART), F32)],
        compiler_params=vmem(16),
        cost_estimate=pl.CostEstimate(
            flops=flops, bytes_accessed=kinds * MIB, transcendentals=0
        ),
    )(info, got)


def owners(parts):
    return tuple(move(part, OWNER[j]) for j, part in enumerate(parts))


def final_kernel(info, *refs):
    downs, pairs, (gate, up, down) = refs[0:4], refs[4:8], refs[8:11]
    for j in range(4):
        lanes = pl.ds(pl.multiple_of(lax.bitwise_xor(info[0], j) * PART, PART), PART)
        down[0, :, :, lanes] = downs[j][0]
        gate[0, :, :, lanes] = pairs[j][0]
        up[0, :, :, lanes] = pairs[j][1]


def finals(info, downs, pairs):
    whole = pl.BlockSpec(memory_space=pltpu.VMEM)
    out = jax.ShapeDtypeStruct((1, EXPERTS, 32, FF), BF)
    return pl.pallas_call(
        final_kernel,
        out_shape=[out] * 3,
        in_specs=[pl.BlockSpec(memory_space=pltpu.SMEM)] + [whole] * 8,
        compiler_params=vmem(16),
        cost_estimate=pl.CostEstimate(flops=0, bytes_accessed=2 * MIB, transcendentals=0),
    )(info, *downs, *pairs)


def add_kernel(*refs):
    total = refs[0][0].astype(F32) + refs[1][0].astype(F32)
    for ref in refs[2:-1]:
        total = total + ref[...].astype(F32)
    refs[-1][...] = total.astype(BF)


def add(which, pairs, *more):
    shape = pairs[0].shape[1:]
    block = (4,) + shape[1:]
    pair = pl.BlockSpec((1,) + block, lambda n: (which, n, 0, 0))
    one = pl.BlockSpec(block, lambda n: (n, 0, 0))
    return pl.pallas_call(
        add_kernel,
        out_shape=jax.ShapeDtypeStruct(shape, BF),
        grid=(4,),
        in_specs=[pair, pair] + [one] * len(more),
        out_specs=one,
        compiler_params=vmem(16),
        cost_estimate=pl.CostEstimate(flops=0, bytes_accessed=1024, transcendentals=0),
    )(*pairs, *more)


def shards(tokens_in, grad_out, route_weight, slot_of, replica_of, w_gate, w_up, w_down):
    pipe, dp = lax.axis_index("pipe"), lax.axis_index("dp")
    core, side, near = pipe % 2, dp // 2, dp % 2
    mine = core == side
    quarter = (2 * core + near).astype(jnp.int32)

    weights = (w_gate, w_up, w_down)
    asked = (2 * (1 - core) + near) * PART
    other = jnp.concatenate([lax.dynamic_slice_in_dim(w[0], asked, PART, 2) for w in weights])
    other, tokens, grads = lax.optimization_barrier((other, tokens_in[0], grad_out[0]))
    other = move(other, CORES)
    replicas = jnp.where(mine, replica_of[0], move(replica_of[0], CORES))

    notes = jnp.concatenate(
        [slot_of[0].T.astype(BF), route_weight[0].T, jnp.zeros((4, TOK), BF)], axis=0
    )
    notes = move(notes, TURN)
    x = move(tokens, TURN)
    g = move(grads, TURN)
    info = jnp.concatenate(
        [
            jnp.arange(EXPERTS, dtype=jnp.int32),
            replicas,
            jnp.stack([quarter, mine.astype(jnp.int32)]),
        ]
    )
    first = spread(pick_weights(info, weights, other))
    rows = pack_rows(notes, x, g)
    first, rows = lax.optimization_barrier((first, rows))
    second = move(first, NEAR)
    third, fourth = move(first, CORES), move(second, CORES)

    rows = spread(rows.reshape(SLOTS, 2 * CAP, D)).reshape(2 * ROWS, D)
    back, xs, scaled, hidden, grads = expert_rows(rows, (first, second, third, fourth))
    down = weight_sums(scaled, hidden, 0)
    xs, down, back = lax.optimization_barrier((xs, down, back))
    back = spread(back.reshape(SLOTS, BACK, D)).reshape(SLOTS * BACK, D)
    pair = weight_sums(xs, grads, 10**10)
    down = (down[0], move(down[1], CORES))
    sent, pair = lax.optimization_barrier((add(1, down), pair))
    got, _ = lax.optimization_barrier((move(sent, NEAR), pair))
    down = add(0, down, got)
    pair = (pair[0], move(pair[1], CORES))
    got, sent = lax.optimization_barrier((got, add(1, pair)))
    sent = move(sent, NEAR)

    sect, route = join_rows(notes, back, g)
    route = move(route, TURN)[0:2].T
    pair = add(0, pair, sent)
    sect, down = lax.optimization_barrier((sect, spread(down)))
    grad_in = move(sect, BEHIND)

    info = jnp.concatenate([replicas, quarter[None]])
    downs = owners(merge_slots(info, down, 10**11))
    pair, _ = lax.optimization_barrier((spread(pair), grad_in))
    pairs = owners(merge_slots(info, pair, 0))
    gate, up, down = finals(dp[None].astype(jnp.int32), downs, pairs)
    return (grad_in[None], route[None], gate, up, down)


def solution(mesh):
    return jax.shard_map(
        shards,
        mesh=mesh,
        in_specs=(
            P("pipe", ("expert", "dp"), None),
            P("pipe", ("expert", "dp"), None),
            P("pipe", ("expert", "dp"), None),
            P("pipe", ("expert", "dp"), None),
            P("pipe", None),
            P("pipe", None, "expert", None),
            P("pipe", None, "expert", None),
            P("pipe", None, "expert", None),
        ),
        out_specs=(
            P("pipe", ("expert", "dp"), None),
            P("pipe", ("expert", "dp"), None),
            P("pipe", None, ("expert", "dp"), None),
            P("pipe", None, ("expert", "dp"), None),
            P("pipe", None, ("expert", "dp"), None),
        ),
        check_vma=False,
    )
```

```python
import functools

import jax
import jax.numpy as jnp
from jax import lax
from jax.experimental import pallas as pl
from jax.experimental.pallas import tpu as pltpu
from jax.sharding import PartitionSpec as P

EXPERTS = 8
CAP = 20
SLOTS = 16
ROWS = SLOTS * CAP
BACK = 24
TOK = 128
D = 2048
FF = 512
PART = 128
OWN = 32
BF = jnp.bfloat16
F32 = jnp.float32
MIB = 1 << 20
SCALE = 8192.0**-0.5


def place(zh, c, k, b):
    return (2 * zh + c) * 4 + 2 * k + b


SPOTS = [(zh, c, k, b) for zh in range(2) for c in range(2) for k in range(2) for b in range(2)]
TURN = [(place(zh, c, k, b), place(zh, k, c, b)) for zh, c, k, b in SPOTS]
CORES = [(place(zh, c, k, b), place(zh, 1 - c, k, b)) for zh, c, k, b in SPOTS]
NEAR = [(place(zh, c, k, b), place(zh, c, k, 1 - b)) for zh, c, k, b in SPOTS]
BEHIND = [(place(zh, c, k, b), ((2 * zh + k - 1) % 4) * 4 + 2 * c + b) for zh, c, k, b in SPOTS]


def move(x, pairs):
    return lax.ppermute(x, ("pipe", "dp"), pairs)


def spread(x):
    return lax.all_to_all(x, "expert", split_axis=0, concat_axis=0, tiled=True)


def mm(a, b, dims=((1,), (0,))):
    return lax.dot_general(a, b, (dims, ((), ())), preferred_element_type=F32)


def count(shape, dim):
    return lax.broadcasted_iota(jnp.int32, shape, dim).astype(F32)


def split_by(index, size):
    block = jnp.floor((index + 0.5) * (1.0 / size))
    return block, index - block * size


def vmem(limit, **kw):
    return pltpu.CompilerParams(vmem_limit_bytes=limit * MIB, **kw)


def pick_kernel(info, gate, up, down, other, out, held, sem_in, sem_out):
    lanes = pl.ds(pl.multiple_of(info[SLOTS] * PART, PART), PART)

    def fetch(refs):
        copies = [
            pltpu.make_async_copy(ref, held.at[n], sem_in.at[n]) for n, ref in enumerate(refs)
        ]
        for copy in copies:
            copy.start()
        for copy in copies:
            copy.wait()

    @pl.when(info[SLOTS + 1] == 1)
    def _():
        fetch([ref.at[0, :, :, lanes] for ref in (gate, up, down)])

    @pl.when(info[SLOTS + 1] == 0)
    def _():
        fetch([other.at[pl.ds(n * EXPERTS, EXPERTS)] for n in range(3)])

    copies = [
        pltpu.make_async_copy(
            held.at[n, info[slot]],
            out.at[slot, pl.ds(n * PART, PART), :],
            sem_out.at[slot * 3 + n],
        )
        for slot in range(SLOTS)
        for n in range(3)
    ]
    for copy in copies:
        copy.start()
    for copy in copies:
        copy.wait()


def pick_weights(info, mine, other):
    hbm = pl.BlockSpec(memory_space=pltpu.HBM)
    anywhere = pl.BlockSpec(memory_space=pl.ANY)
    return pl.pallas_call(
        pick_kernel,
        out_shape=jax.ShapeDtypeStruct((SLOTS, 3 * PART, PART), BF),
        in_specs=[pl.BlockSpec(memory_space=pltpu.SMEM)] + [hbm] * 3 + [anywhere],
        out_specs=anywhere,
        scratch_shapes=[
            pltpu.VMEM((3, EXPERTS, PART, PART), BF),
            pltpu.SemaphoreType.DMA((3,)),
            pltpu.SemaphoreType.DMA((3 * SLOTS,)),
        ],
        compiler_params=vmem(60),
        cost_estimate=pl.CostEstimate(flops=0, bytes_accessed=4 * MIB, transcendentals=0),
    )(info, *mine, other)


def seats(notes, size, caps):
    rows = SLOTS * size
    slot, at = split_by(count((rows, 1), 0), size)
    second, rank = split_by(at, caps)
    first = notes[0:1, :] == slot
    other = notes[1:2, :] == slot
    held = jnp.where(first | other, 1.0, 0.0)
    before = jnp.where(count((TOK, TOK), 0) < count((TOK, TOK), 1), 1.0, 0.0)
    taken = mm(held.astype(BF), before.astype(BF))
    seat = jnp.where(taken == rank, held, 0.0)
    return seat, first, second


def pack_kernel(notes_ref, x_ref, g_ref, out_ref):
    notes = notes_ref[...].astype(F32)
    seat, first, second = seats(notes, 2 * CAP, CAP)
    weight = jnp.where(first, notes[2:3, :], notes[3:4, :])
    pick_x = jnp.where(second == 0.0, seat, 0.0).astype(BF)
    pick_g = jnp.where(second == 1.0, seat * weight, 0.0).astype(BF)
    for n in range(4):
        at = pl.ds(n * 512, 512)
        out_ref[:, at] = (mm(pick_x, x_ref[:, at]) + mm(pick_g, g_ref[:, at])).astype(BF)


def pack_rows(notes, x, g):
    return pl.pallas_call(
        pack_kernel,
        out_shape=jax.ShapeDtypeStruct((2 * ROWS, D), BF),
        compiler_params=vmem(16),
        cost_estimate=pl.CostEstimate(
            flops=200 * ROWS * TOK * D, bytes_accessed=128 * MIB, transcendentals=0
        ),
    )(notes, x, g)


def expert_kernel(
    info,
    rows_ref,
    w0,
    w1,
    w2,
    w3,
    back_ref,
    x_ref,
    s_ref,
    hid_ref,
    gu_ref,
    sg,
    su,
    sd,
    sem,
):
    copies = [
        pltpu.make_async_copy(
            ref.at[:, pl.ds(n * PART, PART), :],
            stack.at[:, :, pl.ds(pl.multiple_of((info[0] ^ side) * PART, PART), PART)],
            sem.at[4 * n + side],
        )
        for n, stack in enumerate((sg, su, sd))
        for side, ref in enumerate((w0, w1, w2, w3))
    ]
    for copy in copies:
        copy.start()
    wg, wu, wd = sg.reshape(D, FF), su.reshape(D, FF), sd.reshape(D, FF)
    source = count((1, 2 * ROWS), 1)
    block, at = split_by(count((ROWS, 1), 0), CAP)
    take_x = jnp.where(source == block * (2 * CAP) + at, 1.0, 0.0).astype(BF)
    take_s = jnp.where(source == block * (2 * CAP) + CAP + at, 1.0, 0.0).astype(BF)
    for n in range(4):
        cols = pl.ds(n * 512, 512)
        x_ref[:, cols] = mm(take_x, rows_ref[:, cols]).astype(BF)
        s_ref[:, cols] = mm(take_s, rows_ref[:, cols]).astype(BF)
    for copy in copies:
        copy.wait()
    gate_pre = mm(x_ref[...], wg[...])
    up_pre = mm(x_ref[...], wu[...])
    hidden_grad = mm(s_ref[...], wd[...])
    sigma = jax.nn.sigmoid(gate_pre)
    active = gate_pre * sigma
    hidden = (active * up_pre).astype(BF)
    gate_grad = (hidden_grad * up_pre * sigma * (1.0 + gate_pre * (1.0 - sigma))).astype(BF)
    up_grad = (hidden_grad * active).astype(BF)
    prob = jnp.sum(hidden.astype(F32) * hidden_grad, axis=1, keepdims=True)
    hid_ref[...] = hidden
    gu_ref[:, 0:FF] = gate_grad
    gu_ref[:, FF : 2 * FF] = up_grad
    row = count((1, ROWS), 1)
    row_block, _ = split_by(row, CAP)
    to_block, to_at = split_by(count((SLOTS * BACK, 1), 0), BACK)
    lay = jnp.where((to_at < CAP) & (row == to_block * CAP + to_at), 1.0, 0.0).astype(BF)
    lay_prob = jnp.where((to_at == CAP) & (row_block == to_block), 1.0, 0.0).astype(BF)
    prob_wide = jnp.where(count((1, PART), 1) == at, prob, 0.0).astype(BF)
    prob_rows = mm(lay_prob, prob_wide)
    dims = ((1,), (1,))
    for n in range(8):
        cols = pl.ds(n * 256, 256)
        grad = mm(gate_grad, wg[cols, :], dims) + mm(up_grad, wu[cols, :], dims)
        laid = mm(lay, grad.astype(BF))
        if n == 0:
            back_ref[:, 0:PART] = (laid[:, 0:PART] + prob_rows).astype(BF)
            back_ref[:, PART:256] = laid[:, PART:256].astype(BF)
        else:
            back_ref[:, cols] = laid.astype(BF)


def expert_rows(info, rows, quarters):
    whole = pl.BlockSpec(memory_space=pltpu.VMEM)
    anywhere = pl.BlockSpec(memory_space=pl.ANY)
    return pl.pallas_call(
        expert_kernel,
        out_shape=[
            jax.ShapeDtypeStruct((SLOTS * BACK, D), BF),
            jax.ShapeDtypeStruct((ROWS, D), BF),
            jax.ShapeDtypeStruct((ROWS, D), BF),
            jax.ShapeDtypeStruct((ROWS, FF), BF),
            jax.ShapeDtypeStruct((ROWS, 2 * FF), BF),
        ],
        in_specs=[pl.BlockSpec(memory_space=pltpu.SMEM), whole] + [anywhere] * 4,
        out_specs=[whole] * 5,
        scratch_shapes=[
            pltpu.VMEM((SLOTS, PART, FF), BF),
            pltpu.VMEM((SLOTS, PART, FF), BF),
            pltpu.VMEM((SLOTS, PART, FF), BF),
            pltpu.SemaphoreType.DMA((12,)),
        ],
        compiler_params=vmem(32),
        cost_estimate=pl.CostEstimate(
            flops=16 * ROWS * D * FF, bytes_accessed=14 * MIB, transcendentals=ROWS * FF
        ),
    )(info, rows, *quarters)


def sums_kernel(kinds, info, a_ref, b_ref, own_ref, oth_ref):
    def run(core):
        for n in range(8):
            part = mm(a_ref[:, pl.ds(n * 256, 256)], b_ref[...], ((0,), (0,))).astype(BF)
            for piece in range(2):
                for q in range(4):
                    rows = slice(piece * PART + q * OWN, piece * PART + (q + 1) * OWN)
                    ref = own_ref if q // 2 == core else oth_ref
                    to = (info[0] % 2) ^ (q % 2)
                    for kind in range(kinds):
                        ref[to, 2 * n + piece, kind * OWN : (kind + 1) * OWN, :] = part[
                            rows, kind * FF : (kind + 1) * FF
                        ]

    @pl.when(info[0] // 2 == 0)
    def _():
        run(0)

    @pl.when(info[0] // 2 == 1)
    def _():
        run(1)


def weight_sums(info, a, b, flops):
    kinds = b.shape[1] // FF
    shape = jax.ShapeDtypeStruct((2, SLOTS, kinds * OWN, FF), BF)
    whole = pl.BlockSpec(memory_space=pltpu.VMEM)
    return pl.pallas_call(
        functools.partial(sums_kernel, kinds),
        out_shape=[shape, shape],
        in_specs=[pl.BlockSpec(memory_space=pltpu.SMEM), whole, whole],
        compiler_params=vmem(24),
        cost_estimate=pl.CostEstimate(
            flops=flops, bytes_accessed=1024, transcendentals=0
        ),
    )(info, a, b)


def join_kernel(notes_ref, back_ref, g_ref, sect_ref, route_ref):
    notes = notes_ref[...].astype(F32)
    rows = SLOTS * BACK
    seat, first, second = seats(notes, BACK, CAP)
    seat = jnp.where(second == 0.0, seat, 0.0)
    slot, at = split_by(count((rows, 1), 0), BACK)
    to_prob = jnp.where(count((1, rows), 1) == slot * BACK + CAP, 1.0, 0.0).astype(BF)
    probs = mm(to_prob, back_ref[:, 0:PART])
    prob = jnp.sum(jnp.where(count((1, PART), 1) == at, probs, 0.0), axis=1, keepdims=True)
    share = seat * prob
    route_first = jnp.sum(jnp.where(first, share, 0.0), axis=0, keepdims=True)
    route_second = jnp.sum(jnp.where(first, 0.0, share), axis=0, keepdims=True)
    line = lax.broadcasted_iota(jnp.int32, (8, TOK), 0)
    route = jnp.where(
        line == 0,
        route_first / notes[2:3, :],
        jnp.where(line == 1, route_second / notes[3:4, :], 0.0),
    )
    route_ref[...] = route.astype(BF)
    pick = seat.astype(BF)
    for n in range(4):
        cols = pl.ds(n * 512, 512)
        branch = mm(pick, back_ref[:, cols], ((0,), (0,))).astype(BF).astype(F32)
        sect_ref[:, cols] = (g_ref[:, cols].astype(F32) + branch).astype(BF)


def join_rows(notes, back, g):
    return pl.pallas_call(
        join_kernel,
        out_shape=[jax.ShapeDtypeStruct((TOK, D), BF), jax.ShapeDtypeStruct((8, TOK), BF)],
        compiler_params=vmem(16),
        cost_estimate=pl.CostEstimate(
            flops=2 * SLOTS * BACK * TOK * D, bytes_accessed=3 * MIB, transcendentals=0
        ),
    )(notes, back, g)


def merge_kernel(info, got_ref, *refs):
    outs, sums = refs[:-1], refs[-1]
    for kind, out in enumerate(outs):
        rows = slice(kind * OWN, (kind + 1) * OWN)
        for e in range(EXPERTS):
            sums[e] = got_ref[e, rows, :].astype(F32)
        for r in range(EXPERTS):
            e = info[r]
            sums[e] = sums[e] + got_ref[EXPERTS + r, rows, :].astype(F32)
        out[0] = (sums[...] * SCALE).astype(BF)


def merge_slots(info, got, flops):
    kinds = got.shape[1] // OWN
    return pl.pallas_call(
        merge_kernel,
        out_shape=[jax.ShapeDtypeStruct((1, EXPERTS, OWN, FF), BF)] * kinds,
        in_specs=[pl.BlockSpec(memory_space=pltpu.SMEM), pl.BlockSpec(memory_space=pltpu.VMEM)],
        scratch_shapes=[pltpu.VMEM((EXPERTS, OWN, FF), F32)],
        compiler_params=vmem(16),
        cost_estimate=pl.CostEstimate(
            flops=flops, bytes_accessed=kinds * MIB, transcendentals=0
        ),
    )(info, got)


def add_kernel(*refs):
    total = refs[0][0].astype(F32) + refs[1][0].astype(F32)
    for ref in refs[2:-1]:
        total = total + ref[...].astype(F32)
    refs[-1][...] = total.astype(BF)


def add(which, pairs, *more):
    shape = pairs[0].shape[1:]
    block = (4,) + shape[1:]
    pair = pl.BlockSpec((1,) + block, lambda n: (which, n, 0, 0))
    one = pl.BlockSpec(block, lambda n: (n, 0, 0))
    return pl.pallas_call(
        add_kernel,
        out_shape=jax.ShapeDtypeStruct(shape, BF),
        grid=(4,),
        in_specs=[pair, pair] + [one] * len(more),
        out_specs=one,
        compiler_params=vmem(16),
        cost_estimate=pl.CostEstimate(flops=0, bytes_accessed=1024, transcendentals=0),
    )(*pairs, *more)


def shards(tokens_in, grad_out, route_weight, slot_of, replica_of, w_gate, w_up, w_down):
    pipe, dp = lax.axis_index("pipe"), lax.axis_index("dp")
    core, side, near = pipe % 2, dp // 2, dp % 2
    mine = core == side
    quarter = (2 * core + near).astype(jnp.int32)
    spot = quarter[None]

    weights = (w_gate, w_up, w_down)
    asked = (2 * (1 - core) + near) * PART
    other = jnp.concatenate([lax.dynamic_slice_in_dim(w[0], asked, PART, 2) for w in weights])
    other, tokens = lax.optimization_barrier((other, tokens_in[0]))
    other = move(other, CORES)
    replicas = jnp.where(mine, replica_of[0], move(replica_of[0], CORES))
    x = move(tokens, TURN)

    info = jnp.concatenate(
        [
            jnp.arange(EXPERTS, dtype=jnp.int32),
            replicas,
            jnp.stack([quarter, mine.astype(jnp.int32)]),
        ]
    )
    notes = jnp.concatenate(
        [slot_of[0].T.astype(BF), route_weight[0].T, jnp.zeros((4, TOK), BF)], axis=0
    )
    picked = pick_weights(info, weights, other)
    picked, notes, grads = lax.optimization_barrier((picked, notes, grad_out[0]))
    notes = move(notes, TURN)
    g = move(grads, TURN)
    first = spread(picked)
    rows = pack_rows(notes, x, g)
    first, rows = lax.optimization_barrier((first, rows))
    second = move(first, NEAR)
    third, fourth = move(first, CORES), move(second, CORES)

    rows = spread(rows.reshape(SLOTS, 2 * CAP, D)).reshape(2 * ROWS, D)
    back, xs, scaled, hidden, grads = expert_rows(spot, rows, (first, second, third, fourth))
    down = weight_sums(spot, scaled, hidden, 0)
    xs, down, back = lax.optimization_barrier((xs, down, back))
    back = spread(back.reshape(SLOTS, BACK, D)).reshape(SLOTS * BACK, D)
    pair = weight_sums(spot, xs, grads, 10**10)
    down = (down[0], move(down[1], CORES))
    sent, pair = lax.optimization_barrier((add(1, down), pair))
    got, _ = lax.optimization_barrier((move(sent, NEAR), pair))
    down = add(0, down, got)
    pair = (pair[0], move(pair[1], CORES))
    got, sent = lax.optimization_barrier((got, add(1, pair)))
    sent = move(sent, NEAR)

    sect, route = join_rows(notes, back, g)
    route = move(route, TURN)
    pair = add(0, pair, sent)
    sect, down = lax.optimization_barrier((sect, spread(down)))
    grad_in = move(sect, BEHIND)

    (down,) = merge_slots(replicas, down, 10**11)
    down = move(down, TURN)
    pair, route, _ = lax.optimization_barrier((spread(pair), route, grad_in))
    gate, up = (move(part, TURN) for part in merge_slots(replicas, pair, 0))
    return (grad_in[None], route[0:2].T[None], gate, up, down)


def solution(mesh):
    return jax.shard_map(
        shards,
        mesh=mesh,
        in_specs=(
            P("pipe", ("expert", "dp"), None),
            P("pipe", ("expert", "dp"), None),
            P("pipe", ("expert", "dp"), None),
            P("pipe", ("expert", "dp"), None),
            P("pipe", None),
            P("pipe", None, "expert", None),
            P("pipe", None, "expert", None),
            P("pipe", None, "expert", None),
        ),
        out_specs=(
            P("pipe", ("expert", "dp"), None),
            P("pipe", ("expert", "dp"), None),
            P("pipe", None, ("expert", "dp"), None),
            P("pipe", None, ("expert", "dp"), None),
            P("pipe", None, ("expert", "dp"), None),
        ),
        check_vma=False,
    )
```

```python
import functools

import jax
import jax.numpy as jnp
from jax import lax
from jax.experimental import pallas as pl
from jax.experimental.pallas import tpu as pltpu
from jax.sharding import PartitionSpec as P

EXPERTS = 8
CAP = 20
SLOTS = 16
ROWS = SLOTS * CAP
BACK = 24
TOK = 128
D = 2048
FF = 512
PART = 128
OWN = 32
BF = jnp.bfloat16
F32 = jnp.float32
MIB = 1 << 20
SCALE = 8192.0**-0.5


def place(zh, c, k, b):
    return (2 * zh + c) * 4 + 2 * k + b


SPOTS = [(zh, c, k, b) for zh in range(2) for c in range(2) for k in range(2) for b in range(2)]
TURN = [(place(zh, c, k, b), place(zh, k, c, b)) for zh, c, k, b in SPOTS]
CORES = [(place(zh, c, k, b), place(zh, 1 - c, k, b)) for zh, c, k, b in SPOTS]
NEAR = [(place(zh, c, k, b), place(zh, c, k, 1 - b)) for zh, c, k, b in SPOTS]
BEHIND = [(place(zh, c, k, b), ((2 * zh + k - 1) % 4) * 4 + 2 * c + b) for zh, c, k, b in SPOTS]


def move(x, pairs):
    return lax.ppermute(x, ("pipe", "dp"), pairs)


def spread(x):
    return lax.all_to_all(x, "expert", split_axis=0, concat_axis=0, tiled=True)


def mm(a, b, dims=((1,), (0,))):
    return lax.dot_general(a, b, (dims, ((), ())), preferred_element_type=F32)


def count(shape, dim):
    return lax.broadcasted_iota(jnp.int32, shape, dim).astype(F32)


def split_by(index, size):
    block = jnp.floor((index + 0.5) * (1.0 / size))
    return block, index - block * size


def vmem(limit, **kw):
    return pltpu.CompilerParams(vmem_limit_bytes=limit * MIB, **kw)


def pick_kernel(info, gate, up, down, other, out, held, sem_in, sem_out):
    lanes = pl.ds(pl.multiple_of(info[SLOTS] * PART, PART), PART)

    def fetch(refs):
        copies = [
            pltpu.make_async_copy(ref, held.at[n], sem_in.at[n]) for n, ref in enumerate(refs)
        ]
        for copy in copies:
            copy.start()
        for copy in copies:
            copy.wait()

    @pl.when(info[SLOTS + 1] == 1)
    def _():
        fetch([ref.at[0, :, :, lanes] for ref in (gate, up, down)])

    @pl.when(info[SLOTS + 1] == 0)
    def _():
        fetch([other.at[pl.ds(n * EXPERTS, EXPERTS)] for n in range(3)])

    copies = [
        pltpu.make_async_copy(
            held.at[n, info[slot]],
            out.at[slot, pl.ds(n * PART, PART), :],
            sem_out.at[slot * 3 + n],
        )
        for slot in range(SLOTS)
        for n in range(3)
    ]
    for copy in copies:
        copy.start()
    for copy in copies:
        copy.wait()


def pick_weights(info, mine, other):
    hbm = pl.BlockSpec(memory_space=pltpu.HBM)
    anywhere = pl.BlockSpec(memory_space=pl.ANY)
    return pl.pallas_call(
        pick_kernel,
        out_shape=jax.ShapeDtypeStruct((SLOTS, 3 * PART, PART), BF),
        in_specs=[pl.BlockSpec(memory_space=pltpu.SMEM)] + [hbm] * 3 + [anywhere],
        out_specs=anywhere,
        scratch_shapes=[
            pltpu.VMEM((3, EXPERTS, PART, PART), BF),
            pltpu.SemaphoreType.DMA((3,)),
            pltpu.SemaphoreType.DMA((3 * SLOTS,)),
        ],
        compiler_params=vmem(60),
        cost_estimate=pl.CostEstimate(flops=0, bytes_accessed=4 * MIB, transcendentals=0),
    )(info, *mine, other)


def seats(notes, size, caps):
    rows = SLOTS * size
    slot, at = split_by(count((rows, 1), 0), size)
    second, rank = split_by(at, caps)
    first = notes[0:1, :] == slot
    other = notes[1:2, :] == slot
    held = jnp.where(first | other, 1.0, 0.0)
    before = jnp.where(count((TOK, TOK), 0) < count((TOK, TOK), 1), 1.0, 0.0)
    taken = mm(held.astype(BF), before.astype(BF))
    seat = jnp.where(taken == rank, held, 0.0)
    return seat, first, second


def pack_kernel(notes_ref, x_ref, g_ref, out_ref):
    notes = notes_ref[...].astype(F32)
    seat, first, second = seats(notes, 2 * CAP, CAP)
    weight = jnp.where(first, notes[2:3, :], notes[3:4, :])
    pick_x = jnp.where(second == 0.0, seat, 0.0).astype(BF)
    pick_g = jnp.where(second == 1.0, seat * weight, 0.0).astype(BF)
    for n in range(4):
        at = pl.ds(n * 512, 512)
        out_ref[:, at] = (mm(pick_x, x_ref[:, at]) + mm(pick_g, g_ref[:, at])).astype(BF)


def pack_rows(notes, x, g):
    return pl.pallas_call(
        pack_kernel,
        out_shape=jax.ShapeDtypeStruct((2 * ROWS, D), BF),
        compiler_params=vmem(16),
        cost_estimate=pl.CostEstimate(
            flops=200 * ROWS * TOK * D, bytes_accessed=128 * MIB, transcendentals=0
        ),
    )(notes, x, g)


def expert_kernel(
    info,
    rows_ref,
    w0,
    w1,
    w2,
    w3,
    back_ref,
    x_ref,
    s_ref,
    hid_ref,
    gu_ref,
    sg,
    su,
    sd,
    sem,
):
    copies = [
        pltpu.make_async_copy(
            ref.at[:, pl.ds(n * PART, PART), :],
            stack.at[:, :, pl.ds(pl.multiple_of((info[0] ^ side) * PART, PART), PART)],
            sem.at[4 * n + side],
        )
        for n, stack in enumerate((sg, su, sd))
        for side, ref in enumerate((w0, w1, w2, w3))
    ]
    for copy in copies:
        copy.start()
    wg, wu, wd = sg.reshape(D, FF), su.reshape(D, FF), sd.reshape(D, FF)
    source = count((1, 2 * ROWS), 1)
    block, at = split_by(count((ROWS, 1), 0), CAP)
    take_x = jnp.where(source == block * (2 * CAP) + at, 1.0, 0.0).astype(BF)
    take_s = jnp.where(source == block * (2 * CAP) + CAP + at, 1.0, 0.0).astype(BF)
    for n in range(4):
        cols = pl.ds(n * 512, 512)
        x_ref[:, cols] = mm(take_x, rows_ref[:, cols]).astype(BF)
        s_ref[:, cols] = mm(take_s, rows_ref[:, cols]).astype(BF)
    for copy in copies:
        copy.wait()
    gate_pre = mm(x_ref[...], wg[...])
    up_pre = mm(x_ref[...], wu[...])
    hidden_grad = mm(s_ref[...], wd[...])
    sigma = jax.nn.sigmoid(gate_pre)
    active = gate_pre * sigma
    hidden = (active * up_pre).astype(BF)
    gate_grad = (hidden_grad * up_pre * sigma * (1.0 + gate_pre * (1.0 - sigma))).astype(BF)
    up_grad = (hidden_grad * active).astype(BF)
    prob = jnp.sum(hidden.astype(F32) * hidden_grad, axis=1, keepdims=True)
    hid_ref[...] = hidden
    gu_ref[:, 0:FF] = gate_grad
    gu_ref[:, FF : 2 * FF] = up_grad
    row = count((1, ROWS), 1)
    row_block, _ = split_by(row, CAP)
    to_block, to_at = split_by(count((SLOTS * BACK, 1), 0), BACK)
    lay = jnp.where((to_at < CAP) & (row == to_block * CAP + to_at), 1.0, 0.0).astype(BF)
    lay_prob = jnp.where((to_at == CAP) & (row_block == to_block), 1.0, 0.0).astype(BF)
    prob_wide = jnp.where(count((1, PART), 1) == at, prob, 0.0).astype(BF)
    prob_rows = mm(lay_prob, prob_wide)
    dims = ((1,), (1,))
    for n in range(8):
        cols = pl.ds(n * 256, 256)
        grad = mm(gate_grad, wg[cols, :], dims) + mm(up_grad, wu[cols, :], dims)
        laid = mm(lay, grad.astype(BF))
        if n == 0:
            back_ref[:, 0:PART] = (laid[:, 0:PART] + prob_rows).astype(BF)
            back_ref[:, PART:256] = laid[:, PART:256].astype(BF)
        else:
            back_ref[:, cols] = laid.astype(BF)


def expert_rows(info, rows, quarters):
    whole = pl.BlockSpec(memory_space=pltpu.VMEM)
    anywhere = pl.BlockSpec(memory_space=pl.ANY)
    return pl.pallas_call(
        expert_kernel,
        out_shape=[
            jax.ShapeDtypeStruct((SLOTS * BACK, D), BF),
            jax.ShapeDtypeStruct((ROWS, D), BF),
            jax.ShapeDtypeStruct((ROWS, D), BF),
            jax.ShapeDtypeStruct((ROWS, FF), BF),
            jax.ShapeDtypeStruct((ROWS, 2 * FF), BF),
        ],
        in_specs=[pl.BlockSpec(memory_space=pltpu.SMEM), whole] + [anywhere] * 4,
        out_specs=[whole] * 5,
        scratch_shapes=[
            pltpu.VMEM((SLOTS, PART, FF), BF),
            pltpu.VMEM((SLOTS, PART, FF), BF),
            pltpu.VMEM((SLOTS, PART, FF), BF),
            pltpu.SemaphoreType.DMA((12,)),
        ],
        compiler_params=vmem(32),
        cost_estimate=pl.CostEstimate(
            flops=16 * ROWS * D * FF, bytes_accessed=14 * MIB, transcendentals=ROWS * FF
        ),
    )(info, rows, *quarters)


def sums_kernel(kinds, info, a_ref, b_ref, own_ref, oth_ref):
    def run(core):
        for n in range(8):
            part = mm(a_ref[:, pl.ds(n * 256, 256)], b_ref[...], ((0,), (0,))).astype(BF)
            for piece in range(2):
                for q in range(4):
                    rows = slice(piece * PART + q * OWN, piece * PART + (q + 1) * OWN)
                    ref = own_ref if q // 2 == core else oth_ref
                    to = (info[0] % 2) ^ (q % 2)
                    for kind in range(kinds):
                        ref[to, 2 * n + piece, kind * OWN : (kind + 1) * OWN, :] = part[
                            rows, kind * FF : (kind + 1) * FF
                        ]

    @pl.when(info[0] // 2 == 0)
    def _():
        run(0)

    @pl.when(info[0] // 2 == 1)
    def _():
        run(1)


def weight_sums(info, a, b, flops):
    kinds = b.shape[1] // FF
    shape = jax.ShapeDtypeStruct((2, SLOTS, kinds * OWN, FF), BF)
    whole = pl.BlockSpec(memory_space=pltpu.VMEM)
    return pl.pallas_call(
        functools.partial(sums_kernel, kinds),
        out_shape=[shape, shape],
        in_specs=[pl.BlockSpec(memory_space=pltpu.SMEM), whole, whole],
        compiler_params=vmem(24),
        cost_estimate=pl.CostEstimate(
            flops=flops, bytes_accessed=1024, transcendentals=0
        ),
    )(info, a, b)


def join_kernel(notes_ref, back_ref, g_ref, sect_ref, route_ref):
    notes = notes_ref[...].astype(F32)
    rows = SLOTS * BACK
    seat, first, second = seats(notes, BACK, CAP)
    seat = jnp.where(second == 0.0, seat, 0.0)
    slot, at = split_by(count((rows, 1), 0), BACK)
    to_prob = jnp.where(count((1, rows), 1) == slot * BACK + CAP, 1.0, 0.0).astype(BF)
    probs = mm(to_prob, back_ref[:, 0:PART])
    prob = jnp.sum(jnp.where(count((1, PART), 1) == at, probs, 0.0), axis=1, keepdims=True)
    share = seat * prob
    route_first = jnp.sum(jnp.where(first, share, 0.0), axis=0, keepdims=True)
    route_second = jnp.sum(jnp.where(first, 0.0, share), axis=0, keepdims=True)
    line = lax.broadcasted_iota(jnp.int32, (8, TOK), 0)
    route = jnp.where(
        line == 0,
        route_first / notes[2:3, :],
        jnp.where(line == 1, route_second / notes[3:4, :], 0.0),
    )
    route_ref[...] = route.astype(BF)
    pick = seat.astype(BF)
    for n in range(4):
        cols = pl.ds(n * 512, 512)
        branch = mm(pick, back_ref[:, cols], ((0,), (0,))).astype(BF).astype(F32)
        sect_ref[:, cols] = (g_ref[:, cols].astype(F32) + branch).astype(BF)


def join_rows(notes, back, g):
    return pl.pallas_call(
        join_kernel,
        out_shape=[jax.ShapeDtypeStruct((TOK, D), BF), jax.ShapeDtypeStruct((8, TOK), BF)],
        compiler_params=vmem(16),
        cost_estimate=pl.CostEstimate(
            flops=2 * SLOTS * BACK * TOK * D, bytes_accessed=3 * MIB, transcendentals=0
        ),
    )(notes, back, g)


def merge_kernel(info, got_ref, *refs):
    outs, sums = refs[:-1], refs[-1]
    for kind, out in enumerate(outs):
        rows = slice(kind * OWN, (kind + 1) * OWN)
        for e in range(EXPERTS):
            sums[e] = got_ref[e, rows, :].astype(F32)
        for r in range(EXPERTS):
            e = info[r]
            sums[e] = sums[e] + got_ref[EXPERTS + r, rows, :].astype(F32)
        out[0] = (sums[...] * SCALE).astype(BF)


def merge_slots(info, got, flops):
    kinds = got.shape[1] // OWN
    return pl.pallas_call(
        merge_kernel,
        out_shape=[jax.ShapeDtypeStruct((1, EXPERTS, OWN, FF), BF)] * kinds,
        in_specs=[pl.BlockSpec(memory_space=pltpu.SMEM), pl.BlockSpec(memory_space=pltpu.VMEM)],
        scratch_shapes=[pltpu.VMEM((EXPERTS, OWN, FF), F32)],
        compiler_params=vmem(16),
        cost_estimate=pl.CostEstimate(
            flops=flops, bytes_accessed=kinds * MIB, transcendentals=0
        ),
    )(info, got)


def add_kernel(*refs):
    total = refs[0][0].astype(F32) + refs[1][0].astype(F32)
    for ref in refs[2:-1]:
        total = total + ref[...].astype(F32)
    refs[-1][...] = total.astype(BF)


def add(which, pairs, *more, cost=0):
    shape = pairs[0].shape[1:]
    block = (4,) + shape[1:]
    pair = pl.BlockSpec((1,) + block, lambda n: (which, n, 0, 0))
    one = pl.BlockSpec(block, lambda n: (n, 0, 0))
    return pl.pallas_call(
        add_kernel,
        out_shape=jax.ShapeDtypeStruct(shape, BF),
        grid=(4,),
        in_specs=[pair, pair] + [one] * len(more),
        out_specs=one,
        compiler_params=vmem(16),
        cost_estimate=pl.CostEstimate(flops=cost, bytes_accessed=1024, transcendentals=0),
    )(*pairs, *more)


def keep_kernel(in_ref, out_ref):
    out_ref[...] = in_ref[...]


def keep(x):
    return pl.pallas_call(
        keep_kernel,
        out_shape=jax.ShapeDtypeStruct(x.shape, x.dtype),
        compiler_params=vmem(8),
        cost_estimate=pl.CostEstimate(flops=0, bytes_accessed=MIB, transcendentals=0),
    )(x)


def shards(tokens_in, grad_out, route_weight, slot_of, replica_of, w_gate, w_up, w_down):
    pipe, dp = lax.axis_index("pipe"), lax.axis_index("dp")
    core, side, near = pipe % 2, dp // 2, dp % 2
    mine = core == side
    quarter = (2 * core + near).astype(jnp.int32)
    spot = quarter[None]

    weights = (w_gate, w_up, w_down)
    asked = (2 * (1 - core) + near) * PART
    other = jnp.concatenate([lax.dynamic_slice_in_dim(w[0], asked, PART, 2) for w in weights])
    other, tokens = lax.optimization_barrier((other, tokens_in[0]))
    other = move(other, CORES)
    replicas = jnp.where(mine, replica_of[0], move(replica_of[0], CORES))
    x = move(tokens, TURN)

    info = jnp.concatenate(
        [
            jnp.arange(EXPERTS, dtype=jnp.int32),
            replicas,
            jnp.stack([quarter, mine.astype(jnp.int32)]),
        ]
    )
    notes = jnp.concatenate(
        [slot_of[0].T.astype(BF), route_weight[0].T, jnp.zeros((4, TOK), BF)], axis=0
    )
    picked = pick_weights(info, weights, other)
    picked, notes, grads = lax.optimization_barrier((picked, notes, grad_out[0]))
    notes = move(notes, TURN)
    g = move(grads, TURN)
    first = spread(picked)
    rows = pack_rows(notes, x, g)
    first, rows = lax.optimization_barrier((first, rows))
    second = move(first, NEAR)
    third, fourth = move(first, CORES), move(second, CORES)

    rows = spread(rows.reshape(SLOTS, 2 * CAP, D)).reshape(2 * ROWS, D)
    back, xs, scaled, hidden, grads = expert_rows(spot, rows, (first, second, third, fourth))
    down = weight_sums(spot, scaled, hidden, 0)
    xs, down, back = lax.optimization_barrier((xs, down, back))
    back = spread(back.reshape(SLOTS, BACK, D)).reshape(SLOTS * BACK, D)
    pair = weight_sums(spot, xs, grads, 10**10)
    down = (down[0], move(down[1], CORES))
    sent, pair = lax.optimization_barrier((add(1, down), pair))
    got, _ = lax.optimization_barrier((move(sent, NEAR), pair))
    down = add(0, down, got)
    pair = (pair[0], move(pair[1], CORES))
    got, sent = lax.optimization_barrier((got, add(1, pair, cost=10**11)))
    sent = move(sent, NEAR)

    sect, route = join_rows(notes, back, g)
    route = move(route, TURN)
    pair = add(0, pair, sent)
    sect, down = lax.optimization_barrier((sect, spread(down)))
    grad_in = keep(move(sect, BEHIND))

    (down,) = merge_slots(replicas, down, 10**11)
    down = move(down, TURN)
    pair, route, grad_in = lax.optimization_barrier((spread(pair), route, grad_in))
    gate, up = (move(part, TURN) for part in merge_slots(replicas, pair, 0))
    return (grad_in[None], route[0:2].T[None], gate, up, down)


def solution(mesh):
    return jax.shard_map(
        shards,
        mesh=mesh,
        in_specs=(
            P("pipe", ("expert", "dp"), None),
            P("pipe", ("expert", "dp"), None),
            P("pipe", ("expert", "dp"), None),
            P("pipe", ("expert", "dp"), None),
            P("pipe", None),
            P("pipe", None, "expert", None),
            P("pipe", None, "expert", None),
            P("pipe", None, "expert", None),
        ),
        out_specs=(
            P("pipe", ("expert", "dp"), None),
            P("pipe", ("expert", "dp"), None),
            P("pipe", None, ("expert", "dp"), None),
            P("pipe", None, ("expert", "dp"), None),
            P("pipe", None, ("expert", "dp"), None),
        ),
        check_vma=False,
    )
```

```python
import functools

import jax
import jax.numpy as jnp
from jax import lax
from jax.experimental import pallas as pl
from jax.experimental.pallas import tpu as pltpu
from jax.sharding import PartitionSpec as P

EXPERTS = 8
CAP = 20
SLOTS = 16
ROWS = SLOTS * CAP
BACK = 24
TOK = 128
D = 2048
FF = 512
PART = 128
OWN = 32
BF = jnp.bfloat16
F32 = jnp.float32
MIB = 1 << 20
SCALE = 8192.0**-0.5


def place(zh, c, k, b):
    return (2 * zh + c) * 4 + 2 * k + b


SPOTS = [(zh, c, k, b) for zh in range(2) for c in range(2) for k in range(2) for b in range(2)]
TURN = [(place(zh, c, k, b), place(zh, k, c, b)) for zh, c, k, b in SPOTS]
CORES = [(place(zh, c, k, b), place(zh, 1 - c, k, b)) for zh, c, k, b in SPOTS]
NEAR = [(place(zh, c, k, b), place(zh, c, k, 1 - b)) for zh, c, k, b in SPOTS]
BEHIND = [(place(zh, c, k, b), ((2 * zh + k - 1) % 4) * 4 + 2 * c + b) for zh, c, k, b in SPOTS]


def move(x, pairs):
    return lax.ppermute(x, ("pipe", "dp"), pairs)


def spread(x):
    return lax.all_to_all(x, "expert", split_axis=0, concat_axis=0, tiled=True)


def mm(a, b, dims=((1,), (0,))):
    return lax.dot_general(a, b, (dims, ((), ())), preferred_element_type=F32)


def count(shape, dim):
    return lax.broadcasted_iota(jnp.int32, shape, dim).astype(F32)


def split_by(index, size):
    block = jnp.floor((index + 0.5) * (1.0 / size))
    return block, index - block * size


def vmem(limit, **kw):
    return pltpu.CompilerParams(vmem_limit_bytes=limit * MIB, **kw)


def pick_kernel(info, gate, up, down, other, out, held, sem_in, sem_out):
    lanes = pl.ds(pl.multiple_of(info[SLOTS] * PART, PART), PART)

    def fetch(refs):
        copies = [
            pltpu.make_async_copy(ref, held.at[n], sem_in.at[n]) for n, ref in enumerate(refs)
        ]
        for copy in copies:
            copy.start()
        for copy in copies:
            copy.wait()

    @pl.when(info[SLOTS + 1] == 1)
    def _():
        fetch([ref.at[0, :, :, lanes] for ref in (gate, up, down)])

    @pl.when(info[SLOTS + 1] == 0)
    def _():
        fetch([other.at[pl.ds(n * EXPERTS, EXPERTS)] for n in range(3)])

    copies = [
        pltpu.make_async_copy(
            held.at[n, info[slot]],
            out.at[slot, pl.ds(n * PART, PART), :],
            sem_out.at[slot * 3 + n],
        )
        for slot in range(SLOTS)
        for n in range(3)
    ]
    for copy in copies:
        copy.start()
    for copy in copies:
        copy.wait()


def pick_weights(info, mine, other):
    hbm = pl.BlockSpec(memory_space=pltpu.HBM)
    anywhere = pl.BlockSpec(memory_space=pl.ANY)
    return pl.pallas_call(
        pick_kernel,
        out_shape=jax.ShapeDtypeStruct((SLOTS, 3 * PART, PART), BF),
        in_specs=[pl.BlockSpec(memory_space=pltpu.SMEM)] + [hbm] * 3 + [anywhere],
        out_specs=anywhere,
        scratch_shapes=[
            pltpu.VMEM((3, EXPERTS, PART, PART), BF),
            pltpu.SemaphoreType.DMA((3,)),
            pltpu.SemaphoreType.DMA((3 * SLOTS,)),
        ],
        compiler_params=vmem(60),
        cost_estimate=pl.CostEstimate(flops=0, bytes_accessed=4 * MIB, transcendentals=0),
    )(info, *mine, other)


def seats(notes, size, caps):
    rows = SLOTS * size
    slot, at = split_by(count((rows, 1), 0), size)
    second, rank = split_by(at, caps)
    first = notes[0:1, :] == slot
    other = notes[1:2, :] == slot
    held = jnp.where(first | other, 1.0, 0.0)
    before = jnp.where(count((TOK, TOK), 0) < count((TOK, TOK), 1), 1.0, 0.0)
    taken = mm(held.astype(BF), before.astype(BF))
    seat = jnp.where(taken == rank, held, 0.0)
    return seat, first, second


def pack_kernel(notes_ref, x_ref, g_ref, out_ref):
    notes = notes_ref[...].astype(F32)
    seat, first, second = seats(notes, 2 * CAP, CAP)
    weight = jnp.where(first, notes[2:3, :], notes[3:4, :])
    pick_x = jnp.where(second == 0.0, seat, 0.0).astype(BF)
    pick_g = jnp.where(second == 1.0, seat * weight, 0.0).astype(BF)
    for n in range(4):
        at = pl.ds(n * 512, 512)
        out_ref[:, at] = (mm(pick_x, x_ref[:, at]) + mm(pick_g, g_ref[:, at])).astype(BF)


def pack_rows(notes, x, g):
    return pl.pallas_call(
        pack_kernel,
        out_shape=jax.ShapeDtypeStruct((2 * ROWS, D), BF),
        compiler_params=vmem(16),
        cost_estimate=pl.CostEstimate(
            flops=200 * ROWS * TOK * D, bytes_accessed=128 * MIB, transcendentals=0
        ),
    )(notes, x, g)


def expert_kernel(
    info,
    rows_ref,
    w0,
    w1,
    w2,
    w3,
    back_ref,
    x_ref,
    s_ref,
    hid_ref,
    gu_ref,
    sg,
    su,
    sd,
    sem,
):
    copies = [
        pltpu.make_async_copy(
            ref.at[:, pl.ds(n * PART, PART), :],
            stack.at[:, :, pl.ds(pl.multiple_of((info[0] ^ side) * PART, PART), PART)],
            sem.at[4 * n + side],
        )
        for n, stack in enumerate((sg, su, sd))
        for side, ref in enumerate((w0, w1, w2, w3))
    ]
    for copy in copies:
        copy.start()
    wg, wu, wd = sg.reshape(D, FF), su.reshape(D, FF), sd.reshape(D, FF)
    source = count((1, 2 * ROWS), 1)
    block, at = split_by(count((ROWS, 1), 0), CAP)
    take_x = jnp.where(source == block * (2 * CAP) + at, 1.0, 0.0).astype(BF)
    take_s = jnp.where(source == block * (2 * CAP) + CAP + at, 1.0, 0.0).astype(BF)
    for n in range(4):
        cols = pl.ds(n * 512, 512)
        x_ref[:, cols] = mm(take_x, rows_ref[:, cols]).astype(BF)
        s_ref[:, cols] = mm(take_s, rows_ref[:, cols]).astype(BF)
    for copy in copies:
        copy.wait()
    gate_pre = mm(x_ref[...], wg[...])
    up_pre = mm(x_ref[...], wu[...])
    hidden_grad = mm(s_ref[...], wd[...])
    sigma = jax.nn.sigmoid(gate_pre)
    active = gate_pre * sigma
    hidden = (active * up_pre).astype(BF)
    gate_grad = (hidden_grad * up_pre * sigma * (1.0 + gate_pre * (1.0 - sigma))).astype(BF)
    up_grad = (hidden_grad * active).astype(BF)
    prob = jnp.sum(hidden.astype(F32) * hidden_grad, axis=1, keepdims=True)
    hid_ref[...] = hidden
    gu_ref[:, 0:FF] = gate_grad
    gu_ref[:, FF : 2 * FF] = up_grad
    row = count((1, ROWS), 1)
    row_block, _ = split_by(row, CAP)
    to_block, to_at = split_by(count((SLOTS * BACK, 1), 0), BACK)
    lay = jnp.where((to_at < CAP) & (row == to_block * CAP + to_at), 1.0, 0.0).astype(BF)
    lay_prob = jnp.where((to_at == CAP) & (row_block == to_block), 1.0, 0.0).astype(BF)
    prob_wide = jnp.where(count((1, PART), 1) == at, prob, 0.0).astype(BF)
    prob_rows = mm(lay_prob, prob_wide)
    dims = ((1,), (1,))
    for n in range(8):
        cols = pl.ds(n * 256, 256)
        grad = mm(gate_grad, wg[cols, :], dims) + mm(up_grad, wu[cols, :], dims)
        laid = mm(lay, grad.astype(BF))
        if n == 0:
            back_ref[:, 0:PART] = (laid[:, 0:PART] + prob_rows).astype(BF)
            back_ref[:, PART:256] = laid[:, PART:256].astype(BF)
        else:
            back_ref[:, cols] = laid.astype(BF)


def expert_rows(info, rows, quarters):
    whole = pl.BlockSpec(memory_space=pltpu.VMEM)
    anywhere = pl.BlockSpec(memory_space=pl.ANY)
    return pl.pallas_call(
        expert_kernel,
        out_shape=[
            jax.ShapeDtypeStruct((SLOTS * BACK, D), BF),
            jax.ShapeDtypeStruct((ROWS, D), BF),
            jax.ShapeDtypeStruct((ROWS, D), BF),
            jax.ShapeDtypeStruct((ROWS, FF), BF),
            jax.ShapeDtypeStruct((ROWS, 2 * FF), BF),
        ],
        in_specs=[pl.BlockSpec(memory_space=pltpu.SMEM), whole] + [anywhere] * 4,
        out_specs=[whole] * 5,
        scratch_shapes=[
            pltpu.VMEM((SLOTS, PART, FF), BF),
            pltpu.VMEM((SLOTS, PART, FF), BF),
            pltpu.VMEM((SLOTS, PART, FF), BF),
            pltpu.SemaphoreType.DMA((12,)),
        ],
        compiler_params=vmem(32),
        cost_estimate=pl.CostEstimate(
            flops=16 * ROWS * D * FF, bytes_accessed=14 * MIB, transcendentals=ROWS * FF
        ),
    )(info, rows, *quarters)


def sums_kernel(kinds, info, a_ref, b_ref, own_ref, oth_ref):
    def run(core):
        for n in range(8):
            part = mm(a_ref[:, pl.ds(n * 256, 256)], b_ref[...], ((0,), (0,))).astype(BF)
            for piece in range(2):
                for q in range(4):
                    rows = slice(piece * PART + q * OWN, piece * PART + (q + 1) * OWN)
                    ref = own_ref if q // 2 == core else oth_ref
                    to = (info[0] % 2) ^ (q % 2)
                    for kind in range(kinds):
                        ref[to, 2 * n + piece, kind * OWN : (kind + 1) * OWN, :] = part[
                            rows, kind * FF : (kind + 1) * FF
                        ]

    @pl.when(info[0] // 2 == 0)
    def _():
        run(0)

    @pl.when(info[0] // 2 == 1)
    def _():
        run(1)


def weight_sums(info, a, b, flops):
    kinds = b.shape[1] // FF
    shape = jax.ShapeDtypeStruct((2, SLOTS, kinds * OWN, FF), BF)
    whole = pl.BlockSpec(memory_space=pltpu.VMEM)
    return pl.pallas_call(
        functools.partial(sums_kernel, kinds),
        out_shape=[shape, shape],
        in_specs=[pl.BlockSpec(memory_space=pltpu.SMEM), whole, whole],
        compiler_params=vmem(24),
        cost_estimate=pl.CostEstimate(
            flops=flops, bytes_accessed=1024, transcendentals=0
        ),
    )(info, a, b)


def join_kernel(notes_ref, back_ref, g_ref, sect_ref, route_ref):
    notes = notes_ref[...].astype(F32)
    rows = SLOTS * BACK
    seat, first, second = seats(notes, BACK, CAP)
    seat = jnp.where(second == 0.0, seat, 0.0)
    slot, at = split_by(count((rows, 1), 0), BACK)
    to_prob = jnp.where(count((1, rows), 1) == slot * BACK + CAP, 1.0, 0.0).astype(BF)
    probs = mm(to_prob, back_ref[:, 0:PART])
    prob = jnp.sum(jnp.where(count((1, PART), 1) == at, probs, 0.0), axis=1, keepdims=True)
    share = seat * prob
    route_first = jnp.sum(jnp.where(first, share, 0.0), axis=0, keepdims=True)
    route_second = jnp.sum(jnp.where(first, 0.0, share), axis=0, keepdims=True)
    line = lax.broadcasted_iota(jnp.int32, (8, TOK), 0)
    route = jnp.where(
        line == 0,
        route_first / notes[2:3, :],
        jnp.where(line == 1, route_second / notes[3:4, :], 0.0),
    )
    route_ref[...] = route.astype(BF)
    pick = seat.astype(BF)
    for n in range(4):
        cols = pl.ds(n * 512, 512)
        branch = mm(pick, back_ref[:, cols], ((0,), (0,))).astype(BF).astype(F32)
        sect_ref[:, cols] = (g_ref[:, cols].astype(F32) + branch).astype(BF)


def join_rows(notes, back, g):
    return pl.pallas_call(
        join_kernel,
        out_shape=[jax.ShapeDtypeStruct((TOK, D), BF), jax.ShapeDtypeStruct((8, TOK), BF)],
        compiler_params=vmem(16),
        cost_estimate=pl.CostEstimate(
            flops=2 * SLOTS * BACK * TOK * D, bytes_accessed=3 * MIB, transcendentals=0
        ),
    )(notes, back, g)


def merge_kernel(info, got_ref, out, sums):
    for kind in range(out.shape[0]):
        rows = slice(kind * OWN, (kind + 1) * OWN)
        for e in range(EXPERTS):
            sums[e] = got_ref[e, rows, :].astype(F32)
        for r in range(EXPERTS):
            e = info[r]
            sums[e] = sums[e] + got_ref[EXPERTS + r, rows, :].astype(F32)
        out[kind] = (sums[...] * SCALE).astype(BF)


def merge_slots(info, got, flops):
    kinds = got.shape[1] // OWN
    return pl.pallas_call(
        merge_kernel,
        out_shape=jax.ShapeDtypeStruct((kinds, EXPERTS, OWN, FF), BF),
        in_specs=[pl.BlockSpec(memory_space=pltpu.SMEM), pl.BlockSpec(memory_space=pltpu.VMEM)],
        scratch_shapes=[pltpu.VMEM((EXPERTS, OWN, FF), F32)],
        compiler_params=vmem(16),
        cost_estimate=pl.CostEstimate(
            flops=flops, bytes_accessed=kinds * MIB, transcendentals=0
        ),
    )(info, got)


def add_kernel(*refs):
    total = refs[0][0].astype(F32) + refs[1][0].astype(F32)
    for ref in refs[2:-1]:
        total = total + ref[...].astype(F32)
    refs[-1][...] = total.astype(BF)


def add(which, pairs, *more, cost=0, room=16):
    shape = pairs[0].shape[1:]
    block = (4,) + shape[1:]
    pair = pl.BlockSpec((1,) + block, lambda n: (which, n, 0, 0))
    one = pl.BlockSpec(block, lambda n: (n, 0, 0))
    return pl.pallas_call(
        add_kernel,
        out_shape=jax.ShapeDtypeStruct(shape, BF),
        grid=(4,),
        in_specs=[pair, pair] + [one] * len(more),
        out_specs=one,
        compiler_params=vmem(room),
        cost_estimate=pl.CostEstimate(flops=cost, bytes_accessed=1024, transcendentals=0),
    )(*pairs, *more)


def keep_kernel(in_ref, out_ref):
    out_ref[...] = in_ref[...]


def keep(x):
    return pl.pallas_call(
        keep_kernel,
        out_shape=jax.ShapeDtypeStruct(x.shape, x.dtype),
        compiler_params=vmem(8),
        cost_estimate=pl.CostEstimate(flops=0, bytes_accessed=MIB, transcendentals=0),
    )(x)


def shards(tokens_in, grad_out, route_weight, slot_of, replica_of, w_gate, w_up, w_down):
    pipe, dp = lax.axis_index("pipe"), lax.axis_index("dp")
    core, side, near = pipe % 2, dp // 2, dp % 2
    mine = core == side
    quarter = (2 * core + near).astype(jnp.int32)
    spot = quarter[None]

    weights = (w_gate, w_up, w_down)
    asked = (2 * (1 - core) + near) * PART
    other = jnp.concatenate([lax.dynamic_slice_in_dim(w[0], asked, PART, 2) for w in weights])
    other, tokens = lax.optimization_barrier((other, tokens_in[0]))
    other = move(other, CORES)
    replicas = jnp.where(mine, replica_of[0], move(replica_of[0], CORES))
    x = move(tokens, TURN)

    info = jnp.concatenate(
        [
            jnp.arange(EXPERTS, dtype=jnp.int32),
            replicas,
            jnp.stack([quarter, mine.astype(jnp.int32)]),
        ]
    )
    notes = jnp.concatenate(
        [slot_of[0].T.astype(BF), route_weight[0].T, jnp.zeros((4, TOK), BF)], axis=0
    )
    picked = pick_weights(info, weights, other)
    picked, notes, grads = lax.optimization_barrier((picked, notes, grad_out[0]))
    notes = move(notes, TURN)
    g = move(grads, TURN)
    first = spread(picked)
    rows = pack_rows(notes, x, g)
    first, rows = lax.optimization_barrier((first, rows))
    second = move(first, NEAR)
    third, fourth = move(first, CORES), move(second, CORES)

    rows = spread(rows.reshape(SLOTS, 2 * CAP, D)).reshape(2 * ROWS, D)
    back, xs, scaled, hidden, grads = expert_rows(spot, rows, (first, second, third, fourth))
    down = weight_sums(spot, scaled, hidden, 0)
    xs, down, back = lax.optimization_barrier((xs, down, back))
    back = spread(back.reshape(SLOTS, BACK, D)).reshape(SLOTS * BACK, D)
    pair = weight_sums(spot, xs, grads, 10**10)
    down = (down[0], move(down[1], CORES))
    sent, pair = lax.optimization_barrier((add(1, down), pair))
    got, _ = lax.optimization_barrier((move(sent, NEAR), pair))
    down = add(0, down, got)
    pair = (pair[0], move(pair[1], CORES))
    got, sent = lax.optimization_barrier((got, add(1, pair, cost=10**11, room=56)))
    sent = move(sent, NEAR)

    back, down = lax.optimization_barrier((back, down))
    sect, route = join_rows(notes, back, g)
    route = move(route, TURN)
    pair = add(0, pair, sent, room=56)
    down, pair = lax.optimization_barrier((spread(down), pair))
    grad_in = keep(move(sect, BEHIND))

    down = move(merge_slots(replicas, down, 10**11), TURN)
    pair, route, grad_in, down = lax.optimization_barrier((spread(pair), route, grad_in, down))
    pair = move(merge_slots(replicas, pair, 0), TURN)
    return (grad_in[None], route[0:2].T[None], pair[0:1], pair[1:2], down)


def solution(mesh):
    return jax.shard_map(
        shards,
        mesh=mesh,
        in_specs=(
            P("pipe", ("expert", "dp"), None),
            P("pipe", ("expert", "dp"), None),
            P("pipe", ("expert", "dp"), None),
            P("pipe", ("expert", "dp"), None),
            P("pipe", None),
            P("pipe", None, "expert", None),
            P("pipe", None, "expert", None),
            P("pipe", None, "expert", None),
        ),
        out_specs=(
            P("pipe", ("expert", "dp"), None),
            P("pipe", ("expert", "dp"), None),
            P("pipe", None, ("expert", "dp"), None),
            P("pipe", None, ("expert", "dp"), None),
            P("pipe", None, ("expert", "dp"), None),
        ),
        check_vma=False,
    )
```

```python
import functools

import jax
import jax.numpy as jnp
from jax import lax
from jax.experimental import pallas as pl
from jax.experimental.pallas import tpu as pltpu
from jax.sharding import PartitionSpec as P

EXPERTS = 8
CAP = 20
SLOTS = 16
ROWS = SLOTS * CAP
BACK = 24
TOK = 128
D = 2048
FF = 512
PART = 128
OWN = 32
BF = jnp.bfloat16
F32 = jnp.float32
MIB = 1 << 20
SCALE = 8192.0**-0.5


def place(zh, c, k, b):
    return (2 * zh + c) * 4 + 2 * k + b


SPOTS = [(zh, c, k, b) for zh in range(2) for c in range(2) for k in range(2) for b in range(2)]
TURN = [(place(zh, c, k, b), place(zh, k, c, b)) for zh, c, k, b in SPOTS]
CORES = [(place(zh, c, k, b), place(zh, 1 - c, k, b)) for zh, c, k, b in SPOTS]
NEAR = [(place(zh, c, k, b), place(zh, c, k, 1 - b)) for zh, c, k, b in SPOTS]
BEHIND = [(place(zh, c, k, b), ((2 * zh + k - 1) % 4) * 4 + 2 * c + b) for zh, c, k, b in SPOTS]


def move(x, pairs):
    return lax.ppermute(x, ("pipe", "dp"), pairs)


def spread(x):
    return lax.all_to_all(x, "expert", split_axis=0, concat_axis=0, tiled=True)


def mm(a, b, dims=((1,), (0,))):
    return lax.dot_general(a, b, (dims, ((), ())), preferred_element_type=F32)


def count(shape, dim):
    return lax.broadcasted_iota(jnp.int32, shape, dim).astype(F32)


def split_by(index, size):
    block = jnp.floor((index + 0.5) * (1.0 / size))
    return block, index - block * size


def vmem(limit, **kw):
    return pltpu.CompilerParams(vmem_limit_bytes=limit * MIB, **kw)


def pick_kernel(info, gate, up, down, other, out, held, sem_in, sem_out):
    lanes = pl.ds(pl.multiple_of(info[SLOTS] * PART, PART), PART)

    def fetch(refs):
        copies = [
            pltpu.make_async_copy(ref, held.at[n], sem_in.at[n]) for n, ref in enumerate(refs)
        ]
        for copy in copies:
            copy.start()
        for copy in copies:
            copy.wait()

    @pl.when(info[SLOTS + 1] == 1)
    def _():
        fetch([ref.at[0, :, :, lanes] for ref in (gate, up, down)])

    @pl.when(info[SLOTS + 1] == 0)
    def _():
        fetch([other.at[pl.ds(n * EXPERTS, EXPERTS)] for n in range(3)])

    copies = [
        pltpu.make_async_copy(
            held.at[n, info[slot]],
            out.at[slot, pl.ds(n * PART, PART), :],
            sem_out.at[slot * 3 + n],
        )
        for slot in range(SLOTS)
        for n in range(3)
    ]
    for copy in copies:
        copy.start()
    for copy in copies:
        copy.wait()


def pick_weights(info, mine, other):
    hbm = pl.BlockSpec(memory_space=pltpu.HBM)
    anywhere = pl.BlockSpec(memory_space=pl.ANY)
    return pl.pallas_call(
        pick_kernel,
        out_shape=jax.ShapeDtypeStruct((SLOTS, 3 * PART, PART), BF),
        in_specs=[pl.BlockSpec(memory_space=pltpu.SMEM)] + [hbm] * 3 + [anywhere],
        out_specs=anywhere,
        scratch_shapes=[
            pltpu.VMEM((3, EXPERTS, PART, PART), BF),
            pltpu.SemaphoreType.DMA((3,)),
            pltpu.SemaphoreType.DMA((3 * SLOTS,)),
        ],
        compiler_params=vmem(60),
        cost_estimate=pl.CostEstimate(flops=0, bytes_accessed=4 * MIB, transcendentals=0),
    )(info, *mine, other)


def seats(notes, size, caps):
    rows = SLOTS * size
    slot, at = split_by(count((rows, 1), 0), size)
    second, rank = split_by(at, caps)
    first = notes[0:1, :] == slot
    other = notes[1:2, :] == slot
    held = jnp.where(first | other, 1.0, 0.0)
    before = jnp.where(count((TOK, TOK), 0) < count((TOK, TOK), 1), 1.0, 0.0)
    taken = mm(held.astype(BF), before.astype(BF))
    seat = jnp.where(taken == rank, held, 0.0)
    return seat, first, second


def pack_kernel(notes_ref, x_ref, g_ref, out_ref):
    notes = notes_ref[...].astype(F32)
    seat, first, second = seats(notes, 2 * CAP, CAP)
    weight = jnp.where(first, notes[2:3, :], notes[3:4, :])
    pick_x = jnp.where(second == 0.0, seat, 0.0).astype(BF)
    pick_g = jnp.where(second == 1.0, seat * weight, 0.0).astype(BF)
    for n in range(4):
        at = pl.ds(n * 512, 512)
        out_ref[:, at] = (mm(pick_x, x_ref[:, at]) + mm(pick_g, g_ref[:, at])).astype(BF)


def pack_rows(notes, x, g):
    return pl.pallas_call(
        pack_kernel,
        out_shape=jax.ShapeDtypeStruct((2 * ROWS, D), BF),
        compiler_params=vmem(16),
        cost_estimate=pl.CostEstimate(
            flops=200 * ROWS * TOK * D, bytes_accessed=128 * MIB, transcendentals=0
        ),
    )(notes, x, g)


def expert_kernel(
    info,
    rows_ref,
    w0,
    w1,
    w2,
    w3,
    back_ref,
    x_ref,
    s_ref,
    hid_ref,
    gu_ref,
    sg,
    su,
    sd,
    sem,
):
    copies = [
        pltpu.make_async_copy(
            ref.at[:, pl.ds(n * PART, PART), :],
            stack.at[:, :, pl.ds(pl.multiple_of((info[0] ^ side) * PART, PART), PART)],
            sem.at[4 * n + side],
        )
        for n, stack in enumerate((sg, su, sd))
        for side, ref in enumerate((w0, w1, w2, w3))
    ]
    for copy in copies:
        copy.start()
    wg, wu, wd = sg.reshape(D, FF), su.reshape(D, FF), sd.reshape(D, FF)
    source = count((1, 2 * ROWS), 1)
    block, at = split_by(count((ROWS, 1), 0), CAP)
    take_x = jnp.where(source == block * (2 * CAP) + at, 1.0, 0.0).astype(BF)
    take_s = jnp.where(source == block * (2 * CAP) + CAP + at, 1.0, 0.0).astype(BF)
    for n in range(4):
        cols = pl.ds(n * 512, 512)
        x_ref[:, cols] = mm(take_x, rows_ref[:, cols]).astype(BF)
        s_ref[:, cols] = mm(take_s, rows_ref[:, cols]).astype(BF)
    for copy in copies:
        copy.wait()
    gate_pre = mm(x_ref[...], wg[...])
    up_pre = mm(x_ref[...], wu[...])
    hidden_grad = mm(s_ref[...], wd[...])
    sigma = jax.nn.sigmoid(gate_pre)
    active = gate_pre * sigma
    hidden = (active * up_pre).astype(BF)
    gate_grad = (hidden_grad * up_pre * sigma * (1.0 + gate_pre * (1.0 - sigma))).astype(BF)
    up_grad = (hidden_grad * active).astype(BF)
    prob = jnp.sum(hidden.astype(F32) * hidden_grad, axis=1, keepdims=True)
    hid_ref[...] = hidden
    gu_ref[:, 0:FF] = gate_grad
    gu_ref[:, FF : 2 * FF] = up_grad
    row = count((1, ROWS), 1)
    row_block, _ = split_by(row, CAP)
    to_block, to_at = split_by(count((SLOTS * BACK, 1), 0), BACK)
    lay = jnp.where((to_at < CAP) & (row == to_block * CAP + to_at), 1.0, 0.0).astype(BF)
    lay_prob = jnp.where((to_at == CAP) & (row_block == to_block), 1.0, 0.0).astype(BF)
    prob_wide = jnp.where(count((1, PART), 1) == at, prob, 0.0).astype(BF)
    prob_rows = mm(lay_prob, prob_wide)
    dims = ((1,), (1,))
    for n in range(8):
        cols = pl.ds(n * 256, 256)
        grad = mm(gate_grad, wg[cols, :], dims) + mm(up_grad, wu[cols, :], dims)
        laid = mm(lay, grad.astype(BF))
        if n == 0:
            back_ref[:, 0:PART] = (laid[:, 0:PART] + prob_rows).astype(BF)
            back_ref[:, PART:256] = laid[:, PART:256].astype(BF)
        else:
            back_ref[:, cols] = laid.astype(BF)


def expert_rows(info, rows, quarters):
    whole = pl.BlockSpec(memory_space=pltpu.VMEM)
    anywhere = pl.BlockSpec(memory_space=pl.ANY)
    return pl.pallas_call(
        expert_kernel,
        out_shape=[
            jax.ShapeDtypeStruct((SLOTS * BACK, D), BF),
            jax.ShapeDtypeStruct((ROWS, D), BF),
            jax.ShapeDtypeStruct((ROWS, D), BF),
            jax.ShapeDtypeStruct((ROWS, FF), BF),
            jax.ShapeDtypeStruct((ROWS, 2 * FF), BF),
        ],
        in_specs=[pl.BlockSpec(memory_space=pltpu.SMEM), whole] + [anywhere] * 4,
        out_specs=[whole] * 5,
        scratch_shapes=[
            pltpu.VMEM((SLOTS, PART, FF), BF),
            pltpu.VMEM((SLOTS, PART, FF), BF),
            pltpu.VMEM((SLOTS, PART, FF), BF),
            pltpu.SemaphoreType.DMA((12,)),
        ],
        compiler_params=vmem(32),
        cost_estimate=pl.CostEstimate(
            flops=16 * ROWS * D * FF, bytes_accessed=14 * MIB, transcendentals=ROWS * FF
        ),
    )(info, rows, *quarters)


def sums_kernel(kinds, info, a_ref, b_ref, own_ref, oth_ref):
    def run(core):
        for n in range(8):
            part = mm(a_ref[:, pl.ds(n * 256, 256)], b_ref[...], ((0,), (0,))).astype(BF)
            for piece in range(2):
                for q in range(4):
                    rows = slice(piece * PART + q * OWN, piece * PART + (q + 1) * OWN)
                    ref = own_ref if q // 2 == core else oth_ref
                    to = (info[0] % 2) ^ (q % 2)
                    for kind in range(kinds):
                        ref[to, 2 * n + piece, kind * OWN : (kind + 1) * OWN, :] = part[
                            rows, kind * FF : (kind + 1) * FF
                        ]

    @pl.when(info[0] // 2 == 0)
    def _():
        run(0)

    @pl.when(info[0] // 2 == 1)
    def _():
        run(1)


def weight_sums(info, a, b, flops):
    kinds = b.shape[1] // FF
    shape = jax.ShapeDtypeStruct((2, SLOTS, kinds * OWN, FF), BF)
    whole = pl.BlockSpec(memory_space=pltpu.VMEM)
    return pl.pallas_call(
        functools.partial(sums_kernel, kinds),
        out_shape=[shape, shape],
        in_specs=[pl.BlockSpec(memory_space=pltpu.SMEM), whole, whole],
        compiler_params=vmem(24),
        cost_estimate=pl.CostEstimate(
            flops=flops, bytes_accessed=1024, transcendentals=0
        ),
    )(info, a, b)


def join_kernel(notes_ref, back_ref, g_ref, sect_ref, route_ref):
    notes = notes_ref[...].astype(F32)
    rows = SLOTS * BACK
    seat, first, second = seats(notes, BACK, CAP)
    seat = jnp.where(second == 0.0, seat, 0.0)
    slot, at = split_by(count((rows, 1), 0), BACK)
    to_prob = jnp.where(count((1, rows), 1) == slot * BACK + CAP, 1.0, 0.0).astype(BF)
    probs = mm(to_prob, back_ref[:, 0:PART])
    prob = jnp.sum(jnp.where(count((1, PART), 1) == at, probs, 0.0), axis=1, keepdims=True)
    share = seat * prob
    route_first = jnp.sum(jnp.where(first, share, 0.0), axis=0, keepdims=True)
    route_second = jnp.sum(jnp.where(first, 0.0, share), axis=0, keepdims=True)
    line = lax.broadcasted_iota(jnp.int32, (8, TOK), 0)
    route = jnp.where(
        line == 0,
        route_first / notes[2:3, :],
        jnp.where(line == 1, route_second / notes[3:4, :], 0.0),
    )
    route_ref[...] = route.astype(BF)
    pick = seat.astype(BF)
    for n in range(4):
        cols = pl.ds(n * 512, 512)
        branch = mm(pick, back_ref[:, cols], ((0,), (0,))).astype(BF).astype(F32)
        sect_ref[:, cols] = (g_ref[:, cols].astype(F32) + branch).astype(BF)


def join_rows(notes, back, g):
    return pl.pallas_call(
        join_kernel,
        out_shape=[jax.ShapeDtypeStruct((TOK, D), BF), jax.ShapeDtypeStruct((8, TOK), BF)],
        compiler_params=vmem(16),
        cost_estimate=pl.CostEstimate(
            flops=2 * SLOTS * BACK * TOK * D, bytes_accessed=3 * MIB, transcendentals=0
        ),
    )(notes, back, g)


def merge_kernel(info, got_ref, out, sums):
    for kind in range(out.shape[0]):
        rows = slice(kind * OWN, (kind + 1) * OWN)
        for e in range(EXPERTS):
            sums[e] = got_ref[e, rows, :].astype(F32)
        for r in range(EXPERTS):
            e = info[r]
            sums[e] = sums[e] + got_ref[EXPERTS + r, rows, :].astype(F32)
        out[kind] = (sums[...] * SCALE).astype(BF)


def merge_slots(info, got, flops):
    kinds = got.shape[1] // OWN
    return pl.pallas_call(
        merge_kernel,
        out_shape=jax.ShapeDtypeStruct((kinds, EXPERTS, OWN, FF), BF),
        in_specs=[pl.BlockSpec(memory_space=pltpu.SMEM), pl.BlockSpec(memory_space=pltpu.VMEM)],
        scratch_shapes=[pltpu.VMEM((EXPERTS, OWN, FF), F32)],
        compiler_params=vmem(16),
        cost_estimate=pl.CostEstimate(
            flops=flops, bytes_accessed=kinds * MIB, transcendentals=0
        ),
    )(info, got)


def add_kernel(*refs):
    total = refs[0][0].astype(F32) + refs[1][0].astype(F32)
    for ref in refs[2:-1]:
        total = total + ref[...].astype(F32)
    refs[-1][...] = total.astype(BF)


def add(which, pairs, *more, cost=0, room=16):
    shape = pairs[0].shape[1:]
    block = (4,) + shape[1:]
    pair = pl.BlockSpec((1,) + block, lambda n: (which, n, 0, 0))
    one = pl.BlockSpec(block, lambda n: (n, 0, 0))
    return pl.pallas_call(
        add_kernel,
        out_shape=jax.ShapeDtypeStruct(shape, BF),
        grid=(4,),
        in_specs=[pair, pair] + [one] * len(more),
        out_specs=one,
        compiler_params=vmem(room),
        cost_estimate=pl.CostEstimate(flops=cost, bytes_accessed=1024, transcendentals=0),
    )(*pairs, *more)


def keep_kernel(in_ref, out_ref):
    out_ref[...] = in_ref[...]


def keep(x):
    return pl.pallas_call(
        keep_kernel,
        out_shape=jax.ShapeDtypeStruct(x.shape, x.dtype),
        compiler_params=vmem(8),
        cost_estimate=pl.CostEstimate(flops=0, bytes_accessed=MIB, transcendentals=0),
    )(x)


def shards(tokens_in, grad_out, route_weight, slot_of, replica_of, w_gate, w_up, w_down):
    pipe, dp = lax.axis_index("pipe"), lax.axis_index("dp")
    core, side, near = pipe % 2, dp // 2, dp % 2
    mine = core == side
    quarter = (2 * core + near).astype(jnp.int32)
    spot = quarter[None]

    weights = (w_gate, w_up, w_down)
    asked = (2 * (1 - core) + near) * PART
    other = jnp.concatenate([lax.dynamic_slice_in_dim(w[0], asked, PART, 2) for w in weights])
    other, tokens = lax.optimization_barrier((other, tokens_in[0]))
    other = move(other, CORES)
    replicas = jnp.where(mine, replica_of[0], move(replica_of[0], CORES))
    x = move(tokens, TURN)

    info = jnp.concatenate(
        [
            jnp.arange(EXPERTS, dtype=jnp.int32),
            replicas,
            jnp.stack([quarter, mine.astype(jnp.int32)]),
        ]
    )
    notes = jnp.concatenate(
        [slot_of[0].T.astype(BF), route_weight[0].T, jnp.zeros((4, TOK), BF)], axis=0
    )
    picked = pick_weights(info, weights, other)
    notes = move(notes, TURN)
    picked, notes, grads = lax.optimization_barrier((picked, notes, grad_out[0]))
    g = move(grads, TURN)
    first = spread(picked)
    rows = pack_rows(notes, x, g)
    first, rows = lax.optimization_barrier((first, rows))
    second = move(first, NEAR)
    third, fourth = move(first, CORES), move(second, CORES)

    rows = spread(rows.reshape(SLOTS, 2 * CAP, D)).reshape(2 * ROWS, D)
    back, xs, scaled, hidden, grads = expert_rows(spot, rows, (first, second, third, fourth))
    down = weight_sums(spot, scaled, hidden, 0)
    xs, down, back = lax.optimization_barrier((xs, down, back))
    back = spread(back.reshape(SLOTS, BACK, D)).reshape(SLOTS * BACK, D)
    pair = weight_sums(spot, xs, grads, 10**10)
    down = (down[0], move(down[1], CORES))
    sent, pair = lax.optimization_barrier((add(1, down), pair))
    got, _ = lax.optimization_barrier((move(sent, NEAR), pair))
    down = add(0, down, got)
    pair = (pair[0], move(pair[1], CORES))
    got, sent = lax.optimization_barrier((got, add(1, pair, cost=10**11, room=56)))
    sent = move(sent, NEAR)

    back, down = lax.optimization_barrier((back, down))
    sect, route = join_rows(notes, back, g)
    route = move(route, TURN)
    pair = add(0, pair, sent, room=56)
    down, pair = lax.optimization_barrier((spread(down), pair))
    grad_in = keep(move(sect, BEHIND))

    down = move(merge_slots(replicas, down, 10**11), TURN)
    pair, route, grad_in, down = lax.optimization_barrier((spread(pair), route, grad_in, down))
    pair = move(merge_slots(replicas, pair, 0), TURN)
    return (grad_in[None], route[0:2].T[None], pair[0:1], pair[1:2], down)


def solution(mesh):
    return jax.shard_map(
        shards,
        mesh=mesh,
        in_specs=(
            P("pipe", ("expert", "dp"), None),
            P("pipe", ("expert", "dp"), None),
            P("pipe", ("expert", "dp"), None),
            P("pipe", ("expert", "dp"), None),
            P("pipe", None),
            P("pipe", None, "expert", None),
            P("pipe", None, "expert", None),
            P("pipe", None, "expert", None),
        ),
        out_specs=(
            P("pipe", ("expert", "dp"), None),
            P("pipe", ("expert", "dp"), None),
            P("pipe", None, ("expert", "dp"), None),
            P("pipe", None, ("expert", "dp"), None),
            P("pipe", None, ("expert", "dp"), None),
        ),
        check_vma=False,
    )
```

```python
import functools

import jax
import jax.numpy as jnp
from jax import lax
from jax.experimental import pallas as pl
from jax.experimental.pallas import tpu as pltpu
from jax.sharding import PartitionSpec as P

EXPERTS = 8
CAP = 20
SLOTS = 16
ROWS = SLOTS * CAP
BACK = 24
TOK = 128
D = 2048
FF = 512
PART = 128
OWN = 32
BF = jnp.bfloat16
F32 = jnp.float32
MIB = 1 << 20
SCALE = 8192.0**-0.5


def place(zh, c, k, b):
    return (2 * zh + c) * 4 + 2 * k + b


SPOTS = [(zh, c, k, b) for zh in range(2) for c in range(2) for k in range(2) for b in range(2)]
TURN = [(place(zh, c, k, b), place(zh, k, c, b)) for zh, c, k, b in SPOTS]
CORES = [(place(zh, c, k, b), place(zh, 1 - c, k, b)) for zh, c, k, b in SPOTS]
NEAR = [(place(zh, c, k, b), place(zh, c, k, 1 - b)) for zh, c, k, b in SPOTS]
BEHIND = [(place(zh, c, k, b), ((2 * zh + k - 1) % 4) * 4 + 2 * c + b) for zh, c, k, b in SPOTS]


def move(x, pairs):
    return lax.ppermute(x, ("pipe", "dp"), pairs)


def spread(x):
    return lax.all_to_all(x, "expert", split_axis=0, concat_axis=0, tiled=True)


def mm(a, b, dims=((1,), (0,))):
    return lax.dot_general(a, b, (dims, ((), ())), preferred_element_type=F32)


def count(shape, dim):
    return lax.broadcasted_iota(jnp.int32, shape, dim).astype(F32)


def split_by(index, size):
    block = jnp.floor((index + 0.5) * (1.0 / size))
    return block, index - block * size


def vmem(limit, **kw):
    return pltpu.CompilerParams(vmem_limit_bytes=limit * MIB, **kw)


def pick_kernel(info, gate, up, down, other, out, held, sem_in, sem_out):
    lanes = pl.ds(pl.multiple_of(info[SLOTS] * PART, PART), PART)

    def fetch(refs):
        copies = [
            pltpu.make_async_copy(ref, held.at[n], sem_in.at[n]) for n, ref in enumerate(refs)
        ]
        for copy in copies:
            copy.start()
        for copy in copies:
            copy.wait()

    @pl.when(info[SLOTS + 1] == 1)
    def _():
        fetch([ref.at[0, :, :, lanes] for ref in (gate, up, down)])

    @pl.when(info[SLOTS + 1] == 0)
    def _():
        fetch([other.at[pl.ds(n * EXPERTS, EXPERTS)] for n in range(3)])

    copies = [
        pltpu.make_async_copy(
            held.at[n, info[slot]],
            out.at[slot, pl.ds(n * PART, PART), :],
            sem_out.at[slot * 3 + n],
        )
        for slot in range(SLOTS)
        for n in range(3)
    ]
    for copy in copies:
        copy.start()
    for copy in copies:
        copy.wait()


def pick_weights(info, mine, other):
    hbm = pl.BlockSpec(memory_space=pltpu.HBM)
    anywhere = pl.BlockSpec(memory_space=pl.ANY)
    return pl.pallas_call(
        pick_kernel,
        out_shape=jax.ShapeDtypeStruct((SLOTS, 3 * PART, PART), BF),
        in_specs=[pl.BlockSpec(memory_space=pltpu.SMEM)] + [hbm] * 3 + [anywhere],
        out_specs=anywhere,
        scratch_shapes=[
            pltpu.VMEM((3, EXPERTS, PART, PART), BF),
            pltpu.SemaphoreType.DMA((3,)),
            pltpu.SemaphoreType.DMA((3 * SLOTS,)),
        ],
        compiler_params=vmem(60),
        cost_estimate=pl.CostEstimate(flops=0, bytes_accessed=4 * MIB, transcendentals=0),
    )(info, *mine, other)


def seats(notes, size, caps):
    rows = SLOTS * size
    slot, at = split_by(count((rows, 1), 0), size)
    second, rank = split_by(at, caps)
    first = notes[0:1, :] == slot
    other = notes[1:2, :] == slot
    held = jnp.where(first | other, 1.0, 0.0)
    before = jnp.where(count((TOK, TOK), 0) < count((TOK, TOK), 1), 1.0, 0.0)
    taken = mm(held.astype(BF), before.astype(BF))
    seat = jnp.where(taken == rank, held, 0.0)
    return seat, first, second


def pack_kernel(notes_ref, x_ref, g_ref, out_ref):
    notes = notes_ref[...].astype(F32)
    seat, first, second = seats(notes, 2 * CAP, CAP)
    weight = jnp.where(first, notes[2:3, :], notes[3:4, :])
    pick_x = jnp.where(second == 0.0, seat, 0.0).astype(BF)
    pick_g = jnp.where(second == 1.0, seat * weight, 0.0).astype(BF)
    for n in range(4):
        at = pl.ds(n * 512, 512)
        out_ref[:, at] = (mm(pick_x, x_ref[:, at]) + mm(pick_g, g_ref[:, at])).astype(BF)


def pack_rows(notes, x, g):
    return pl.pallas_call(
        pack_kernel,
        out_shape=jax.ShapeDtypeStruct((2 * ROWS, D), BF),
        compiler_params=vmem(16),
        cost_estimate=pl.CostEstimate(
            flops=200 * ROWS * TOK * D, bytes_accessed=128 * MIB, transcendentals=0
        ),
    )(notes, x, g)


def expert_kernel(
    info,
    rows_ref,
    w0,
    w1,
    w2,
    w3,
    back_ref,
    x_ref,
    s_ref,
    hid_ref,
    gu_ref,
    sg,
    su,
    sd,
    sem,
):
    copies = [
        pltpu.make_async_copy(
            ref.at[:, pl.ds(n * PART, PART), :],
            stack.at[:, :, pl.ds(pl.multiple_of((info[0] ^ side) * PART, PART), PART)],
            sem.at[4 * n + side],
        )
        for n, stack in enumerate((sg, su, sd))
        for side, ref in enumerate((w0, w1, w2, w3))
    ]
    for copy in copies:
        copy.start()
    wg, wu, wd = sg.reshape(D, FF), su.reshape(D, FF), sd.reshape(D, FF)
    source = count((1, 2 * ROWS), 1)
    block, at = split_by(count((ROWS, 1), 0), CAP)
    take_x = jnp.where(source == block * (2 * CAP) + at, 1.0, 0.0).astype(BF)
    take_s = jnp.where(source == block * (2 * CAP) + CAP + at, 1.0, 0.0).astype(BF)
    for n in range(4):
        cols = pl.ds(n * 512, 512)
        x_ref[:, cols] = mm(take_x, rows_ref[:, cols]).astype(BF)
        s_ref[:, cols] = mm(take_s, rows_ref[:, cols]).astype(BF)
    for copy in copies:
        copy.wait()
    gate_pre = mm(x_ref[...], wg[...])
    up_pre = mm(x_ref[...], wu[...])
    hidden_grad = mm(s_ref[...], wd[...])
    sigma = jax.nn.sigmoid(gate_pre)
    active = gate_pre * sigma
    hidden = (active * up_pre).astype(BF)
    gate_grad = (hidden_grad * up_pre * sigma * (1.0 + gate_pre * (1.0 - sigma))).astype(BF)
    up_grad = (hidden_grad * active).astype(BF)
    prob = jnp.sum(hidden.astype(F32) * hidden_grad, axis=1, keepdims=True)
    hid_ref[...] = hidden
    gu_ref[:, 0:FF] = gate_grad
    gu_ref[:, FF : 2 * FF] = up_grad
    row = count((1, ROWS), 1)
    row_block, _ = split_by(row, CAP)
    to_block, to_at = split_by(count((SLOTS * BACK, 1), 0), BACK)
    lay = jnp.where((to_at < CAP) & (row == to_block * CAP + to_at), 1.0, 0.0).astype(BF)
    lay_prob = jnp.where((to_at == CAP) & (row_block == to_block), 1.0, 0.0).astype(BF)
    prob_wide = jnp.where(count((1, PART), 1) == at, prob, 0.0).astype(BF)
    prob_rows = mm(lay_prob, prob_wide)
    dims = ((1,), (1,))
    for n in range(8):
        cols = pl.ds(n * 256, 256)
        grad = mm(gate_grad, wg[cols, :], dims) + mm(up_grad, wu[cols, :], dims)
        laid = mm(lay, grad.astype(BF))
        if n == 0:
            back_ref[:, 0:PART] = (laid[:, 0:PART] + prob_rows).astype(BF)
            back_ref[:, PART:256] = laid[:, PART:256].astype(BF)
        else:
            back_ref[:, cols] = laid.astype(BF)


def expert_rows(info, rows, quarters):
    whole = pl.BlockSpec(memory_space=pltpu.VMEM)
    anywhere = pl.BlockSpec(memory_space=pl.ANY)
    return pl.pallas_call(
        expert_kernel,
        out_shape=[
            jax.ShapeDtypeStruct((SLOTS * BACK, D), BF),
            jax.ShapeDtypeStruct((ROWS, D), BF),
            jax.ShapeDtypeStruct((ROWS, D), BF),
            jax.ShapeDtypeStruct((ROWS, FF), BF),
            jax.ShapeDtypeStruct((ROWS, 2 * FF), BF),
        ],
        in_specs=[pl.BlockSpec(memory_space=pltpu.SMEM), whole] + [anywhere] * 4,
        out_specs=[whole] * 5,
        scratch_shapes=[
            pltpu.VMEM((SLOTS, PART, FF), BF),
            pltpu.VMEM((SLOTS, PART, FF), BF),
            pltpu.VMEM((SLOTS, PART, FF), BF),
            pltpu.SemaphoreType.DMA((12,)),
        ],
        compiler_params=vmem(32),
        cost_estimate=pl.CostEstimate(
            flops=16 * ROWS * D * FF, bytes_accessed=14 * MIB, transcendentals=ROWS * FF
        ),
    )(info, rows, *quarters)


def sums_kernel(kinds, info, a_ref, b_ref, own_ref, oth_ref):
    def run(core):
        for n in range(8):
            part = mm(a_ref[:, pl.ds(n * 256, 256)], b_ref[...], ((0,), (0,))).astype(BF)
            for piece in range(2):
                for q in range(4):
                    rows = slice(piece * PART + q * OWN, piece * PART + (q + 1) * OWN)
                    ref = own_ref if q // 2 == core else oth_ref
                    to = (info[0] % 2) ^ (q % 2)
                    for kind in range(kinds):
                        ref[to, 2 * n + piece, kind * OWN : (kind + 1) * OWN, :] = part[
                            rows, kind * FF : (kind + 1) * FF
                        ]

    @pl.when(info[0] // 2 == 0)
    def _():
        run(0)

    @pl.when(info[0] // 2 == 1)
    def _():
        run(1)


def weight_sums(info, a, b, flops):
    kinds = b.shape[1] // FF
    shape = jax.ShapeDtypeStruct((2, SLOTS, kinds * OWN, FF), BF)
    whole = pl.BlockSpec(memory_space=pltpu.VMEM)
    return pl.pallas_call(
        functools.partial(sums_kernel, kinds),
        out_shape=[shape, shape],
        in_specs=[pl.BlockSpec(memory_space=pltpu.SMEM), whole, whole],
        compiler_params=vmem(24),
        cost_estimate=pl.CostEstimate(
            flops=flops, bytes_accessed=1024, transcendentals=0
        ),
    )(info, a, b)


def join_kernel(notes_ref, back_ref, g_ref, sect_ref, route_ref):
    notes = notes_ref[...].astype(F32)
    rows = SLOTS * BACK
    seat, first, second = seats(notes, BACK, CAP)
    seat = jnp.where(second == 0.0, seat, 0.0)
    slot, at = split_by(count((rows, 1), 0), BACK)
    to_prob = jnp.where(count((1, rows), 1) == slot * BACK + CAP, 1.0, 0.0).astype(BF)
    probs = mm(to_prob, back_ref[:, 0:PART])
    prob = jnp.sum(jnp.where(count((1, PART), 1) == at, probs, 0.0), axis=1, keepdims=True)
    share = seat * prob
    route_first = jnp.sum(jnp.where(first, share, 0.0), axis=0, keepdims=True)
    route_second = jnp.sum(jnp.where(first, 0.0, share), axis=0, keepdims=True)
    line = lax.broadcasted_iota(jnp.int32, (8, TOK), 0)
    route = jnp.where(
        line == 0,
        route_first / notes[2:3, :],
        jnp.where(line == 1, route_second / notes[3:4, :], 0.0),
    )
    route_ref[...] = route.astype(BF)
    pick = seat.astype(BF)
    for n in range(4):
        cols = pl.ds(n * 512, 512)
        branch = mm(pick, back_ref[:, cols], ((0,), (0,))).astype(BF).astype(F32)
        sect_ref[:, cols] = (g_ref[:, cols].astype(F32) + branch).astype(BF)


def join_rows(notes, back, g):
    return pl.pallas_call(
        join_kernel,
        out_shape=[jax.ShapeDtypeStruct((TOK, D), BF), jax.ShapeDtypeStruct((8, TOK), BF)],
        compiler_params=vmem(16),
        cost_estimate=pl.CostEstimate(
            flops=2 * SLOTS * BACK * TOK * D, bytes_accessed=3 * MIB, transcendentals=0
        ),
    )(notes, back, g)


def merge_kernel(info, got_ref, out, sums):
    for kind in range(out.shape[0]):
        rows = slice(kind * OWN, (kind + 1) * OWN)
        for e in range(EXPERTS):
            sums[e] = got_ref[e, rows, :].astype(F32)
        for r in range(EXPERTS):
            e = info[r]
            sums[e] = sums[e] + got_ref[EXPERTS + r, rows, :].astype(F32)
        out[kind] = (sums[...] * SCALE).astype(BF)


def merge_slots(info, got, flops):
    kinds = got.shape[1] // OWN
    return pl.pallas_call(
        merge_kernel,
        out_shape=jax.ShapeDtypeStruct((kinds, EXPERTS, OWN, FF), BF),
        in_specs=[pl.BlockSpec(memory_space=pltpu.SMEM), pl.BlockSpec(memory_space=pltpu.VMEM)],
        scratch_shapes=[pltpu.VMEM((EXPERTS, OWN, FF), F32)],
        compiler_params=vmem(16),
        cost_estimate=pl.CostEstimate(
            flops=flops, bytes_accessed=kinds * MIB, transcendentals=0
        ),
    )(info, got)


def add_kernel(*refs):
    total = refs[0][0].astype(F32) + refs[1][0].astype(F32)
    for ref in refs[2:-1]:
        total = total + ref[...].astype(F32)
    refs[-1][...] = total.astype(BF)


def add(which, pairs, *more, cost=0, room=16):
    shape = pairs[0].shape[1:]
    block = (8,) + shape[1:]
    pair = pl.BlockSpec((1,) + block, lambda n: (which, n, 0, 0))
    one = pl.BlockSpec(block, lambda n: (n, 0, 0))
    return pl.pallas_call(
        add_kernel,
        out_shape=jax.ShapeDtypeStruct(shape, BF),
        grid=(2,),
        in_specs=[pair, pair] + [one] * len(more),
        out_specs=one,
        compiler_params=vmem(room),
        cost_estimate=pl.CostEstimate(flops=cost, bytes_accessed=1024, transcendentals=0),
    )(*pairs, *more)


def keep_kernel(in_ref, out_ref):
    out_ref[...] = in_ref[...]


def keep(x):
    return pl.pallas_call(
        keep_kernel,
        out_shape=jax.ShapeDtypeStruct(x.shape, x.dtype),
        compiler_params=vmem(8),
        cost_estimate=pl.CostEstimate(flops=0, bytes_accessed=MIB, transcendentals=0),
    )(x)


def shards(tokens_in, grad_out, route_weight, slot_of, replica_of, w_gate, w_up, w_down):
    pipe, dp = lax.axis_index("pipe"), lax.axis_index("dp")
    core, side, near = pipe % 2, dp // 2, dp % 2
    mine = core == side
    quarter = (2 * core + near).astype(jnp.int32)
    spot = quarter[None]

    weights = (w_gate, w_up, w_down)
    asked = (2 * (1 - core) + near) * PART
    other = jnp.concatenate([lax.dynamic_slice_in_dim(w[0], asked, PART, 2) for w in weights])
    other, tokens = lax.optimization_barrier((other, tokens_in[0]))
    other = move(other, CORES)
    replicas = jnp.where(mine, replica_of[0], move(replica_of[0], CORES))
    x = move(tokens, TURN)

    info = jnp.concatenate(
        [
            jnp.arange(EXPERTS, dtype=jnp.int32),
            replicas,
            jnp.stack([quarter, mine.astype(jnp.int32)]),
        ]
    )
    notes = jnp.concatenate(
        [slot_of[0].T.astype(BF), route_weight[0].T, jnp.zeros((4, TOK), BF)], axis=0
    )
    picked = pick_weights(info, weights, other)
    picked, notes, grads = lax.optimization_barrier((picked, notes, grad_out[0]))
    notes = move(notes, TURN)
    g = move(grads, TURN)
    first = spread(picked)
    rows = pack_rows(notes, x, g)
    first, rows = lax.optimization_barrier((first, rows))
    second = move(first, NEAR)
    third, fourth = move(first, CORES), move(second, CORES)

    rows = spread(rows.reshape(SLOTS, 2 * CAP, D)).reshape(2 * ROWS, D)
    back, xs, scaled, hidden, grads = expert_rows(spot, rows, (first, second, third, fourth))
    down = weight_sums(spot, scaled, hidden, 0)
    xs, down, back = lax.optimization_barrier((xs, down, back))
    back = spread(back.reshape(SLOTS, BACK, D)).reshape(SLOTS * BACK, D)
    pair = weight_sums(spot, xs, grads, 10**10)
    down = (down[0], move(down[1], CORES))
    sent, pair = lax.optimization_barrier((add(1, down), pair))
    got, _ = lax.optimization_barrier((move(sent, NEAR), pair))
    down = add(0, down, got)
    pair = (pair[0], move(pair[1], CORES))
    got, sent = lax.optimization_barrier((got, add(1, pair, cost=10**11, room=56)))
    sent = move(sent, NEAR)

    back, down = lax.optimization_barrier((back, down))
    sect, route = join_rows(notes, back, g)
    route = move(route, TURN)
    pair = add(0, pair, sent, room=56)
    down, pair = lax.optimization_barrier((spread(down), pair))
    grad_in = keep(move(sect, BEHIND))

    down = move(merge_slots(replicas, down, 10**11), TURN)
    pair, route, grad_in, down = lax.optimization_barrier((spread(pair), route, grad_in, down))
    pair = move(merge_slots(replicas, pair, 0), TURN)
    return (grad_in[None], route[0:2].T[None], pair[0:1], pair[1:2], down)


def solution(mesh):
    return jax.shard_map(
        shards,
        mesh=mesh,
        in_specs=(
            P("pipe", ("expert", "dp"), None),
            P("pipe", ("expert", "dp"), None),
            P("pipe", ("expert", "dp"), None),
            P("pipe", ("expert", "dp"), None),
            P("pipe", None),
            P("pipe", None, "expert", None),
            P("pipe", None, "expert", None),
            P("pipe", None, "expert", None),
        ),
        out_specs=(
            P("pipe", ("expert", "dp"), None),
            P("pipe", ("expert", "dp"), None),
            P("pipe", None, ("expert", "dp"), None),
            P("pipe", None, ("expert", "dp"), None),
            P("pipe", None, ("expert", "dp"), None),
        ),
        check_vma=False,
    )
```

```python
import functools

import jax
import jax.numpy as jnp
from jax import lax
from jax.experimental import pallas as pl
from jax.experimental.pallas import tpu as pltpu
from jax.sharding import PartitionSpec as P

EXPERTS = 8
CAP = 20
SLOTS = 16
ROWS = SLOTS * CAP
BACK = 24
TOK = 128
D = 2048
FF = 512
PART = 128
OWN = 32
BF = jnp.bfloat16
F32 = jnp.float32
MIB = 1 << 20
SCALE = 8192.0**-0.5


def place(zh, c, k, b):
    return (2 * zh + c) * 4 + 2 * k + b


SPOTS = [(zh, c, k, b) for zh in range(2) for c in range(2) for k in range(2) for b in range(2)]
TURN = [(place(zh, c, k, b), place(zh, k, c, b)) for zh, c, k, b in SPOTS]
CORES = [(place(zh, c, k, b), place(zh, 1 - c, k, b)) for zh, c, k, b in SPOTS]
NEAR = [(place(zh, c, k, b), place(zh, c, k, 1 - b)) for zh, c, k, b in SPOTS]
BEHIND = [(place(zh, c, k, b), ((2 * zh + k - 1) % 4) * 4 + 2 * c + b) for zh, c, k, b in SPOTS]


def move(x, pairs):
    return lax.ppermute(x, ("pipe", "dp"), pairs)


def spread(x):
    return lax.all_to_all(x, "expert", split_axis=0, concat_axis=0, tiled=True)


def mm(a, b, dims=((1,), (0,))):
    return lax.dot_general(a, b, (dims, ((), ())), preferred_element_type=F32)


def count(shape, dim):
    return lax.broadcasted_iota(jnp.int32, shape, dim).astype(F32)


def split_by(index, size):
    block = jnp.floor((index + 0.5) * (1.0 / size))
    return block, index - block * size


def vmem(limit, **kw):
    return pltpu.CompilerParams(vmem_limit_bytes=limit * MIB, **kw)


def pick_kernel(info, gate, up, down, other, out, held, sem_in, sem_out):
    lanes = pl.ds(pl.multiple_of(info[SLOTS] * PART, PART), PART)

    def fetch(refs):
        copies = [
            pltpu.make_async_copy(ref, held.at[n], sem_in.at[n]) for n, ref in enumerate(refs)
        ]
        for copy in copies:
            copy.start()
        for copy in copies:
            copy.wait()

    @pl.when(info[SLOTS + 1] == 1)
    def _():
        fetch([ref.at[0, :, :, lanes] for ref in (gate, up, down)])

    @pl.when(info[SLOTS + 1] == 0)
    def _():
        fetch([other.at[pl.ds(n * EXPERTS, EXPERTS)] for n in range(3)])

    copies = [
        pltpu.make_async_copy(
            held.at[n, info[slot]],
            out.at[slot, pl.ds(n * PART, PART), :],
            sem_out.at[slot * 3 + n],
        )
        for slot in range(SLOTS)
        for n in range(3)
    ]
    for copy in copies:
        copy.start()
    for copy in copies:
        copy.wait()


def pick_weights(info, mine, other):
    hbm = pl.BlockSpec(memory_space=pltpu.HBM)
    anywhere = pl.BlockSpec(memory_space=pl.ANY)
    return pl.pallas_call(
        pick_kernel,
        out_shape=jax.ShapeDtypeStruct((SLOTS, 3 * PART, PART), BF),
        in_specs=[pl.BlockSpec(memory_space=pltpu.SMEM)] + [hbm] * 3 + [anywhere],
        out_specs=anywhere,
        scratch_shapes=[
            pltpu.VMEM((3, EXPERTS, PART, PART), BF),
            pltpu.SemaphoreType.DMA((3,)),
            pltpu.SemaphoreType.DMA((3 * SLOTS,)),
        ],
        compiler_params=vmem(60),
        cost_estimate=pl.CostEstimate(flops=0, bytes_accessed=4 * MIB, transcendentals=0),
    )(info, *mine, other)


def seats(notes, size, caps):
    rows = SLOTS * size
    slot, at = split_by(count((rows, 1), 0), size)
    second, rank = split_by(at, caps)
    first = notes[0:1, :] == slot
    other = notes[1:2, :] == slot
    held = jnp.where(first | other, 1.0, 0.0)
    before = jnp.where(count((TOK, TOK), 0) < count((TOK, TOK), 1), 1.0, 0.0)
    taken = mm(held.astype(BF), before.astype(BF))
    seat = jnp.where(taken == rank, held, 0.0)
    return seat, first, second


def pack_kernel(notes_ref, x_ref, g_ref, out_ref):
    notes = notes_ref[...].astype(F32)
    seat, first, second = seats(notes, 2 * CAP, CAP)
    weight = jnp.where(first, notes[2:3, :], notes[3:4, :])
    pick_x = jnp.where(second == 0.0, seat, 0.0).astype(BF)
    pick_g = jnp.where(second == 1.0, seat * weight, 0.0).astype(BF)
    for n in range(4):
        at = pl.ds(n * 512, 512)
        out_ref[:, at] = (mm(pick_x, x_ref[:, at]) + mm(pick_g, g_ref[:, at])).astype(BF)


def pack_rows(notes, x, g):
    return pl.pallas_call(
        pack_kernel,
        out_shape=jax.ShapeDtypeStruct((2 * ROWS, D), BF),
        compiler_params=vmem(16),
        cost_estimate=pl.CostEstimate(
            flops=200 * ROWS * TOK * D, bytes_accessed=128 * MIB, transcendentals=0
        ),
    )(notes, x, g)


def expert_kernel(
    info,
    rows_ref,
    w0,
    w1,
    w2,
    w3,
    back_ref,
    x_ref,
    s_ref,
    hid_ref,
    gu_ref,
    sg,
    su,
    sd,
    sem,
):
    copies = [
        pltpu.make_async_copy(
            ref.at[:, pl.ds(n * PART, PART), :],
            stack.at[:, :, pl.ds(pl.multiple_of((info[0] ^ side) * PART, PART), PART)],
            sem.at[4 * n + side],
        )
        for n, stack in enumerate((sg, su, sd))
        for side, ref in enumerate((w0, w1, w2, w3))
    ]
    for copy in copies:
        copy.start()
    wg, wu, wd = sg.reshape(D, FF), su.reshape(D, FF), sd.reshape(D, FF)
    source = count((1, 2 * ROWS), 1)
    block, at = split_by(count((ROWS, 1), 0), CAP)
    take_x = jnp.where(source == block * (2 * CAP) + at, 1.0, 0.0).astype(BF)
    take_s = jnp.where(source == block * (2 * CAP) + CAP + at, 1.0, 0.0).astype(BF)
    for n in range(4):
        cols = pl.ds(n * 512, 512)
        x_ref[:, cols] = mm(take_x, rows_ref[:, cols]).astype(BF)
        s_ref[:, cols] = mm(take_s, rows_ref[:, cols]).astype(BF)
    for copy in copies:
        copy.wait()
    gate_pre = mm(x_ref[...], wg[...])
    up_pre = mm(x_ref[...], wu[...])
    hidden_grad = mm(s_ref[...], wd[...])
    sigma = jax.nn.sigmoid(gate_pre)
    active = gate_pre * sigma
    hidden = (active * up_pre).astype(BF)
    gate_grad = (hidden_grad * up_pre * sigma * (1.0 + gate_pre * (1.0 - sigma))).astype(BF)
    up_grad = (hidden_grad * active).astype(BF)
    prob = jnp.sum(hidden.astype(F32) * hidden_grad, axis=1, keepdims=True)
    hid_ref[...] = hidden
    gu_ref[:, 0:FF] = gate_grad
    gu_ref[:, FF : 2 * FF] = up_grad
    row = count((1, ROWS), 1)
    row_block, _ = split_by(row, CAP)
    to_block, to_at = split_by(count((SLOTS * BACK, 1), 0), BACK)
    lay = jnp.where((to_at < CAP) & (row == to_block * CAP + to_at), 1.0, 0.0).astype(BF)
    lay_prob = jnp.where((to_at == CAP) & (row_block == to_block), 1.0, 0.0).astype(BF)
    prob_wide = jnp.where(count((1, PART), 1) == at, prob, 0.0).astype(BF)
    prob_rows = mm(lay_prob, prob_wide)
    dims = ((1,), (1,))
    for n in range(8):
        cols = pl.ds(n * 256, 256)
        grad = mm(gate_grad, wg[cols, :], dims) + mm(up_grad, wu[cols, :], dims)
        laid = mm(lay, grad.astype(BF))
        if n == 0:
            back_ref[:, 0:PART] = (laid[:, 0:PART] + prob_rows).astype(BF)
            back_ref[:, PART:256] = laid[:, PART:256].astype(BF)
        else:
            back_ref[:, cols] = laid.astype(BF)


def expert_rows(info, rows, quarters):
    whole = pl.BlockSpec(memory_space=pltpu.VMEM)
    anywhere = pl.BlockSpec(memory_space=pl.ANY)
    return pl.pallas_call(
        expert_kernel,
        out_shape=[
            jax.ShapeDtypeStruct((SLOTS * BACK, D), BF),
            jax.ShapeDtypeStruct((ROWS, D), BF),
            jax.ShapeDtypeStruct((ROWS, D), BF),
            jax.ShapeDtypeStruct((ROWS, FF), BF),
            jax.ShapeDtypeStruct((ROWS, 2 * FF), BF),
        ],
        in_specs=[pl.BlockSpec(memory_space=pltpu.SMEM), whole] + [anywhere] * 4,
        out_specs=[whole] * 5,
        scratch_shapes=[
            pltpu.VMEM((SLOTS, PART, FF), BF),
            pltpu.VMEM((SLOTS, PART, FF), BF),
            pltpu.VMEM((SLOTS, PART, FF), BF),
            pltpu.SemaphoreType.DMA((12,)),
        ],
        compiler_params=vmem(32),
        cost_estimate=pl.CostEstimate(
            flops=16 * ROWS * D * FF, bytes_accessed=14 * MIB, transcendentals=ROWS * FF
        ),
    )(info, rows, *quarters)


def sums_kernel(kinds, info, a_ref, b_ref, own_ref, oth_ref):
    def run(core):
        for n in range(8):
            part = mm(a_ref[:, pl.ds(n * 256, 256)], b_ref[...], ((0,), (0,))).astype(BF)
            for piece in range(2):
                for q in range(4):
                    rows = slice(piece * PART + q * OWN, piece * PART + (q + 1) * OWN)
                    ref = own_ref if q // 2 == core else oth_ref
                    to = (info[0] % 2) ^ (q % 2)
                    for kind in range(kinds):
                        ref[to, 2 * n + piece, kind * OWN : (kind + 1) * OWN, :] = part[
                            rows, kind * FF : (kind + 1) * FF
                        ]

    @pl.when(info[0] // 2 == 0)
    def _():
        run(0)

    @pl.when(info[0] // 2 == 1)
    def _():
        run(1)


def weight_sums(info, a, b, flops):
    kinds = b.shape[1] // FF
    shape = jax.ShapeDtypeStruct((2, SLOTS, kinds * OWN, FF), BF)
    whole = pl.BlockSpec(memory_space=pltpu.VMEM)
    return pl.pallas_call(
        functools.partial(sums_kernel, kinds),
        out_shape=[shape, shape],
        in_specs=[pl.BlockSpec(memory_space=pltpu.SMEM), whole, whole],
        compiler_params=vmem(24),
        cost_estimate=pl.CostEstimate(
            flops=flops, bytes_accessed=1024, transcendentals=0
        ),
    )(info, a, b)


def join_kernel(notes_ref, back_ref, g_ref, sect_ref, route_ref):
    notes = notes_ref[...].astype(F32)
    rows = SLOTS * BACK
    seat, first, second = seats(notes, BACK, CAP)
    seat = jnp.where(second == 0.0, seat, 0.0)
    slot, at = split_by(count((rows, 1), 0), BACK)
    to_prob = jnp.where(count((1, rows), 1) == slot * BACK + CAP, 1.0, 0.0).astype(BF)
    probs = mm(to_prob, back_ref[:, 0:PART])
    prob = jnp.sum(jnp.where(count((1, PART), 1) == at, probs, 0.0), axis=1, keepdims=True)
    share = seat * prob
    route_first = jnp.sum(jnp.where(first, share, 0.0), axis=0, keepdims=True)
    route_second = jnp.sum(jnp.where(first, 0.0, share), axis=0, keepdims=True)
    line = lax.broadcasted_iota(jnp.int32, (8, TOK), 0)
    route = jnp.where(
        line == 0,
        route_first / notes[2:3, :],
        jnp.where(line == 1, route_second / notes[3:4, :], 0.0),
    )
    route_ref[...] = route.astype(BF)
    pick = seat.astype(BF)
    for n in range(4):
        cols = pl.ds(n * 512, 512)
        branch = mm(pick, back_ref[:, cols], ((0,), (0,))).astype(BF).astype(F32)
        sect_ref[:, cols] = (g_ref[:, cols].astype(F32) + branch).astype(BF)


def join_rows(notes, back, g):
    return pl.pallas_call(
        join_kernel,
        out_shape=[jax.ShapeDtypeStruct((TOK, D), BF), jax.ShapeDtypeStruct((8, TOK), BF)],
        compiler_params=vmem(16),
        cost_estimate=pl.CostEstimate(
            flops=2 * SLOTS * BACK * TOK * D, bytes_accessed=3 * MIB, transcendentals=0
        ),
    )(notes, back, g)


def merge_kernel(info, got_ref, out, sums):
    for kind in range(out.shape[0]):
        rows = slice(kind * OWN, (kind + 1) * OWN)
        for e in range(EXPERTS):
            sums[e] = got_ref[e, rows, :].astype(F32)
        for r in range(EXPERTS):
            e = info[r]
            sums[e] = sums[e] + got_ref[EXPERTS + r, rows, :].astype(F32)
        out[kind] = (sums[...] * SCALE).astype(BF)


def merge_slots(info, got, flops):
    kinds = got.shape[1] // OWN
    return pl.pallas_call(
        merge_kernel,
        out_shape=jax.ShapeDtypeStruct((kinds, EXPERTS, OWN, FF), BF),
        in_specs=[pl.BlockSpec(memory_space=pltpu.SMEM), pl.BlockSpec(memory_space=pltpu.VMEM)],
        scratch_shapes=[pltpu.VMEM((EXPERTS, OWN, FF), F32)],
        compiler_params=vmem(16),
        cost_estimate=pl.CostEstimate(
            flops=flops, bytes_accessed=kinds * MIB, transcendentals=0
        ),
    )(info, got)


def add_kernel(*refs):
    total = refs[0][0].astype(F32) + refs[1][0].astype(F32)
    for ref in refs[2:-1]:
        total = total + ref[...].astype(F32)
    refs[-1][...] = total.astype(BF)


def add(which, pairs, *more, cost=0, room=16):
    shape = pairs[0].shape[1:]
    block = (16,) + shape[1:]
    pair = pl.BlockSpec((1,) + block, lambda n: (which, n, 0, 0))
    one = pl.BlockSpec(block, lambda n: (n, 0, 0))
    return pl.pallas_call(
        add_kernel,
        out_shape=jax.ShapeDtypeStruct(shape, BF),
        grid=(1,),
        in_specs=[pair, pair] + [one] * len(more),
        out_specs=one,
        compiler_params=vmem(room),
        cost_estimate=pl.CostEstimate(flops=cost, bytes_accessed=1024, transcendentals=0),
    )(*pairs, *more)


def keep_kernel(in_ref, out_ref):
    out_ref[...] = in_ref[...]


def keep(x):
    return pl.pallas_call(
        keep_kernel,
        out_shape=jax.ShapeDtypeStruct(x.shape, x.dtype),
        compiler_params=vmem(8),
        cost_estimate=pl.CostEstimate(flops=0, bytes_accessed=MIB, transcendentals=0),
    )(x)


def shards(tokens_in, grad_out, route_weight, slot_of, replica_of, w_gate, w_up, w_down):
    pipe, dp = lax.axis_index("pipe"), lax.axis_index("dp")
    core, side, near = pipe % 2, dp // 2, dp % 2
    mine = core == side
    quarter = (2 * core + near).astype(jnp.int32)
    spot = quarter[None]

    weights = (w_gate, w_up, w_down)
    asked = (2 * (1 - core) + near) * PART
    other = jnp.concatenate([lax.dynamic_slice_in_dim(w[0], asked, PART, 2) for w in weights])
    other, tokens = lax.optimization_barrier((other, tokens_in[0]))
    other = move(other, CORES)
    replicas = jnp.where(mine, replica_of[0], move(replica_of[0], CORES))
    x = move(tokens, TURN)

    info = jnp.concatenate(
        [
            jnp.arange(EXPERTS, dtype=jnp.int32),
            replicas,
            jnp.stack([quarter, mine.astype(jnp.int32)]),
        ]
    )
    notes = jnp.concatenate(
        [slot_of[0].T.astype(BF), route_weight[0].T, jnp.zeros((4, TOK), BF)], axis=0
    )
    picked = pick_weights(info, weights, other)
    picked, notes, grads = lax.optimization_barrier((picked, notes, grad_out[0]))
    notes = move(notes, TURN)
    g = move(grads, TURN)
    first = spread(picked)
    rows = pack_rows(notes, x, g)
    first, rows = lax.optimization_barrier((first, rows))
    second = move(first, NEAR)
    third, fourth = move(first, CORES), move(second, CORES)

    rows = spread(rows.reshape(SLOTS, 2 * CAP, D)).reshape(2 * ROWS, D)
    back, xs, scaled, hidden, grads = expert_rows(spot, rows, (first, second, third, fourth))
    down = weight_sums(spot, scaled, hidden, 0)
    xs, down, back = lax.optimization_barrier((xs, down, back))
    back = spread(back.reshape(SLOTS, BACK, D)).reshape(SLOTS * BACK, D)
    pair = weight_sums(spot, xs, grads, 10**10)
    down = (down[0], move(down[1], CORES))
    sent, pair = lax.optimization_barrier((add(1, down), pair))
    got, _ = lax.optimization_barrier((move(sent, NEAR), pair))
    down = add(0, down, got)
    pair = (pair[0], move(pair[1], CORES))
    got, sent = lax.optimization_barrier((got, add(1, pair, cost=10**11, room=56)))
    sent = move(sent, NEAR)

    back, down = lax.optimization_barrier((back, down))
    sect, route = join_rows(notes, back, g)
    route = move(route, TURN)
    pair = add(0, pair, sent, room=56)
    down, pair = lax.optimization_barrier((spread(down), pair))
    grad_in = keep(move(sect, BEHIND))

    down = move(merge_slots(replicas, down, 10**11), TURN)
    pair, route, grad_in, down = lax.optimization_barrier((spread(pair), route, grad_in, down))
    pair = move(merge_slots(replicas, pair, 0), TURN)
    return (grad_in[None], route[0:2].T[None], pair[0:1], pair[1:2], down)


def solution(mesh):
    return jax.shard_map(
        shards,
        mesh=mesh,
        in_specs=(
            P("pipe", ("expert", "dp"), None),
            P("pipe", ("expert", "dp"), None),
            P("pipe", ("expert", "dp"), None),
            P("pipe", ("expert", "dp"), None),
            P("pipe", None),
            P("pipe", None, "expert", None),
            P("pipe", None, "expert", None),
            P("pipe", None, "expert", None),
        ),
        out_specs=(
            P("pipe", ("expert", "dp"), None),
            P("pipe", ("expert", "dp"), None),
            P("pipe", None, ("expert", "dp"), None),
            P("pipe", None, ("expert", "dp"), None),
            P("pipe", None, ("expert", "dp"), None),
        ),
        check_vma=False,
    )
```
